128 devices in a mesh: gx: 8 (over y, core), gy: 16 (over x, z).
Axes of the slice: x: 4, y: 4, z: 4, core: 2. Of those that a mesh axis runs over, the one named last changes fastest.
Arguments:
- point_feats: bfloat16 [262144, 96], P(('gx', 'gy')), may hold values from -6 to 6
- point_owner: int32 [262144, 1], P(('gx', 'gy')), may hold values from 0 to 127, as said below
- point_cell: int32 [262144], P(('gx', 'gy')), may hold values from 0 to 2047
- occupancy: int32 [64, 256, 16], P('gx', 'gy'), may hold values from 0 to 1, as said below
- w_conv: bfloat16 [27, 96, 96], replicated, may hold values from -0.125 to 0.125
- w_down: bfloat16 [8, 96, 192], replicated, may hold values from -0.21875 to 0.21875
- cotangent: bfloat16 [32, 128, 8, 192], P('gx', 'gy'), may hold values from -6 to 6
Outputs:
- features_out: bfloat16 [32, 128, 8, 192], P('gx', 'gy')
- grad_points: bfloat16 [262144, 96], P(('gx', 'gy'))
- grad_conv: float32 [27, 96, 96], replicated
- grad_down: float32 [8, 96, 192], replicated
The draws below stay inside these ranges and needn't reach their ends.
Inputs may be any that keep to these rules, and one draw needn't show every extreme that they name: `point_owner`: among the points of one device no owner is named more than 32 times, and in every draw some owner is named exactly 32 times among the points of each device. `occupancy`: every voxel that holds some point is active.
All inputs are finite; a program needn't handle non-finite values.
Results may differ from the reference program's by a relative error of at most 0.0067.
Values may be sent and summed in bfloat16 or wider, within the bound.
No kernel may reach another device: no remote copies, remote signals or barrier semaphores. Data moves between devices by JAX's collectives and lax.ppermute only.
A program may use at most 64 MiB of HBM per device.

```python
import jax
import jax.numpy as jnp
from jax import lax

C1 = 96
C2 = 192
VX = 8
VY = 16
VZ = 16
PTS_DEV = 2048
VOX_DEV = 2048
CAP = 32
POINTS = 262144
NX = 64
NY = 256
NZ = 16
N_GY = 16


def scene_layout(key):
    region_count = NX // VX * (NY // VY)
    slot_count = region_count * CAP
    keys = jax.random.split(key, 9)
    bonuses = jax.random.randint(keys[0], (region_count,), 256, 1024, dtype=jnp.int32)
    forced = jax.random.randint(keys[1], (region_count,), 0, region_count, dtype=jnp.int32)
    jitter = jax.random.randint(keys[2], (region_count, slot_count), 0, 1024, dtype=jnp.int32)
    slot_owner = jnp.arange(slot_count, dtype=jnp.int32) // CAP
    favored = (slot_owner[None, :] == forced[:, None]).astype(jnp.int32)
    scores = jitter + bonuses[slot_owner][None, :] + 4096 * favored
    scores = scores * slot_count + jnp.arange(slot_count, dtype=jnp.int32)[None, :]
    picked = lax.top_k(scores, PTS_DEV)[1].astype(jnp.int32)
    shuffle = jax.vmap(lambda sub_key: jax.random.permutation(sub_key, PTS_DEV))(jax.random.split(keys[3], region_count))
    picked = jnp.take_along_axis(picked, shuffle.astype(jnp.int32), axis=1)
    owners = (picked // CAP).reshape(-1).astype(jnp.int32)
    column_x = jax.random.randint(keys[4], (POINTS,), 0, VX, dtype=jnp.int32)
    column_y = jax.random.randint(keys[5], (POINTS,), 0, VY, dtype=jnp.int32)
    ground = jax.random.randint(keys[6], (region_count, VX, VY), 0, VZ - 1, dtype=jnp.int32)
    thickness = jax.random.randint(keys[7], (region_count, VX, VY), 1, VZ - ground + 1, dtype=jnp.int32)
    bottom = ground[owners, column_x, column_y]
    spans = thickness[owners, column_x, column_y]
    levels = jax.random.randint(keys[8], (POINTS,), 0, 1 << 20, dtype=jnp.int32) % spans
    cell_ids = (column_x * VY + column_y) * VZ + bottom + levels
    local_index = jnp.arange(POINTS, dtype=jnp.int32) % PTS_DEV
    cell_ids = jnp.where(local_index == 0, VOX_DEV - 1, jnp.where(local_index == 1, 0, cell_ids))
    return (owners, cell_ids.astype(jnp.int32))


def draw_point_owner(key, part):
    owners, cell_ids = scene_layout(key)
    return owners[:, None]


def draw_point_cell(key, part):
    owners, cell_ids = scene_layout(key)
    return cell_ids


def draw_occupancy(key, part):
    owners, cell_ids = scene_layout(key)
    key = jax.random.fold_in(key, 3)
    region_count = NX // VX * (NY // VY)
    holding = jnp.zeros((region_count * VOX_DEV,), jnp.int32).at[owners * VOX_DEV + cell_ids].max(1)
    extras = (jax.random.randint(key, (region_count * VOX_DEV,), 0, 32, dtype=jnp.int32) == 0).astype(jnp.int32)
    active = jnp.maximum(holding, extras)
    return active.reshape(NX // VX, NY // VY, VX, VY, VZ).transpose(0, 2, 1, 3, 4).reshape(NX, NY, NZ)


def level_of(stream_key, dims, cuts, smallest, largest):
    loudness, own = 1.0, jax.random.fold_in(stream_key, 6)
    for dim, shards_of in cuts:
        steps = jnp.exp(jax.random.uniform(jax.random.fold_in(own, dim), (shards_of,), jnp.float32, smallest / len(cuts), largest / len(cuts)))
        loudness = loudness * jnp.repeat(steps, dims[dim] // shards_of).reshape([-1 if axis == dim else 1 for axis in range(len(dims))])
    return loudness


def noise(rng, shape, scale, bound, shards=(), kind=jnp.bfloat16):
    gain = level_of(rng, shape, shards, -0.22, 0.18) if shards else 1.0
    result = jax.random.normal(rng, shape, jnp.float32) * scale * gain
    return jnp.minimum(jnp.maximum(result, -bound), bound).astype(kind)


def setup_inputs(seed: int = 0) -> dict:
    key_list = jax.random.split(jax.random.key(seed), 8)
    return {
        "point_feats": noise(key_list[0], (POINTS, C1), 1.0, 6.0, ((0, 128),)),
        "point_owner": draw_point_owner(jax.random.fold_in(key_list[7], 71), 0),
        "point_cell": draw_point_cell(jax.random.fold_in(key_list[7], 71), 0),
        "occupancy": draw_occupancy(jax.random.fold_in(key_list[7], 71), 0),
        "w_conv": noise(key_list[4], (27, C1, C1), (27 * C1) ** -0.5, 0.125),
        "w_down": noise(key_list[5], (8, C1, C2), (8 * C1) ** -0.5, 0.21875),
        "cotangent": noise(key_list[6], (NX // 2, NY // 2, NZ // 2, C2), 1.0, 6.0, ((0, 8), (1, 16))),
    }


def silu_slope(values):
    sigma = jax.nn.sigmoid(values)
    return sigma * (1.0 + values * (1.0 - sigma))

def conv_forward(padded, weights, ext_x, ext_y, ext_z):
    channels = padded.shape[-1]
    total = jnp.zeros((ext_x * ext_y * ext_z, weights.shape[2]), jnp.float32)
    for offset in range(27):
        shift_x, shift_y, shift_z = (offset // 9, offset // 3 % 3, offset % 3)
        window = padded[shift_x:shift_x + ext_x, shift_y:shift_y + ext_y, shift_z:shift_z + ext_z].reshape(-1, channels)
        total = total + jnp.dot(window, weights[offset], preferred_element_type=jnp.float32)
    return total

def conv_weight_grad(padded, delta_flat, ext_x, ext_y, ext_z):
    channels = padded.shape[-1]
    pieces = []
    for offset in range(27):
        shift_x, shift_y, shift_z = (offset // 9, offset // 3 % 3, offset % 3)
        window = padded[shift_x:shift_x + ext_x, shift_y:shift_y + ext_y, shift_z:shift_z + ext_z].reshape(-1, channels)
        pieces.append(lax.dot_general(window, delta_flat, (((0,), (0,)), ((), ())), preferred_element_type=jnp.float32))
    return jnp.stack(pieces, 0)

def conv_input_grad(delta_padded, weights, ext_x, ext_y, ext_z):
    channels = delta_padded.shape[-1]
    total = jnp.zeros((ext_x * ext_y * ext_z, weights.shape[1]), jnp.float32)
    for offset in range(27):
        shift_x, shift_y, shift_z = (2 - offset // 9, 2 - offset // 3 % 3, 2 - offset % 3)
        window = delta_padded[shift_x:shift_x + ext_x, shift_y:shift_y + ext_y, shift_z:shift_z + ext_z].reshape(-1, channels)
        total = total + lax.dot_general(window, weights[offset], (((1,), (1,)), ((), ())), preferred_element_type=jnp.float32)
    return total

def down_pieces(field):
    ext_x, ext_y, ext_z, channels = field.shape
    folded = field.reshape(ext_x // 2, 2, ext_y // 2, 2, ext_z // 2, 2, channels)
    pieces = []
    for offset in range(8):
        pieces.append(folded[:, offset // 4, :, offset // 2 % 2, :, offset % 2].reshape(-1, channels))
    return pieces

def unfold_pieces(pieces, ext_x, ext_y, ext_z):
    channels = pieces[0].shape[-1]
    stacked = jnp.stack(pieces, 0).reshape(2, 2, 2, ext_x // 2, ext_y // 2, ext_z // 2, channels)
    return stacked.transpose(3, 0, 4, 1, 5, 2, 6).reshape(ext_x, ext_y, ext_z, channels)

def level_pass(grid, occupancy, w_conv, w_down, cotangent, ext_x, ext_y, ext_z):
    pad_all = ((1, 1), (1, 1), (1, 1), (0, 0))
    padded = jnp.pad(grid, pad_all)
    pre_fine = conv_forward(padded, w_conv, ext_x, ext_y, ext_z)
    mask_fine = occupancy.reshape(-1, 1).astype(jnp.float32)
    fine_flat = (jax.nn.silu(pre_fine) * mask_fine).astype(jnp.bfloat16)
    fine = fine_flat.reshape(ext_x, ext_y, ext_z, -1)
    pieces = down_pieces(fine)
    pre_coarse = jnp.zeros((pieces[0].shape[0], w_down.shape[2]), jnp.float32)
    for offset in range(8):
        pre_coarse = pre_coarse + jnp.dot(pieces[offset], w_down[offset], preferred_element_type=jnp.float32)
    mask_pieces = down_pieces(occupancy[..., None])
    coarse_mask = mask_pieces[0]
    for offset in range(1, 8):
        coarse_mask = jnp.maximum(coarse_mask, mask_pieces[offset])
    coarse_mask = coarse_mask.astype(jnp.float32)
    features_flat = (jax.nn.silu(pre_coarse) * coarse_mask).astype(jnp.bfloat16)
    cot_flat = cotangent.reshape(-1, cotangent.shape[-1]).astype(jnp.float32)
    delta_coarse = (cot_flat * coarse_mask * silu_slope(pre_coarse)).astype(jnp.bfloat16)
    grad_down = jnp.stack([lax.dot_general(pieces[offset], delta_coarse, (((0,), (0,)), ((), ())), preferred_element_type=jnp.float32) for offset in range(8)], 0)
    back_pieces = [lax.dot_general(delta_coarse, w_down[offset], (((1,), (1,)), ((), ())), preferred_element_type=jnp.float32) for offset in range(8)]
    back_fine = unfold_pieces(back_pieces, ext_x, ext_y, ext_z).reshape(-1, w_down.shape[1])
    delta_fine = (back_fine * mask_fine * silu_slope(pre_fine)).astype(jnp.bfloat16)
    grad_conv = conv_weight_grad(padded, delta_fine, ext_x, ext_y, ext_z)
    delta_padded = jnp.pad(delta_fine.reshape(ext_x, ext_y, ext_z, -1), pad_all)
    grad_grid = conv_input_grad(delta_padded, w_conv, ext_x, ext_y, ext_z).astype(jnp.bfloat16)
    features_out = features_flat.reshape(ext_x // 2, ext_y // 2, ext_z // 2, -1)
    return (features_out, grad_grid, grad_conv, grad_down)

def reference(point_feats, point_owner, point_cell, occupancy, w_conv, w_down, cotangent):
    owner_ids = point_owner[:, 0]
    voxel_x = owner_ids // N_GY * VX + point_cell // (VY * VZ)
    voxel_y = owner_ids % N_GY * VY + point_cell // VZ % VY
    voxel_z = point_cell % VZ
    flat_voxel = ((voxel_x * NY + voxel_y) * NZ + voxel_z).astype(jnp.int32)
    channels = point_feats.shape[1]
    pooled = jnp.zeros((NX * NY * NZ, channels), jnp.float32).at[flat_voxel].add(point_feats.astype(jnp.float32))
    grid = pooled.astype(jnp.bfloat16).reshape(NX, NY, NZ, channels)
    features_out, grad_grid, grad_conv, grad_down = level_pass(grid, occupancy, w_conv, w_down, cotangent, NX, NY, NZ)
    grad_points = grad_grid[flat_voxel]
    grad_scale = 1.0 / float(NX * NY * NZ) ** 0.5
    return (features_out, grad_points, grad_conv * grad_scale, grad_down * grad_scale)
```

```python
import functools
import math

import jax
import jax.numpy as jnp
from jax import lax
from jax.experimental import pallas as pl
from jax.experimental.pallas import tpu as pltpu
from jax.sharding import PartitionSpec as P

F32 = jnp.float32
BF16 = jnp.bfloat16
LANE = 128
WIDE = 256
PACK = 4
AXES = ("gx", "gy")
NT = (((1,), (1,)), ((), ()))
NN = (((1,), (0,)), ((), ()))
TN = (((0,), (0,)), ((), ()))


def iota(shape, dim):
    return lax.broadcasted_iota(jnp.int32, shape, dim)


def mm(a, b, dims=NN):
    return lax.dot_general(a, b, dims, preferred_element_type=F32)


def one_hot(mask):
    return jnp.where(mask, 1.0, 0.0).astype(BF16)


def call(kernel, outs, args, name, scratch=(), flops=0, megabytes=4):
    return pl.pallas_call(
        kernel,
        out_shape=outs,
        in_specs=[pl.BlockSpec(memory_space=pltpu.VMEM)] * len(args),
        out_specs=jax.tree.map(lambda _: pl.BlockSpec(memory_space=pltpu.VMEM), outs),
        scratch_shapes=list(scratch),
        compiler_params=pltpu.CompilerParams(vmem_limit_bytes=48 * 1024 * 1024),
        cost_estimate=pl.CostEstimate(
            flops=flops, bytes_accessed=megabytes * 1000000, transcendentals=0
        ),
        name=name,
    )(*args)


def struct(shape, dtype):
    return jax.ShapeDtypeStruct(shape, dtype)


def dispatch_kernel(feats_ref, owner_ref, cell_ref, send_ref, slot_ref, *, devices, cap):
    channels, points = feats_ref.shape
    owner = owner_ref[...]
    hot = iota((devices, points), 0) == owner
    block = min(256, points)
    upper = one_hot(iota((block, block), 0) < iota((block, block), 1))
    carry = jnp.zeros((devices, 1), F32)
    ranks = []
    for start in range(0, points, block):
        part = jnp.where(hot[:, start : start + block], 1.0, 0.0)
        before = mm(part.astype(BF16), upper) + carry
        ranks.append(jnp.sum(part * before, axis=0, keepdims=True))
        carry = carry + jnp.sum(part, axis=1, keepdims=True)
    rank = jnp.concatenate(ranks, axis=1).astype(jnp.int32)
    row = owner * (cap // PACK) + (rank >> 2)
    quarter = rank & 3
    slot_ref[0:1, :] = row
    slot_ref[1:2, :] = quarter
    cell = cell_ref[...]
    line = iota((LANE - channels, points), 0)
    extra = jnp.where(line == 0, cell >> 6, 0)
    extra = jnp.where(line == 1, (cell >> 1) & 31, extra)
    extra = jnp.where(line == 2, cell & 1, extra)
    whole = jnp.concatenate([feats_ref[...], extra.astype(F32).astype(BF16)], axis=0)
    spread = jnp.concatenate([whole * one_hot(quarter == q) for q in range(PACK)], axis=0)
    rows = send_ref.shape[0]
    step = min(256, rows)
    for start in range(0, rows, step):
        pick = one_hot(iota((step, points), 0) + start == row)
        send_ref[start : start + step, :] = mm(pick, spread, NT).astype(BF16)


def pool_kernel(got_ref, grid_ref, total_ref, *, channels):
    rows = got_ref.shape[0]
    pairs = grid_ref.shape[0]
    lane = iota((8, LANE), 1)
    weigh = jnp.where(lane == channels, 32.0, jnp.where(lane == channels + 1, 1.0, 0.0))
    weigh = weigh.astype(BF16)
    step = 256
    for q in range(PACK):
        block = got_ref[:, q * LANE : (q + 1) * LANE]
        place = mm(weigh, block, NT)[0:1].astype(jnp.int32)
        odd = block * block[:, channels + 2 : channels + 3]
        both = jnp.concatenate([block - odd, odd], axis=1)
        for start in range(0, pairs, step):
            pick = one_hot(iota((step, rows), 0) + start == place)
            part = mm(pick, both)
            if q == 0:
                total_ref[start : start + step, :] = part
            elif q < PACK - 1:
                total_ref[start : start + step, :] += part
            else:
                grid_ref[start : start + step, :] = (
                    total_ref[start : start + step, :] + part
                ).astype(BF16)


def weights_kernel(conv_ref, down_ref, conv_out, down_out):
    channels = conv_ref.shape[1]
    conv_out[...] = jnp.zeros(conv_out.shape, BF16)
    down_out[...] = jnp.zeros(down_out.shape, BF16)
    a, b = slice(0, channels), slice(LANE, LANE + channels)
    for j in range(9):
        low, mid, high = conv_ref[3 * j], conv_ref[3 * j + 1], conv_ref[3 * j + 2]
        conv_out[j, 0, a, a] = mid
        conv_out[j, 0, a, b] = low
        conv_out[j, 0, b, a] = high
        conv_out[j, 0, b, b] = mid
        conv_out[j, 1, a, b] = high
        conv_out[j, 1, b, a] = low
    for j in range(4):
        down_out[j, a, :] = down_ref[2 * j]
        down_out[j, b, :] = down_ref[2 * j + 1]


def fill(center_ref, x_low, x_high, y_low, y_high, pad_ref, side_ref):
    ext_x, ext_y, half, wide = pad_ref.shape
    pad_ref[1 : ext_x - 1, 1 : ext_y - 1] = (
        center_ref[...].astype(F32).reshape(ext_x - 2, ext_y - 2, half, wide)
    )
    pad_ref[0, 1 : ext_y - 1] = x_low[...].astype(F32).reshape(ext_y - 2, half, wide)
    pad_ref[ext_x - 1, 1 : ext_y - 1] = x_high[...].astype(F32).reshape(ext_y - 2, half, wide)
    pad_ref[:, 0] = y_low[...].astype(F32).reshape(ext_x, half, wide)
    pad_ref[:, ext_y - 1] = y_high[...].astype(F32).reshape(ext_x, half, wide)
    level = iota((ext_x * ext_y, half, LANE), 1)
    even = pad_ref[:, :, :, :LANE].reshape(ext_x * ext_y, half, LANE)
    odd = pad_ref[:, :, :, LANE:].reshape(ext_x * ext_y, half, LANE)
    even = jnp.where(level == half - 1, 0.0, pltpu.roll(even, half - 1, 1))
    odd = jnp.where(level == 0, 0.0, pltpu.roll(odd, 1, 1))
    side_ref[:, :, :, :LANE] = even.reshape(ext_x, ext_y, half, LANE)
    side_ref[:, :, :, LANE:] = odd.reshape(ext_x, ext_y, half, LANE)


def window(ref, j, first, count):
    dx, dy = j // 3, j % 3
    ext_y, half, wide = ref.shape[1] - 2, ref.shape[2], ref.shape[3]
    rows = ref[first + dx : first + dx + count, dy : dy + ext_y]
    return rows.reshape(count * ext_y * half, wide).astype(BF16)


def convolve(pad_ref, side_ref, weight_ref, first, count, back):
    total = None
    for j in range(9):
        for t, ref in enumerate((pad_ref, side_ref)):
            weight = weight_ref[8 - j if back else j, t]
            part = mm(window(ref, j, first, count), weight, NT if back else NN)
            total = part if total is None else total + part
    return total


def logistic(values):
    return 1.0 / (1.0 + jnp.exp(-values))


def level_kernel(
    center_ref, x_low, x_high, y_low, y_high, mask_ref, coarse_ref, conv_ref, down_ref, cot_ref,
    features_ref, fine_ref, delta_coarse_ref, delta_ref,
    pad_ref, side_ref, fine_s, slope_s,
):
    fill(center_ref, x_low, x_high, y_low, y_high, pad_ref, side_ref)
    ext_x, ext_y, half, wide = (
        pad_ref.shape[0] - 2, pad_ref.shape[1] - 2, pad_ref.shape[2], pad_ref.shape[3]
    )
    count = 4
    for first in range(0, ext_x, count):
        rows = slice(first * ext_y * half, (first + count) * ext_y * half)
        pre = convolve(pad_ref, side_ref, conv_ref, first, count, False)
        mask = mask_ref[rows, :].astype(F32)
        sigma = logistic(pre)
        fine = (pre * sigma * mask).astype(BF16)
        slope = sigma * (1.0 + pre * (1.0 - sigma)) * mask
        fine_ref[rows, :] = fine
        shape = (count // 2, 2, ext_y // 2, 2, half, wide)
        fine_s[first // 2 : (first + count) // 2] = fine.astype(F32).reshape(shape)
        slope_s[first // 2 : (first + count) // 2] = slope.reshape(shape)
    coarse_rows = ext_x // 2 * (ext_y // 2) * half
    pre = None
    for j in range(4):
        piece = fine_s[:, j // 2, :, j % 2].reshape(coarse_rows, wide).astype(BF16)
        part = mm(piece, down_ref[j])
        pre = part if pre is None else pre + part
    sigma = logistic(pre)
    mask = coarse_ref[...].astype(F32)
    features_ref[...] = (pre * sigma * mask).astype(BF16)
    slope = sigma * (1.0 + pre * (1.0 - sigma))
    delta = (cot_ref[...].astype(F32) * mask * slope).astype(BF16)
    delta_coarse_ref[...] = delta
    for j in range(4):
        back = mm(delta, down_ref[j], NT).reshape(ext_x // 2, ext_y // 2, half, wide)
        fine_s[:, j // 2, :, j % 2] = back * slope_s[:, j // 2, :, j % 2]
    delta_ref[...] = fine_s[...].reshape(ext_x * ext_y * half, wide).astype(BF16)


def weight_grad_kernel(
    center_ref, x_low, x_high, y_low, y_high, fine_ref, delta_coarse_ref, delta_ref, out_ref,
    pad_ref, side_ref, fine_s, *, channels, scale,
):
    fill(center_ref, x_low, x_high, y_low, y_high, pad_ref, side_ref)
    ext_x, ext_y, half, wide = (
        pad_ref.shape[0] - 2, pad_ref.shape[1] - 2, pad_ref.shape[2], pad_ref.shape[3]
    )
    turned = delta_ref[...].astype(F32).T.astype(BF16)
    lo, hi = slice(0, LANE), slice(LANE, WIDE)
    for j in range(9):
        main = mm(turned, window(pad_ref, j, 0, ext_x))
        side = mm(turned, window(side_ref, j, 0, ext_x))
        low = main[hi, lo] + side[lo, hi]
        mid = main[lo, lo] + main[hi, hi]
        high = main[lo, hi] + side[hi, lo]
        for t, part in enumerate((low, mid, high)):
            start = (3 * j + t) * channels
            out_ref[start : start + channels, :] = (part.T[:channels] * scale).astype(BF16)
    fine_s[...] = fine_ref[...].astype(F32).reshape(fine_s.shape)
    coarse_rows = ext_x // 2 * (ext_y // 2) * half
    base = 27 * channels
    for j in range(4):
        piece = fine_s[:, j // 2, :, j % 2].reshape(coarse_rows, wide).astype(BF16)
        grad = mm(piece, delta_coarse_ref[...], TN) * scale
        first, second = grad[:channels], grad[LANE : LANE + channels]
        start = base + 2 * j * channels
        out_ref[start : start + channels, :] = first[:, :LANE].astype(BF16)
        out_ref[start + channels : start + 2 * channels, :] = second[:, :LANE].astype(BF16)
        start = base + (8 + j) * channels
        tail = jnp.concatenate([first[:, LANE:], second[:, LANE:]], axis=1)
        out_ref[start : start + channels, :] = tail.astype(BF16)
    end = base + 12 * channels
    out_ref[end:, :] = jnp.zeros((out_ref.shape[0] - end, LANE), BF16)


def input_grad_kernel(
    center_ref, x_low, x_high, y_low, y_high, conv_ref, got_ref, back_ref,
    pad_ref, side_ref, grad_s, *, channels,
):
    fill(center_ref, x_low, x_high, y_low, y_high, pad_ref, side_ref)
    ext_x, ext_y, half = pad_ref.shape[0] - 2, pad_ref.shape[1] - 2, pad_ref.shape[2]
    count = 4
    for first in range(0, ext_x, count):
        rows = slice(first * ext_y * half, (first + count) * ext_y * half)
        grad_s[rows, :] = convolve(pad_ref, side_ref, conv_ref, first, count, True).astype(BF16)
    grad = grad_s[...]
    pairs = grad.shape[0]
    rows = got_ref.shape[0]
    step = min(256, rows)
    for q in range(PACK):
        for start in range(0, rows, step):
            info = got_ref[start : start + step, q * LANE : (q + 1) * LANE].astype(F32)
            place = info[:, channels : channels + 1] * 32.0 + info[:, channels + 1 : channels + 2]
            pick = one_hot(iota((step, pairs), 1) == place.astype(jnp.int32))
            both = mm(pick, grad)
            odd = info[:, channels + 2 : channels + 3] > 0.5
            row = jnp.where(odd, both[:, LANE:], both[:, :LANE])
            back_ref[start : start + step, q * LANE : (q + 1) * LANE] = row.astype(BF16)


def collect_kernel(back_ref, slot_ref, out_ref):
    channels, points = out_ref.shape
    rows = back_ref.shape[0]
    step = min(512, points)
    for start in range(0, points, step):
        row = slot_ref[0:1, start : start + step]
        quarter = slot_ref[1:2, start : start + step]
        pick = one_hot(iota((rows, step), 0) == row)
        found = mm(back_ref[...], pick, TN)
        total = jnp.zeros((channels, step), F32)
        for q in range(PACK):
            total = jnp.where(quarter == q, found[q * LANE : q * LANE + channels], total)
        out_ref[:, start : start + step] = total.astype(BF16)


def sum_kernel(parts_ref, out_ref):
    total = jnp.sum(parts_ref[...].astype(F32), axis=0).astype(BF16)
    out_ref[...] = jnp.broadcast_to(total[None], out_ref.shape)


def unpack_kernel(all_ref, conv_ref, down_ref):
    channels = conv_ref.shape[1]
    base = 27 * channels
    for j in range(27):
        conv_ref[j] = all_ref[j * channels : (j + 1) * channels, :channels].astype(F32)
    for j in range(8):
        start = base + j * channels
        down_ref[j, :, :LANE] = all_ref[start : start + channels, :].astype(F32)
        start = base + (8 + j // 2) * channels
        tail = all_ref[start : start + channels, :].astype(F32)
        rest = down_ref.shape[2] - LANE
        down_ref[j, :, LANE:] = tail[:, (j % 2) * rest : (j % 2 + 1) * rest]


def shift(block, axis, step):
    count = lax.axis_size(axis)
    pairs = [(i, i + step) for i in range(count) if 0 <= i + step < count]
    return lax.ppermute(block, axis, pairs)


def halo(center, ext_x, ext_y, half):
    wide = center.shape[1]
    slab = ext_y * half
    x_low = shift(center[-slab:], "gx", 1)
    x_high = shift(center[:slab], "gx", -1)
    whole = center.reshape(ext_x, ext_y, half, wide)
    low, high = x_low.reshape(1, ext_y, half, wide), x_high.reshape(1, ext_y, half, wide)

    def edge(y):
        parts = [low[:, y], whole[:, y], high[:, y]]
        return jnp.concatenate(parts, axis=0).reshape((ext_x + 2) * half, wide)

    y_low = shift(edge(ext_y - 1), "gy", 1)
    y_high = shift(edge(0), "gy", -1)
    return x_low, x_high, y_low, y_high


def exchange(blocks):
    return lax.all_to_all(blocks, AXES, split_axis=0, concat_axis=0, tiled=True)


def shards(point_feats, point_owner, point_cell, occupancy, w_conv, w_down, cotangent):
    points, channels = point_feats.shape
    devices = lax.axis_size("gx") * lax.axis_size("gy")
    cap = 32
    ext_x, ext_y, ext_z = occupancy.shape
    half = ext_z // 2
    pairs = ext_x * ext_y * half
    coarse = w_down.shape[2]
    coarse_rows = ext_x // 2 * (ext_y // 2) * half
    slot_rows = devices * cap // PACK
    scale = 1.0 / math.sqrt(float(ext_x * ext_y * ext_z * devices))
    padded = (ext_x + 2, ext_y + 2, half, WIDE)
    split = (ext_x // 2, 2, ext_y // 2, 2, half, WIDE)

    send, slot = call(
        functools.partial(dispatch_kernel, devices=devices, cap=cap),
        (struct((slot_rows, PACK * LANE), BF16), struct((2, points), jnp.int32)),
        (point_feats.T, point_owner.reshape(1, points), point_cell.reshape(1, points)),
        "dispatch",
        flops=2 * points * slot_rows * PACK * LANE,
    )
    got = exchange(send.reshape(devices, cap // PACK, PACK * LANE)).reshape(
        slot_rows, PACK * LANE
    )
    conv_blocks, down_blocks = call(
        weights_kernel,
        (struct((9, 2, WIDE, WIDE), BF16), struct((4, WIDE, coarse), BF16)),
        (w_conv, w_down),
        "weights",
    )
    mask = jnp.broadcast_to(
        occupancy.reshape(pairs, 2, 1).astype(BF16), (pairs, 2, LANE)
    ).reshape(pairs, WIDE)
    coarse_mask = jnp.max(occupancy.reshape(ext_x // 2, 2, ext_y // 2, 2, half, 2), axis=(1, 3, 5))
    coarse_mask = jnp.broadcast_to(
        coarse_mask.reshape(coarse_rows, 1).astype(BF16), (coarse_rows, coarse)
    )
    grid = call(
        functools.partial(pool_kernel, channels=channels),
        struct((pairs, WIDE), BF16),
        (got,),
        "pool",
        scratch=[pltpu.VMEM((pairs, WIDE), F32)],
        flops=2 * pairs * slot_rows * PACK * WIDE,
    )
    rim = halo(grid, ext_x, ext_y, half)
    conv_flops = 2 * pairs * 18 * WIDE * WIDE
    features, fine, delta_coarse, delta = call(
        level_kernel,
        (
            struct((coarse_rows, coarse), BF16),
            struct((pairs, WIDE), BF16),
            struct((coarse_rows, coarse), BF16),
            struct((pairs, WIDE), BF16),
        ),
        (grid, *rim, mask, coarse_mask, conv_blocks, down_blocks,
         cotangent.reshape(coarse_rows, coarse)),
        "level",
        scratch=[
            pltpu.VMEM(padded, F32),
            pltpu.VMEM(padded, F32),
            pltpu.VMEM(split, F32),
            pltpu.VMEM(split, F32),
        ],
        flops=conv_flops,
        megabytes=8,
    )
    delta_rim = halo(delta, ext_x, ext_y, half)
    used = 27 * channels + 12 * channels
    chunk = -(-used // (16 * devices)) * 16
    packed = call(
        functools.partial(weight_grad_kernel, channels=channels, scale=scale),
        struct((devices * chunk, LANE), BF16),
        (grid, *rim, fine, delta_coarse, delta),
        "weight_grad",
        scratch=[pltpu.VMEM(padded, F32), pltpu.VMEM(padded, F32), pltpu.VMEM(split, F32)],
        flops=conv_flops,
        megabytes=8,
    )
    terms = exchange(packed.reshape(devices, chunk, LANE))
    back = call(
        functools.partial(input_grad_kernel, channels=channels),
        struct((slot_rows, PACK * LANE), BF16),
        (delta, *delta_rim, conv_blocks, got),
        "input_grad",
        scratch=[
            pltpu.VMEM(padded, F32), pltpu.VMEM(padded, F32), pltpu.VMEM((pairs, WIDE), BF16)
        ],
        flops=conv_flops + 2 * pairs * slot_rows * PACK * WIDE,
        megabytes=8,
    )
    returned = exchange(back.reshape(devices, cap // PACK, PACK * LANE)).reshape(
        slot_rows, PACK * LANE
    )
    summed = call(
        sum_kernel, struct((devices, chunk, LANE), BF16), (terms,), "sum", flops=devices * chunk * LANE
    )
    gathered = exchange(summed).reshape(devices * chunk, LANE)
    grad_points = call(
        collect_kernel,
        struct((channels, points), BF16),
        (returned, slot),
        "collect",
        flops=2 * points * slot_rows * PACK * LANE,
    ).T
    grad_conv, grad_down = call(
        unpack_kernel,
        (struct(w_conv.shape, F32), struct(w_down.shape, F32)),
        (gathered,),
        "unpack",
    )
    return (
        features.reshape(ext_x // 2, ext_y // 2, half, coarse),
        grad_points,
        grad_conv,
        grad_down,
    )


def solution(mesh):
    placed = (
        P(("gx", "gy"), None),
        P(("gx", "gy"), None),
        P(("gx", "gy")),
        P("gx", "gy", None),
        P(),
        P(),
        P("gx", "gy", None, None),
    )
    return jax.shard_map(
        shards,
        mesh=mesh,
        in_specs=placed,
        out_specs=(P("gx", "gy", None, None), P(("gx", "gy"), None), P(), P()),
        check_vma=False,
    )
```

```python
import functools
import math

import jax
import jax.numpy as jnp
from jax import lax
from jax.experimental import pallas as pl
from jax.experimental.pallas import tpu as pltpu
from jax.sharding import PartitionSpec as P

F32 = jnp.float32
BF16 = jnp.bfloat16
LANE = 128
WIDE = 256
PACK = 4
AXES = ("gx", "gy")
NT = (((1,), (1,)), ((), ()))
NN = (((1,), (0,)), ((), ()))
TN = (((0,), (0,)), ((), ()))


def iota(shape, dim):
    return lax.broadcasted_iota(jnp.int32, shape, dim)


def mm(a, b, dims=NN):
    return lax.dot_general(a, b, dims, preferred_element_type=F32)


def one_hot(mask):
    return jnp.where(mask, 1.0, 0.0).astype(BF16)


def call(kernel, outs, args, name, scratch=(), flops=0, megabytes=4):
    return pl.pallas_call(
        kernel,
        out_shape=outs,
        in_specs=[pl.BlockSpec(memory_space=pltpu.VMEM)] * len(args),
        out_specs=jax.tree.map(lambda _: pl.BlockSpec(memory_space=pltpu.VMEM), outs),
        scratch_shapes=list(scratch),
        compiler_params=pltpu.CompilerParams(vmem_limit_bytes=48 * 1024 * 1024),
        cost_estimate=pl.CostEstimate(
            flops=flops, bytes_accessed=megabytes * 1000000, transcendentals=0
        ),
        name=name,
    )(*args)


def struct(shape, dtype):
    return jax.ShapeDtypeStruct(shape, dtype)


def dispatch_kernel(feats_ref, owner_ref, cell_ref, send_ref, slot_ref, *, devices, cap):
    channels, points = feats_ref.shape
    owner = owner_ref[...]
    hot = iota((devices, points), 0) == owner
    block = min(256, points)
    upper = one_hot(iota((block, block), 0) < iota((block, block), 1))
    carry = jnp.zeros((devices, 1), F32)
    ranks = []
    for start in range(0, points, block):
        part = jnp.where(hot[:, start : start + block], 1.0, 0.0)
        before = mm(part.astype(BF16), upper) + carry
        ranks.append(jnp.sum(part * before, axis=0, keepdims=True))
        carry = carry + jnp.sum(part, axis=1, keepdims=True)
    rank = jnp.concatenate(ranks, axis=1).astype(jnp.int32)
    row = owner * (cap // PACK) + (rank >> 2)
    quarter = rank & 3
    slot_ref[0:1, :] = row
    slot_ref[1:2, :] = quarter
    cell = cell_ref[...]
    line = iota((LANE - channels, points), 0)
    extra = jnp.where(line == 0, cell >> 6, 0)
    extra = jnp.where(line == 1, (cell >> 1) & 31, extra)
    extra = jnp.where(line == 2, cell & 1, extra)
    whole = jnp.concatenate([feats_ref[...], extra.astype(F32).astype(BF16)], axis=0)
    spread = jnp.concatenate([whole * one_hot(quarter == q) for q in range(PACK)], axis=0)
    rows = send_ref.shape[0]
    step = min(256, rows)
    for start in range(0, rows, step):
        pick = one_hot(iota((step, points), 0) + start == row)
        send_ref[start : start + step, :] = mm(pick, spread, NT).astype(BF16)


def pool_kernel(
    got_ref, coarse_ref, grid_ref, first_ref, last_ref, total_ref, *, channels, rim, slab, coarse_slab
):
    rows = got_ref.shape[0]
    pairs = grid_ref.shape[0]
    lane = iota((8, LANE), 1)
    weigh = jnp.where(lane == channels, 32.0, jnp.where(lane == channels + 1, 1.0, 0.0))
    weigh = weigh.astype(BF16)
    step = 256
    for q in range(PACK):
        block = got_ref[:, q * LANE : (q + 1) * LANE]
        place = mm(weigh, block, NT)[0:1].astype(jnp.int32)
        odd = block * block[:, channels + 2 : channels + 3]
        both = jnp.concatenate([block - odd, odd], axis=1)
        for start in range(0, pairs, step):
            pick = one_hot(iota((step, rows), 0) + start == place)
            part = mm(pick, both)
            if q == 0:
                total_ref[start : start + step, :] = part
            elif q < PACK - 1:
                total_ref[start : start + step, :] += part
            else:
                grid_ref[start : start + step, :] = (
                    total_ref[start : start + step, :] + part
                ).astype(BF16)
    edge = rim * slab
    first_ref[:edge, :] = grid_ref[:edge, :]
    first_ref[edge:, :] = coarse_ref[:coarse_slab, :]
    last_ref[:edge, :] = grid_ref[pairs - edge :, :]
    last_ref[edge:, :] = coarse_ref[coarse_ref.shape[0] - coarse_slab :, :]


def prepare_kernel(conv_ref, down_ref, cot_ref, occ_ref, conv_out, down_out, coarse_out, *, ext_y):
    channels = conv_ref.shape[1]
    conv_out[...] = jnp.zeros(conv_out.shape, BF16)
    down_out[...] = jnp.zeros(down_out.shape, BF16)
    a, b = slice(0, channels), slice(LANE, LANE + channels)
    for j in range(9):
        low, mid, high = conv_ref[3 * j], conv_ref[3 * j + 1], conv_ref[3 * j + 2]
        conv_out[j, 0, a, a] = mid
        conv_out[j, 0, a, b] = low
        conv_out[j, 0, b, a] = high
        conv_out[j, 0, b, b] = mid
        conv_out[j, 1, a, b] = high
        conv_out[j, 1, b, a] = low
    for j in range(4):
        down_out[j, a, :] = down_ref[2 * j]
        down_out[j, b, :] = down_ref[2 * j + 1]
    columns, depth = occ_ref.shape
    rows, coarse = cot_ref.shape
    half = depth // 2
    rest = WIDE - coarse
    occ = occ_ref[...].astype(F32).astype(BF16)
    row = iota((rows, columns), 0)
    place, column = row // half, iota((rows, columns), 1)
    base = place // (ext_y // 2) * 2 * ext_y + place % (ext_y // 2) * 2
    level = iota((rows, depth), 1) // 2 == iota((rows, depth), 0) % half
    total = jnp.zeros((rows, rest), F32)
    for j in range(4):
        pick = one_hot(base + j // 2 * ext_y + j % 2 == column)
        found = jnp.where(level, mm(pick, occ), 0.0).astype(BF16)
        spot = iota((depth, rest), 1) == 2 * j + iota((depth, rest), 0) % 2
        total = total + mm(found, one_hot(spot))
    coarse_out[:, :coarse] = cot_ref[...]
    coarse_out[:, coarse:] = total.astype(BF16)


def as_field(rows, ext_x, ext_y, half):
    return rows.astype(F32).reshape(ext_x, ext_y, half, rows.shape[1])


def edge_kernel(grid_ref, coarse_ref, low_ref, high_ref, first_ref, last_ref, *, fields):
    start_in, start_out = 0, 0
    for ref, (ext_x, ext_y, half, rim) in zip((grid_ref, coarse_ref), fields):
        size_in = rim * ext_y * half
        parts = [
            as_field(low_ref[start_in : start_in + size_in, :], rim, ext_y, half),
            as_field(ref[...], ext_x, ext_y, half),
            as_field(high_ref[start_in : start_in + size_in, :], rim, ext_y, half),
        ]
        at = start_out
        for part in parts:
            size = part.shape[0] * rim * half
            for out, y in ((first_ref, 0), (last_ref, ext_y - rim)):
                out[at : at + size, :] = part[:, y : y + rim].reshape(size, WIDE).astype(BF16)
            at += size
        start_in += size_in
        start_out = at


def fill_field(pad_ref, center, low, high, first, last, rim):
    ext_x, ext_y = pad_ref.shape[0] - 2 * rim, pad_ref.shape[1] - 2 * rim
    half = pad_ref.shape[2]
    pad_ref[rim : rim + ext_x, rim : rim + ext_y] = as_field(center, ext_x, ext_y, half)
    pad_ref[:rim, rim : rim + ext_y] = as_field(low, rim, ext_y, half)
    pad_ref[rim + ext_x :, rim : rim + ext_y] = as_field(high, rim, ext_y, half)
    pad_ref[:, :rim] = as_field(first, ext_x + 2 * rim, rim, half)
    pad_ref[:, rim + ext_y :] = as_field(last, ext_x + 2 * rim, rim, half)


def fill_side(pad_ref, side_ref):
    ext_x, ext_y, half, wide = pad_ref.shape
    level = iota((ext_x * ext_y, half, LANE), 1)
    even = pad_ref[:, :, :, :LANE].reshape(ext_x * ext_y, half, LANE)
    odd = pad_ref[:, :, :, LANE:].reshape(ext_x * ext_y, half, LANE)
    even = jnp.where(level == half - 1, 0.0, pltpu.roll(even, half - 1, 1))
    odd = jnp.where(level == 0, 0.0, pltpu.roll(odd, 1, 1))
    side_ref[:, :, :, :LANE] = even.reshape(ext_x, ext_y, half, LANE)
    side_ref[:, :, :, LANE:] = odd.reshape(ext_x, ext_y, half, LANE)


def window(ref, j, first, count):
    dx, dy = j // 3, j % 3
    ext_y, half, wide = ref.shape[1] - 2, ref.shape[2], ref.shape[3]
    rows = ref[first + dx : first + dx + count, dy : dy + ext_y]
    return rows.reshape(count * ext_y * half, wide).astype(BF16)


def convolve(pad_ref, side_ref, weight_ref, first, count, back):
    total = None
    for j in range(9):
        for t, ref in enumerate((pad_ref, side_ref)):
            weight = weight_ref[8 - j if back else j, t]
            part = mm(window(ref, j, first, count), weight, NT if back else NN)
            total = part if total is None else total + part
    return total


def logistic(values):
    return 1.0 / (1.0 + jnp.exp(-values))


def inner(field, rim):
    part = field[rim : field.shape[0] - rim, rim : field.shape[1] - rim]
    return part.reshape(part.shape[0] * part.shape[1] * part.shape[2], part.shape[3])


def level_kernel(
    grid_ref, coarse_ref, x_low, x_high, y_low, y_high, conv_ref, down_ref,
    features_ref, fine_ref, delta_coarse_ref, delta_ref, near_ref,
    pad_ref, side_ref, coarse_s, mask_s, fine_s, slope_s,
):
    ext_x, ext_y, half, wide = (
        pad_ref.shape[0] - 2, pad_ref.shape[1] - 2, pad_ref.shape[2], pad_ref.shape[3]
    )
    cut_x, cut_y = 3 * (ext_y - 4) * half, 3 * (ext_x + 2) * half
    fill_field(
        pad_ref, grid_ref[...], x_low[:cut_x, :], x_high[:cut_x, :],
        y_low[:cut_y, :], y_high[:cut_y, :], 3,
    )
    fill_field(
        coarse_s, coarse_ref[...], x_low[cut_x:, :], x_high[cut_x:, :],
        y_low[cut_y:, :], y_high[cut_y:, :], 1,
    )
    fill_side(pad_ref, side_ref)
    near_ref[...] = inner(pad_ref[...], 2).astype(BF16)
    coarse_x, coarse_y = ext_x // 2, ext_y // 2
    coarse_rows = coarse_x * coarse_y * half
    coarse = down_ref.shape[2]
    given = coarse_s[...].reshape(coarse_rows, wide).astype(BF16)
    largest = None
    for j in range(4):
        spot = iota((wide, wide), 0) == coarse + 2 * j + iota((wide, wide), 1) // LANE
        mask = mm(given, one_hot(spot))
        mask_s[:, j // 2, :, j % 2] = mask.reshape(coarse_x, coarse_y, half, wide)
        largest = mask if largest is None else jnp.maximum(largest, mask)
    largest = jnp.maximum(largest[:, :LANE], largest[:, LANE:])
    coarse_mask = jnp.concatenate([largest, largest[:, : coarse - LANE]], axis=1)
    count = 4
    for first in range(0, ext_x, count):
        pre = convolve(pad_ref, side_ref, conv_ref, first, count, False)
        part = slice(first // 2, (first + count) // 2)
        mask = mask_s[part].reshape(count * ext_y * half, wide)
        sigma = logistic(pre)
        shape = (count // 2, 2, coarse_y, 2, half, wide)
        fine_s[part] = (pre * sigma * mask).astype(BF16).astype(F32).reshape(shape)
        slope_s[part] = (sigma * (1.0 + pre * (1.0 - sigma)) * mask).reshape(shape)
    field = (ext_x, ext_y, half, wide)
    fine_ref[...] = inner(fine_s[...].reshape(field), 2).astype(BF16)
    pre = None
    for j in range(4):
        piece = fine_s[:, j // 2, :, j % 2].reshape(coarse_rows, wide).astype(BF16)
        part = mm(piece, down_ref[j])
        pre = part if pre is None else pre + part
    sigma = logistic(pre)
    coarse_field = (coarse_x, coarse_y, half, coarse)
    features = pre * sigma * coarse_mask
    features_ref[...] = inner(features.reshape(coarse_field), 1).astype(BF16)
    slope = sigma * (1.0 + pre * (1.0 - sigma))
    cot = coarse_s[:, :, :, :coarse].reshape(coarse_rows, coarse)
    delta = cot * coarse_mask * slope
    delta_coarse_ref[...] = inner(delta.reshape(coarse_field), 1).astype(BF16)
    delta = delta.astype(BF16)
    for j in range(4):
        back = mm(delta, down_ref[j], NT).reshape(coarse_x, coarse_y, half, wide)
        fine_s[:, j // 2, :, j % 2] = back * slope_s[:, j // 2, :, j % 2]
    delta_ref[...] = inner(fine_s[...].reshape(field), 1).astype(BF16)


def weight_grad_kernel(
    near_ref, fine_ref, delta_coarse_ref, delta_ref, out_ref,
    pad_ref, side_ref, delta_s, fine_s, *, channels, scale,
):
    ext_x, ext_y, half, wide = (
        pad_ref.shape[0] - 2, pad_ref.shape[1] - 2, pad_ref.shape[2], pad_ref.shape[3]
    )
    pad_ref[...] = as_field(near_ref[...], ext_x + 2, ext_y + 2, half)
    fill_side(pad_ref, side_ref)
    delta_s[...] = as_field(delta_ref[...], ext_x + 2, ext_y + 2, half)
    turned = inner(delta_s[...], 1).T.astype(BF16)
    lo, hi = slice(0, LANE), slice(LANE, WIDE)
    for j in range(9):
        main = mm(turned, window(pad_ref, j, 0, ext_x))
        side = mm(turned, window(side_ref, j, 0, ext_x))
        low = main[hi, lo] + side[lo, hi]
        mid = main[lo, lo] + main[hi, hi]
        high = main[lo, hi] + side[hi, lo]
        for t, part in enumerate((low, mid, high)):
            start = (3 * j + t) * channels
            out_ref[start : start + channels, :] = (part.T[:channels] * scale).astype(BF16)
    fine_s[...] = fine_ref[...].astype(F32).reshape(fine_s.shape)
    coarse_rows = ext_x // 2 * (ext_y // 2) * half
    base = 27 * channels
    for j in range(4):
        piece = fine_s[:, j // 2, :, j % 2].reshape(coarse_rows, wide).astype(BF16)
        grad = mm(piece, delta_coarse_ref[...], TN) * scale
        first, second = grad[:channels], grad[LANE : LANE + channels]
        start = base + 2 * j * channels
        out_ref[start : start + channels, :] = first[:, :LANE].astype(BF16)
        out_ref[start + channels : start + 2 * channels, :] = second[:, :LANE].astype(BF16)
        start = base + (8 + j) * channels
        tail = jnp.concatenate([first[:, LANE:], second[:, LANE:]], axis=1)
        out_ref[start : start + channels, :] = tail.astype(BF16)
    end = base + 12 * channels
    out_ref[end:, :] = jnp.zeros((out_ref.shape[0] - end, LANE), BF16)


def input_grad_kernel(delta_ref, conv_ref, got_ref, back_ref, pad_ref, side_ref, grad_s, *, channels):
    ext_x, ext_y, half = pad_ref.shape[0] - 2, pad_ref.shape[1] - 2, pad_ref.shape[2]
    pad_ref[...] = as_field(delta_ref[...], ext_x + 2, ext_y + 2, half)
    fill_side(pad_ref, side_ref)
    count = 4
    for first in range(0, ext_x, count):
        rows = slice(first * ext_y * half, (first + count) * ext_y * half)
        grad_s[rows, :] = convolve(pad_ref, side_ref, conv_ref, first, count, True).astype(BF16)
    grad = grad_s[...]
    pairs = grad.shape[0]
    rows = got_ref.shape[0]
    step = min(256, rows)
    for start in range(0, rows, step):
        found = []
        for q in range(PACK):
            info = got_ref[start : start + step, q * LANE : (q + 1) * LANE].astype(F32)
            place = info[:, channels : channels + 1] * 32.0 + info[:, channels + 1 : channels + 2]
            pick = one_hot(iota((step, pairs), 1) == place.astype(jnp.int32))
            both = mm(pick, grad)
            odd = info[:, channels + 2 : channels + 3] > 0.5
            found.append(jnp.where(odd, both[:, LANE:], both[:, :LANE])[:, :channels])
        back_ref[start : start + step, :] = jnp.concatenate(found, axis=1).astype(BF16)


def join_kernel(terms_ref, back_ref, out_ref, *, block, per_axis):
    total = jnp.sum(terms_ref[...].astype(F32), axis=0)
    rows, wide = back_ref.shape
    out_ref[:, :wide] = back_ref[...]
    lines = total.shape[0] // 2
    halves = []
    for h in range(2):
        parts = [total[h * lines + k : h * lines + k + block] for k in range(0, lines, block)]
        half = jnp.concatenate(parts, axis=1)
        halves.append(jnp.concatenate([half] * per_axis, axis=0).astype(BF16))
    step = block * per_axis
    for g in range(rows // step):
        out_ref[g * step : (g + 1) * step, wide:] = halves[g % 2]


def collect_kernel(back_ref, slot_ref, out_ref):
    channels, points = out_ref.shape
    rows = back_ref.shape[0]
    back = back_ref[:, : PACK * channels]
    step = min(512, points)
    for start in range(0, points, step):
        row = slot_ref[0:1, start : start + step]
        quarter = slot_ref[1:2, start : start + step]
        pick = one_hot(iota((rows, step), 0) == row)
        found = mm(back, pick, TN)
        total = jnp.zeros((channels, step), F32)
        for q in range(PACK):
            total = jnp.where(quarter == q, found[q * channels : (q + 1) * channels], total)
        out_ref[:, start : start + step] = total.astype(BF16)


def unpack_kernel(core_ref, mine_ref, theirs_ref, conv_ref, down_ref, all_s, *, block):
    channels = conv_ref.shape[1]
    devices, count = all_s.shape[0], all_s.shape[1] // 2
    skip = mine_ref.shape[1] - theirs_ref.shape[1]
    swap = jnp.broadcast_to(core_ref[...], (block * devices, LANE)) > 0
    for k in range(count):
        mine = mine_ref[:, skip + k * LANE : skip + (k + 1) * LANE].astype(F32)
        theirs = theirs_ref[:, k * LANE : (k + 1) * LANE].astype(F32)
        shape = (devices, block, LANE)
        all_s[:, k] = jnp.where(swap, theirs, mine).reshape(shape)
        all_s[:, count + k] = jnp.where(swap, mine, theirs).reshape(shape)
    whole = all_s[...].reshape(devices * 2 * count * block, LANE)
    base = 27 * channels
    for j in range(27):
        conv_ref[j] = whole[j * channels : (j + 1) * channels, :channels]
    rest = down_ref.shape[2] - LANE
    for j in range(8):
        start = base + j * channels
        down_ref[j, :, :LANE] = whole[start : start + channels]
        start = base + (8 + j // 2) * channels
        tail = whole[start : start + channels]
        down_ref[j, :, LANE:] = tail[:, (j % 2) * rest : (j % 2 + 1) * rest]


def shift(block, axis, step):
    count = lax.axis_size(axis)
    pairs = [(i, i + step) for i in range(count) if 0 <= i + step < count]
    return lax.ppermute(block, axis, pairs)


def exchange(blocks):
    return lax.all_to_all(blocks, AXES, split_axis=0, concat_axis=0, tiled=True)


def shards(point_feats, point_owner, point_cell, occupancy, w_conv, w_down, cotangent):
    points, channels = point_feats.shape
    count_x, count_y = lax.axis_size("gx"), lax.axis_size("gy")
    devices = count_x * count_y
    cap = 32
    block = cap // PACK
    ext_x, ext_y, ext_z = occupancy.shape
    half = ext_z // 2
    pairs = ext_x * ext_y * half
    coarse = w_down.shape[2]
    coarse_x, coarse_y = ext_x // 2, ext_y // 2
    coarse_rows = coarse_x * coarse_y * half
    slot_rows = devices * block
    scale = 1.0 / math.sqrt(float(ext_x * ext_y * ext_z * devices))
    conv_flops = 2 * pairs * 18 * WIDE * WIDE
    pick_flops = 2 * pairs * slot_rows * PACK * WIDE

    send, slot = call(
        functools.partial(dispatch_kernel, devices=devices, cap=cap),
        (struct((slot_rows, PACK * LANE), BF16), struct((2, points), jnp.int32)),
        (point_feats.T, point_owner.reshape(1, points), point_cell.reshape(1, points)),
        "dispatch",
        flops=2 * points * slot_rows * PACK * LANE,
    )
    got = exchange(send.reshape(devices, block, PACK * LANE)).reshape(slot_rows, PACK * LANE)
    conv_blocks, down_blocks, given = call(
        functools.partial(prepare_kernel, ext_y=ext_y),
        (
            struct((9, 2, WIDE, WIDE), BF16),
            struct((4, WIDE, coarse), BF16),
            struct((coarse_rows, WIDE), BF16),
        ),
        (w_conv, w_down, cotangent.reshape(coarse_rows, coarse),
         occupancy.reshape(ext_x * ext_y, ext_z)),
        "prepare",
    )
    x_rows = 3 * ext_y * half + coarse_y * half
    grid, x_first, x_last = call(
        functools.partial(
            pool_kernel, channels=channels, rim=3, slab=ext_y * half, coarse_slab=coarse_y * half
        ),
        (struct((pairs, WIDE), BF16), struct((x_rows, WIDE), BF16), struct((x_rows, WIDE), BF16)),
        (got, given),
        "pool",
        scratch=[pltpu.VMEM((pairs, WIDE), F32)],
        flops=pick_flops,
    )
    x_low, x_high = shift(x_last, "gx", 1), shift(x_first, "gx", -1)
    y_rows = 3 * (ext_x + 6) * half + (coarse_x + 2) * half
    y_first, y_last = call(
        functools.partial(
            edge_kernel, fields=((ext_x, ext_y, half, 3), (coarse_x, coarse_y, half, 1))
        ),
        (struct((y_rows, WIDE), BF16), struct((y_rows, WIDE), BF16)),
        (grid, given, x_low, x_high),
        "edge",
    )
    y_low, y_high = shift(y_last, "gy", 1), shift(y_first, "gy", -1)
    near = (ext_x + 2, ext_y + 2, half, WIDE)
    near_rows = near[0] * near[1] * half
    far = (ext_x + 6, ext_y + 6, half, WIDE)
    split = (coarse_x + 2, 2, coarse_y + 2, 2, half, WIDE)
    features, fine, delta_coarse, delta, grid_near = call(
        level_kernel,
        (
            struct((coarse_rows, coarse), BF16),
            struct((pairs, WIDE), BF16),
            struct((coarse_rows, coarse), BF16),
            struct((near_rows, WIDE), BF16),
            struct((near_rows, WIDE), BF16),
        ),
        (grid, given, x_low, x_high, y_low, y_high, conv_blocks, down_blocks),
        "level",
        scratch=[
            pltpu.VMEM(far, F32),
            pltpu.VMEM(far, F32),
            pltpu.VMEM((coarse_x + 2, coarse_y + 2, half, WIDE), F32),
            pltpu.VMEM(split, F32),
            pltpu.VMEM(split, F32),
            pltpu.VMEM(split, F32),
        ],
        flops=2 * conv_flops,
        megabytes=8,
    )
    used = 39 * channels
    chunk = -(-used // (32 * devices)) * 32
    packed = call(
        functools.partial(weight_grad_kernel, channels=channels, scale=scale),
        struct((devices * chunk, LANE), BF16),
        (grid_near, fine, delta_coarse, delta),
        "weight_grad",
        scratch=[
            pltpu.VMEM(near, F32),
            pltpu.VMEM(near, F32),
            pltpu.VMEM(near, F32),
            pltpu.VMEM((coarse_x, 2, coarse_y, 2, half, WIDE), F32),
        ],
        flops=conv_flops,
        megabytes=8,
    )
    terms = exchange(packed.reshape(devices, chunk, LANE))
    back = call(
        functools.partial(input_grad_kernel, channels=channels),
        struct((slot_rows, PACK * channels), BF16),
        (delta, conv_blocks, got),
        "input_grad",
        scratch=[pltpu.VMEM(near, F32), pltpu.VMEM(near, F32), pltpu.VMEM((pairs, WIDE), BF16)],
        flops=conv_flops + pick_flops,
        megabytes=8,
    )
    half_lanes = chunk // 2 // block * LANE
    joined_lanes = PACK * channels + half_lanes
    joined = call(
        functools.partial(join_kernel, block=block, per_axis=count_y),
        struct((slot_rows, joined_lanes), BF16),
        (terms, back),
        "join",
        flops=devices * chunk * LANE,
    )
    returned = exchange(joined.reshape(devices, block, joined_lanes)).reshape(
        slot_rows, joined_lanes
    )
    theirs = lax.ppermute(
        returned[:, PACK * channels :], "gx", [(i, i ^ 1) for i in range(count_x)]
    )
    grad_points = call(
        collect_kernel,
        struct((channels, points), BF16),
        (returned, slot),
        "collect",
        flops=2 * points * slot_rows * PACK * LANE,
    ).T
    core = jnp.broadcast_to(lax.axis_index("gx") & 1, (1, LANE)).astype(jnp.int32)
    grad_conv, grad_down = call(
        functools.partial(unpack_kernel, block=block),
        (struct(w_conv.shape, F32), struct(w_down.shape, F32)),
        (core, returned, theirs),
        "unpack",
        scratch=[pltpu.VMEM((devices, chunk // block, block, LANE), F32)],
    )
    return (
        features.reshape(coarse_x, coarse_y, half, coarse),
        grad_points,
        grad_conv,
        grad_down,
    )


def solution(mesh):
    placed = (
        P(("gx", "gy"), None),
        P(("gx", "gy"), None),
        P(("gx", "gy")),
        P("gx", "gy", None),
        P(),
        P(),
        P("gx", "gy", None, None),
    )
    return jax.shard_map(
        shards,
        mesh=mesh,
        in_specs=placed,
        out_specs=(P("gx", "gy", None, None), P(("gx", "gy"), None), P(), P()),
        check_vma=False,
    )
```

```python
import functools
import math

import jax
import jax.numpy as jnp
from jax import lax
from jax.experimental import pallas as pl
from jax.experimental.pallas import tpu as pltpu
from jax.sharding import PartitionSpec as P

F32 = jnp.float32
BF16 = jnp.bfloat16
LANE = 128
WIDE = 256
PACK = 4
AXES = ("gx", "gy")
NT = (((1,), (1,)), ((), ()))
NN = (((1,), (0,)), ((), ()))
TN = (((0,), (0,)), ((), ()))


def iota(shape, dim):
    return lax.broadcasted_iota(jnp.int32, shape, dim)


def mm(a, b, dims=NN):
    return lax.dot_general(a, b, dims, preferred_element_type=F32)


def one_hot(mask):
    return jnp.where(mask, 1.0, 0.0).astype(BF16)


def call(kernel, outs, args, name, scratch=(), flops=0, megabytes=4):
    return pl.pallas_call(
        kernel,
        out_shape=outs,
        in_specs=[pl.BlockSpec(memory_space=pltpu.VMEM)] * len(args),
        out_specs=jax.tree.map(lambda _: pl.BlockSpec(memory_space=pltpu.VMEM), outs),
        scratch_shapes=list(scratch),
        compiler_params=pltpu.CompilerParams(vmem_limit_bytes=48 * 1024 * 1024),
        cost_estimate=pl.CostEstimate(
            flops=flops, bytes_accessed=megabytes * 1000000, transcendentals=0
        ),
        name=name,
    )(*args)


def struct(shape, dtype):
    return jax.ShapeDtypeStruct(shape, dtype)


def dispatch_kernel(feats_ref, owner_ref, cell_ref, send_ref, slot_ref, *, devices, cap):
    channels, points = feats_ref.shape
    owner = owner_ref[...]
    hot = iota((devices, points), 0) == owner
    block = min(256, points)
    upper = one_hot(iota((block, block), 0) < iota((block, block), 1))
    carry = jnp.zeros((devices, 1), F32)
    ranks = []
    for start in range(0, points, block):
        part = jnp.where(hot[:, start : start + block], 1.0, 0.0)
        before = mm(part.astype(BF16), upper) + carry
        ranks.append(jnp.sum(part * before, axis=0, keepdims=True))
        carry = carry + jnp.sum(part, axis=1, keepdims=True)
    rank = jnp.concatenate(ranks, axis=1).astype(jnp.int32)
    row = owner * (cap // PACK) + (rank >> 2)
    quarter = rank & 3
    slot_ref[0:1, :] = row
    slot_ref[1:2, :] = quarter
    cell = cell_ref[...]
    line = iota((LANE - channels, points), 0)
    extra = jnp.where(line == 0, cell >> 6, 0)
    extra = jnp.where(line == 1, (cell >> 1) & 31, extra)
    extra = jnp.where(line == 2, cell & 1, extra)
    whole = jnp.concatenate([feats_ref[...], extra.astype(F32).astype(BF16)], axis=0)
    spread = jnp.concatenate([whole * one_hot(quarter == q) for q in range(PACK)], axis=0)
    rows = send_ref.shape[0]
    step = min(256, rows)
    for start in range(0, rows, step):
        pick = one_hot(iota((step, points), 0) + start == row)
        send_ref[start : start + step, :] = mm(pick, spread, NT).astype(BF16)


def pool_kernel(
    got_ref, coarse_ref, grid_ref, x_first, x_last, y_first, y_last, total_ref, *, channels, fields
):
    rows = got_ref.shape[0]
    pairs = grid_ref.shape[0]
    lane = iota((8, LANE), 1)
    weigh = jnp.where(lane == channels, 32.0, jnp.where(lane == channels + 1, 1.0, 0.0))
    weigh = weigh.astype(BF16)
    step = 256
    for q in range(PACK):
        block = got_ref[:, q * LANE : (q + 1) * LANE]
        place = mm(weigh, block, NT)[0:1].astype(jnp.int32)
        odd = block * block[:, channels + 2 : channels + 3]
        both = jnp.concatenate([block - odd, odd], axis=1)
        for start in range(0, pairs, step):
            pick = one_hot(iota((step, rows), 0) + start == place)
            part = mm(pick, both)
            if q:
                part = total_ref[start : start + step, :] + part
            total_ref[start : start + step, :] = part
    x_at, y_at = 0, 0
    for ref, (ext_x, ext_y, half, rim) in zip((total_ref, coarse_ref), fields):
        field = as_field(ref[...], ext_x, ext_y, half)
        x_at = put_rows(x_first, x_at, field[:rim])
        put_rows(x_last, x_at - rim * ext_y * half, field[ext_x - rim :])
        y_at = put_rows(y_first, y_at, field[:, :rim])
        put_rows(y_last, y_at - rim * ext_x * half, field[:, ext_y - rim :])
    grid_ref[...] = total_ref[...].astype(BF16)


def as_field(rows, ext_x, ext_y, half):
    return rows.astype(F32).reshape(ext_x, ext_y, half, rows.shape[1])


def put_rows(ref, at, field):
    size = field.shape[0] * field.shape[1] * field.shape[2]
    ref[at : at + size, :] = field.reshape(size, field.shape[3]).astype(BF16)
    return at + size


def corner_kernel(low_ref, high_ref, first_ref, last_ref, *, fields):
    start, at = 0, 0
    for _, ext_y, half, rim in fields:
        size = rim * ext_y * half
        for ref in (low_ref, high_ref):
            field = as_field(ref[start : start + size, :], rim, ext_y, half)
            put_rows(first_ref, at, field[:, :rim])
            at = put_rows(last_ref, at, field[:, ext_y - rim :])
        start += size


def prepare_kernel(
    conv_ref, down_ref, cot_ref, occ_ref, conv_out, back_out, down_out, coarse_out, *, ext_y
):
    channels = conv_ref.shape[1]
    conv_out[...] = jnp.zeros(conv_out.shape, BF16)
    back_out[...] = jnp.zeros(back_out.shape, BF16)
    down_out[...] = jnp.zeros(down_out.shape, BF16)
    four = 4 * channels
    a, b = slice(0, channels), slice(LANE, LANE + channels)
    for j in range(9):
        for k in range(3):
            weight = conv_ref[3 * j + k]
            turned = weight.astype(F32).T.astype(BF16)
            for z in range(2):
                at, side = j * four + (k + z) * channels, (a, b)[z]
                conv_out[at : at + channels, side] = weight
                at = (8 - j) * four + (2 - k + z) * channels
                back_out[at : at + channels, side] = turned
    for j in range(4):
        down_out[j, a, :] = down_ref[2 * j]
        down_out[j, b, :] = down_ref[2 * j + 1]
    columns, depth = occ_ref.shape
    rows, coarse = cot_ref.shape
    half = depth // 2
    rest = WIDE - coarse
    occ = occ_ref[...].astype(F32).astype(BF16)
    row = iota((rows, columns), 0)
    place, column = row // half, iota((rows, columns), 1)
    base = place // (ext_y // 2) * 2 * ext_y + place % (ext_y // 2) * 2
    level = iota((rows, depth), 1) // 2 == iota((rows, depth), 0) % half
    total = jnp.zeros((rows, rest), F32)
    for j in range(4):
        pick = one_hot(base + j // 2 * ext_y + j % 2 == column)
        found = jnp.where(level, mm(pick, occ), 0.0).astype(BF16)
        spot = iota((depth, rest), 1) == 2 * j + iota((depth, rest), 0) % 2
        total = total + mm(found, one_hot(spot))
    coarse_out[:, :coarse] = cot_ref[...]
    coarse_out[:, coarse:] = total.astype(BF16)


def fill_four(pad_ref, four_ref, channels):
    ext_x, ext_y, half, wide = pad_ref.shape
    columns = ext_x * ext_y
    level = iota((columns, half, LANE), 1)
    even = pad_ref[:, :, :, :LANE].reshape(columns, half, LANE)
    odd = pad_ref[:, :, :, LANE:].reshape(columns, half, LANE)
    after = jnp.where(level == half - 1, 0.0, pltpu.roll(even, half - 1, 1))
    before = jnp.where(level == 0, 0.0, pltpu.roll(odd, 1, 1))
    parts = [part[:, :, :channels] for part in (before, even, odd, after)]
    four = jnp.concatenate(parts, axis=2)
    four_ref[...] = four.reshape(ext_x, ext_y, half, 4 * channels)


def windows(ref, first_x, count_x, first_y, count_y):
    parts = []
    for j in range(9):
        x, y = first_x + j // 3, first_y + j % 3
        part = ref[x : x + count_x, y : y + count_y]
        parts.append(part.reshape(count_x * count_y * part.shape[2], part.shape[3]).astype(BF16))
    return parts


def convolve(four_ref, weight_ref, boxes):
    rows = [jnp.concatenate(windows(four_ref, *box), axis=1) for box in boxes]
    return mm(rows[0] if len(rows) == 1 else jnp.concatenate(rows, axis=0), weight_ref[...])


def logistic(values):
    return 1.0 / (1.0 + jnp.exp(-values))


def silu_and_slope(pre):
    sigma = logistic(pre)
    return (pre * sigma).astype(BF16), sigma * (1.0 + pre * (1.0 - sigma))


def inner(field, rim):
    part = field[rim : field.shape[0] - rim, rim : field.shape[1] - rim]
    return part.reshape(part.shape[0] * part.shape[1] * part.shape[2], part.shape[3])


def column_kernel(
    grid_ref, x_low, x_high, conv_ref, silu_ref, slope_ref, pad_ref, four_ref, *, channels
):
    ext_x, ext_y, half = pad_ref.shape[0], pad_ref.shape[1], pad_ref.shape[2]
    rim = 3
    size = rim * ext_y * half
    pad_ref[:rim] = as_field(x_low[:size, :], rim, ext_y, half)
    pad_ref[rim : ext_x - rim] = as_field(grid_ref[...], ext_x - 2 * rim, ext_y, half)
    pad_ref[ext_x - rim :] = as_field(x_high[:size, :], rim, ext_y, half)
    fill_four(pad_ref, four_ref, channels)
    count = 4
    step = count * (ext_y - 2) * half
    for first in range(0, ext_x - 2, count):
        pre = convolve(four_ref, conv_ref, [(first, count, 0, ext_y - 2)])
        rows = slice(first // count * step, (first // count + 1) * step)
        silu_ref[rows, :], slope_ref[rows, :] = silu_and_slope(pre)


def level_kernel(
    grid_ref, coarse_ref, x_low, x_high, y_low, y_high, c_low, c_high, silu_ref, slope_ref,
    conv_ref, down_ref,
    features_ref, fine_ref, delta_coarse_ref, delta_ref,
    pad_ref, four_ref, coarse_s, mask_s, fine_s, slope_s, *, channels, fields,
):
    (ext_x, ext_y, half, rim), (coarse_x, coarse_y, _, _) = fields
    wide = WIDE
    slab, face, corner = rim * ext_y * half, ext_x * rim * half, rim * rim * half
    long = ext_x + 2 * rim
    grid = as_field(grid_ref[...], ext_x, ext_y, half)
    low = as_field(x_low[:slab, :], rim, ext_y, half)
    high = as_field(x_high[:slab, :], rim, ext_y, half)
    for s, (y_ref, c_ref) in enumerate(((y_low, c_low), (y_high, c_high))):
        ours, here, there = ((0, 3, 0), (ext_y - 2, 0, 2))[s]
        base = s * long
        parts = (
            (low, as_field(c_ref[:corner, :], rim, rim, half)),
            (grid, as_field(y_ref[:face, :], ext_x, rim, half)),
            (high, as_field(c_ref[corner : 2 * corner, :], rim, rim, half)),
        )
        at = base
        for mine, theirs in parts:
            count = mine.shape[0]
            pad_ref[at : at + count, here : here + 2] = mine[:, ours : ours + 2]
            pad_ref[at : at + count, there : there + rim] = theirs
            at += count
    fill_four(pad_ref, four_ref, channels)
    coarse_s[1 : 1 + coarse_x, 1 : 1 + coarse_y] = as_field(
        coarse_ref[...], coarse_x, coarse_y, half
    )
    coarse_s[:1, 1 : 1 + coarse_y] = as_field(x_low[slab:, :], 1, coarse_y, half)
    coarse_s[1 + coarse_x :, 1 : 1 + coarse_y] = as_field(x_high[slab:, :], 1, coarse_y, half)
    for y, y_ref, c_ref in ((0, y_low, c_low), (1 + coarse_y, y_high, c_high)):
        coarse_s[1 : 1 + coarse_x, y : y + 1] = as_field(y_ref[face:, :], coarse_x, 1, half)
        corners = as_field(c_ref[2 * corner :, :], 2, 1, half)
        coarse_s[:1, y : y + 1] = corners[:1]
        coarse_s[1 + coarse_x :, y : y + 1] = corners[1:]
    wide_x, wide_y = coarse_x + 2, coarse_y + 2
    coarse_rows = wide_x * wide_y * half
    coarse = down_ref.shape[2]
    given = coarse_s[...].reshape(coarse_rows, wide).astype(BF16)
    largest = None
    for j in range(4):
        spot = iota((wide, wide), 0) == coarse + 2 * j + iota((wide, wide), 1) // LANE
        mask = mm(given, one_hot(spot))
        mask_s[:, j // 2, :, j % 2] = mask.reshape(wide_x, wide_y, half, wide)
        largest = mask if largest is None else jnp.maximum(largest, mask)
    largest = jnp.maximum(largest[:, :LANE], largest[:, LANE:])
    coarse_mask = jnp.concatenate([largest, largest[:, : coarse - LANE]], axis=1)

    out_x, out_y = 2 * wide_x, 2 * wide_y
    strip = 3
    boxes = [(0, out_x, 0, strip), (long, out_x, 0, strip)]
    silu, slope = silu_and_slope(convolve(four_ref, conv_ref, boxes))
    shape = (2, out_x, strip, half, wide)
    edge_silu, edge_slope = silu.astype(F32).reshape(shape), slope.reshape(shape)
    columns = out_y - 2 * strip
    mid_silu = as_field(silu_ref[...], out_x, columns, half)
    mid_slope = slope_ref[...].reshape(out_x, columns, half, wide)
    shape = (wide_x, 2, half, wide)
    for y in range(out_y):
        if y < strip:
            silu, slope = edge_silu[0, :, y], edge_slope[0, :, y]
        elif y >= out_y - strip:
            at = y - (out_y - strip)
            silu, slope = edge_silu[1, :, at], edge_slope[1, :, at]
        else:
            silu, slope = mid_silu[:, y - strip], mid_slope[:, y - strip]
        mask = mask_s[:, :, y // 2, y % 2]
        fine_s[:, :, y // 2, y % 2] = silu.reshape(shape) * mask
        slope_s[:, :, y // 2, y % 2] = slope.reshape(shape) * mask
    field = (out_x, out_y, half, wide)
    fine_ref[...] = inner(fine_s[...].reshape(field), 2).astype(BF16)

    pre = None
    for j in range(4):
        piece = fine_s[:, j // 2, :, j % 2].reshape(coarse_rows, wide).astype(BF16)
        part = mm(piece, down_ref[j])
        pre = part if pre is None else pre + part
    sigma = logistic(pre)
    coarse_field = (wide_x, wide_y, half, coarse)
    features = pre * sigma * coarse_mask
    features_ref[...] = inner(features.reshape(coarse_field), 1).astype(BF16)
    slope = sigma * (1.0 + pre * (1.0 - sigma))
    cot = coarse_s[:, :, :, :coarse].reshape(coarse_rows, coarse)
    delta = cot * coarse_mask * slope
    delta_coarse_ref[...] = inner(delta.reshape(coarse_field), 1).astype(BF16)
    delta = delta.astype(BF16)
    for j in range(4):
        back = mm(delta, down_ref[j], NT).reshape(wide_x, wide_y, half, wide)
        fine_s[:, j // 2, :, j % 2] = back * slope_s[:, j // 2, :, j % 2]
    delta_ref[...] = inner(fine_s[...].reshape(field), 1).astype(BF16)


def weight_grad_kernel(
    grid_ref, x_low, x_high, y_low, y_high, c_low, c_high, fine_ref, delta_coarse_ref, delta_ref,
    out_ref, pad_ref, four_ref, delta_s, fine_s, *, channels, fields, scale,
):
    (ext_x, ext_y, half, rim), _ = fields
    slab, face, corner = rim * ext_y * half, ext_x * rim * half, rim * rim * half
    pad_ref[1 : 1 + ext_x, 1 : 1 + ext_y] = as_field(grid_ref[...], ext_x, ext_y, half)
    near = (rim - 1, 0)
    for x, x_ref, at in ((0, x_low, near[0]), (1 + ext_x, x_high, near[1])):
        field = as_field(x_ref[:slab, :], rim, ext_y, half)
        pad_ref[x : x + 1, 1 : 1 + ext_y] = field[at : at + 1]
    for y, y_ref, c_ref, at in ((0, y_low, c_low, near[0]), (1 + ext_y, y_high, c_high, near[1])):
        field = as_field(y_ref[:face, :], ext_x, rim, half)
        pad_ref[1 : 1 + ext_x, y : y + 1] = field[:, at : at + 1]
        field = as_field(c_ref[: 2 * corner, :], 2 * rim, rim, half)[:, at : at + 1]
        pad_ref[:1, y : y + 1] = field[rim - 1 : rim]
        pad_ref[1 + ext_x :, y : y + 1] = field[rim : rim + 1]
    fill_four(pad_ref, four_ref, channels)
    delta_s[...] = as_field(delta_ref[...], ext_x + 2, ext_y + 2, half)
    turned = inner(delta_s[...], 1).T.astype(BF16)
    three = 3 * channels
    for j, part in enumerate(windows(four_ref, 0, ext_x, 0, ext_y)):
        grad = mm(turned, part)
        grad = grad[:LANE, :three] + grad[LANE:, channels:]
        out_ref[j * three : (j + 1) * three, :] = (grad.T * scale).astype(BF16)
    fine_s[...] = fine_ref[...].astype(F32).reshape(fine_s.shape)
    coarse_rows = ext_x // 2 * (ext_y // 2) * half
    base = 27 * channels
    for j in range(4):
        piece = fine_s[:, j // 2, :, j % 2].reshape(coarse_rows, WIDE).astype(BF16)
        grad = mm(piece, delta_coarse_ref[...], TN) * scale
        first, second = grad[:channels], grad[LANE : LANE + channels]
        start = base + 2 * j * channels
        out_ref[start : start + channels, :] = first[:, :LANE].astype(BF16)
        out_ref[start + channels : start + 2 * channels, :] = second[:, :LANE].astype(BF16)
        start = base + (8 + j) * channels
        tail = jnp.concatenate([first[:, LANE:], second[:, LANE:]], axis=1)
        out_ref[start : start + channels, :] = tail.astype(BF16)
    end = base + 12 * channels
    out_ref[end:, :] = jnp.zeros((out_ref.shape[0] - end, LANE), BF16)


def input_grad_kernel(delta_ref, conv_ref, got_ref, back_ref, pad_ref, four_ref, grad_s, *, channels):
    ext_x, ext_y, half = pad_ref.shape[0] - 2, pad_ref.shape[1] - 2, pad_ref.shape[2]
    pad_ref[...] = as_field(delta_ref[...], ext_x + 2, ext_y + 2, half)
    fill_four(pad_ref, four_ref, channels)
    count = 4
    for first in range(0, ext_x, count):
        rows = slice(first * ext_y * half, (first + count) * ext_y * half)
        grad_s[rows, :] = convolve(four_ref, conv_ref, [(first, count, 0, ext_y)]).astype(BF16)
    grad = grad_s[...]
    pairs = grad.shape[0]
    rows = got_ref.shape[0]
    step = min(256, rows)
    for start in range(0, rows, step):
        found = []
        for q in range(PACK):
            info = got_ref[start : start + step, q * LANE : (q + 1) * LANE].astype(F32)
            place = info[:, channels : channels + 1] * 32.0 + info[:, channels + 1 : channels + 2]
            pick = one_hot(iota((step, pairs), 1) == place.astype(jnp.int32))
            both = mm(pick, grad)
            odd = info[:, channels + 2 : channels + 3] > 0.5
            found.append(jnp.where(odd, both[:, LANE:], both[:, :LANE])[:, :channels])
        back_ref[start : start + step, :] = jnp.concatenate(found, axis=1).astype(BF16)


def join_kernel(terms_ref, back_ref, out_ref, *, block, per_axis):
    total = jnp.sum(terms_ref[...].astype(F32), axis=0)
    rows, wide = back_ref.shape
    out_ref[:, :wide] = back_ref[...]
    lines = total.shape[0] // 2
    halves = []
    for h in range(2):
        parts = [total[h * lines + k : h * lines + k + block] for k in range(0, lines, block)]
        half = jnp.concatenate(parts, axis=1)
        halves.append(jnp.concatenate([half] * per_axis, axis=0).astype(BF16))
    step = block * per_axis
    for g in range(rows // step):
        out_ref[g * step : (g + 1) * step, wide:] = halves[g % 2]


def collect_kernel(back_ref, slot_ref, out_ref):
    channels, points = out_ref.shape
    rows = back_ref.shape[0]
    back = back_ref[:, : PACK * channels]
    step = min(512, points)
    for start in range(0, points, step):
        row = slot_ref[0:1, start : start + step]
        quarter = slot_ref[1:2, start : start + step]
        pick = one_hot(iota((rows, step), 0) == row)
        found = mm(back, pick, TN)
        total = jnp.zeros((channels, step), F32)
        for q in range(PACK):
            total = jnp.where(quarter == q, found[q * channels : (q + 1) * channels], total)
        out_ref[:, start : start + step] = total.astype(BF16)


def unpack_kernel(core_ref, mine_ref, theirs_ref, conv_ref, down_ref, all_s, *, block):
    channels = conv_ref.shape[1]
    devices, count = all_s.shape[0], all_s.shape[1] // 2
    skip = mine_ref.shape[1] - theirs_ref.shape[1]
    swap = jnp.broadcast_to(core_ref[...], (block * devices, LANE)) > 0
    for k in range(count):
        mine = mine_ref[:, skip + k * LANE : skip + (k + 1) * LANE].astype(F32)
        theirs = theirs_ref[:, k * LANE : (k + 1) * LANE].astype(F32)
        shape = (devices, block, LANE)
        all_s[:, k] = jnp.where(swap, theirs, mine).reshape(shape)
        all_s[:, count + k] = jnp.where(swap, mine, theirs).reshape(shape)
    whole = all_s[...].reshape(devices * 2 * count * block, LANE)
    base = 27 * channels
    for j in range(27):
        conv_ref[j] = whole[j * channels : (j + 1) * channels, :channels]
    rest = down_ref.shape[2] - LANE
    for j in range(8):
        start = base + j * channels
        down_ref[j, :, :LANE] = whole[start : start + channels]
        start = base + (8 + j // 2) * channels
        tail = whole[start : start + channels]
        down_ref[j, :, LANE:] = tail[:, (j % 2) * rest : (j % 2 + 1) * rest]


def shift(block, axis, step):
    count = lax.axis_size(axis)
    pairs = [(i, i + step) for i in range(count) if 0 <= i + step < count]
    return lax.ppermute(block, axis, pairs)


def exchange(blocks):
    return lax.all_to_all(blocks, AXES, split_axis=0, concat_axis=0, tiled=True)


def shards(point_feats, point_owner, point_cell, occupancy, w_conv, w_down, cotangent):
    points, channels = point_feats.shape
    count_x, count_y = lax.axis_size("gx"), lax.axis_size("gy")
    devices = count_x * count_y
    cap = 32
    block = cap // PACK
    ext_x, ext_y, ext_z = occupancy.shape
    half = ext_z // 2
    pairs = ext_x * ext_y * half
    coarse = w_down.shape[2]
    coarse_x, coarse_y = ext_x // 2, ext_y // 2
    coarse_rows = coarse_x * coarse_y * half
    slot_rows = devices * block
    scale = 1.0 / math.sqrt(float(ext_x * ext_y * ext_z * devices))
    four = 4 * channels
    conv_flops = 2 * pairs * 9 * four * WIDE
    pick_flops = 2 * pairs * slot_rows * PACK * WIDE
    rim = 3
    fields = ((ext_x, ext_y, half, rim), (coarse_x, coarse_y, half, 1))

    send, slot = call(
        functools.partial(dispatch_kernel, devices=devices, cap=cap),
        (struct((slot_rows, PACK * LANE), BF16), struct((2, points), jnp.int32)),
        (point_feats.T, point_owner.reshape(1, points), point_cell.reshape(1, points)),
        "dispatch",
        flops=2 * points * slot_rows * PACK * LANE,
    )
    got = exchange(send.reshape(devices, block, PACK * LANE)).reshape(slot_rows, PACK * LANE)
    conv_blocks, back_blocks, down_blocks, given = call(
        functools.partial(prepare_kernel, ext_y=ext_y),
        (
            struct((9 * four, WIDE), BF16),
            struct((9 * four, WIDE), BF16),
            struct((4, WIDE, coarse), BF16),
            struct((coarse_rows, WIDE), BF16),
        ),
        (w_conv, w_down, cotangent.reshape(coarse_rows, coarse),
         occupancy.reshape(ext_x * ext_y, ext_z)),
        "prepare",
        flops=1000000000,
    )
    x_rows = sum(e[3] * e[1] * e[2] for e in fields)
    y_rows = sum(e[3] * e[0] * e[2] for e in fields)
    c_rows = sum(2 * e[3] * e[3] * e[2] for e in fields)
    grid, x_first, x_last, y_first, y_last = call(
        functools.partial(pool_kernel, channels=channels, fields=fields),
        tuple(struct((n, WIDE), BF16) for n in (pairs, x_rows, x_rows, y_rows, y_rows)),
        (got, given),
        "pool",
        scratch=[pltpu.VMEM((pairs, WIDE), F32)],
        flops=pick_flops,
    )
    x_low, x_high = shift(x_last, "gx", 1), shift(x_first, "gx", -1)
    y_low, y_high = shift(y_last, "gy", 1), shift(y_first, "gy", -1)
    c_first, c_last = call(
        functools.partial(corner_kernel, fields=fields),
        tuple(struct((n, WIDE), BF16) for n in (c_rows, c_rows)),
        (x_low, x_high),
        "corner",
    )
    c_low, c_high = shift(c_last, "gy", 1), shift(c_first, "gy", -1)
    long = ext_x + 2 * rim
    mid_rows = (ext_x + 4) * (ext_y - 2) * half
    silu, slope = call(
        functools.partial(column_kernel, channels=channels),
        (struct((mid_rows, WIDE), BF16), struct((mid_rows, WIDE), F32)),
        (grid, x_low, x_high, conv_blocks),
        "column",
        scratch=[
            pltpu.VMEM((long, ext_y, half, WIDE), F32),
            pltpu.VMEM((long, ext_y, half, four), F32),
        ],
        flops=2 * conv_flops,
    )
    near = (ext_x + 2, ext_y + 2, half)
    near_rows = near[0] * near[1] * half
    split = (coarse_x + 2, 2, coarse_y + 2, 2, half, WIDE)
    faces = (x_low, x_high, y_low, y_high, c_low, c_high)
    features, fine, delta_coarse, delta = call(
        functools.partial(level_kernel, channels=channels, fields=fields),
        (
            struct((coarse_rows, coarse), BF16),
            struct((pairs, WIDE), BF16),
            struct((coarse_rows, coarse), BF16),
            struct((near_rows, WIDE), BF16),
        ),
        (grid, given, *faces, silu, slope, conv_blocks, down_blocks),
        "level",
        scratch=[
            pltpu.VMEM((2 * long, 5, half, WIDE), F32),
            pltpu.VMEM((2 * long, 5, half, four), F32),
            pltpu.VMEM((coarse_x + 2, coarse_y + 2, half, WIDE), F32),
            pltpu.VMEM(split, F32),
            pltpu.VMEM(split, F32),
            pltpu.VMEM(split, F32),
        ],
        flops=conv_flops,
        megabytes=8,
    )
    used = 39 * channels
    chunk = -(-used // (32 * devices)) * 32
    packed = call(
        functools.partial(weight_grad_kernel, channels=channels, fields=fields, scale=scale),
        struct((devices * chunk, LANE), BF16),
        (grid, *faces, fine, delta_coarse, delta),
        "weight_grad",
        scratch=[
            pltpu.VMEM((*near, WIDE), F32),
            pltpu.VMEM((*near, four), F32),
            pltpu.VMEM((*near, WIDE), F32),
            pltpu.VMEM((coarse_x, 2, coarse_y, 2, half, WIDE), F32),
        ],
        flops=conv_flops,
        megabytes=8,
    )
    terms = exchange(packed.reshape(devices, chunk, LANE))
    back = call(
        functools.partial(input_grad_kernel, channels=channels),
        struct((slot_rows, PACK * channels), BF16),
        (delta, back_blocks, got),
        "input_grad",
        scratch=[
            pltpu.VMEM((*near, WIDE), F32),
            pltpu.VMEM((*near, four), F32),
            pltpu.VMEM((pairs, WIDE), BF16),
        ],
        flops=conv_flops + pick_flops,
        megabytes=8,
    )
    half_lanes = chunk // 2 // block * LANE
    joined_lanes = PACK * channels + half_lanes
    joined = call(
        functools.partial(join_kernel, block=block, per_axis=count_y),
        struct((slot_rows, joined_lanes), BF16),
        (terms, back),
        "join",
        flops=devices * chunk * LANE,
    )
    returned = exchange(joined.reshape(devices, block, joined_lanes)).reshape(
        slot_rows, joined_lanes
    )
    theirs = lax.ppermute(
        returned[:, PACK * channels :], "gx", [(i, i ^ 1) for i in range(count_x)]
    )
    grad_points = call(
        collect_kernel,
        struct((channels, points), BF16),
        (returned, slot),
        "collect",
        flops=2 * points * slot_rows * PACK * LANE,
    ).T
    core = jnp.broadcast_to(lax.axis_index("gx") & 1, (1, LANE)).astype(jnp.int32)
    grad_conv, grad_down = call(
        functools.partial(unpack_kernel, block=block),
        (struct(w_conv.shape, F32), struct(w_down.shape, F32)),
        (core, returned, theirs),
        "unpack",
        scratch=[pltpu.VMEM((devices, chunk // block, block, LANE), F32)],
    )
    return (
        features.reshape(coarse_x, coarse_y, half, coarse),
        grad_points,
        grad_conv,
        grad_down,
    )


def solution(mesh):
    placed = (
        P(("gx", "gy"), None),
        P(("gx", "gy"), None),
        P(("gx", "gy")),
        P("gx", "gy", None),
        P(),
        P(),
        P("gx", "gy", None, None),
    )
    return jax.shard_map(
        shards,
        mesh=mesh,
        in_specs=placed,
        out_specs=(P("gx", "gy", None, None), P(("gx", "gy"), None), P(), P()),
        check_vma=False,
    )
```

```python
import functools
import math

import jax
import jax.numpy as jnp
from jax import lax
from jax.experimental import pallas as pl
from jax.experimental.pallas import tpu as pltpu
from jax.sharding import PartitionSpec as P

F32 = jnp.float32
BF16 = jnp.bfloat16
LANE = 128
WIDE = 256
PACK = 4
AXES = ("gx", "gy")
NT = (((1,), (1,)), ((), ()))
NN = (((1,), (0,)), ((), ()))
TN = (((0,), (0,)), ((), ()))


def iota(shape, dim):
    return lax.broadcasted_iota(jnp.int32, shape, dim)


def mm(a, b, dims=NN):
    return lax.dot_general(a, b, dims, preferred_element_type=F32)


def one_hot(mask):
    return jnp.where(mask, 1.0, 0.0).astype(BF16)


def call(kernel, outs, args, name, scratch=(), flops=0, megabytes=4):
    return pl.pallas_call(
        kernel,
        out_shape=outs,
        in_specs=[
            pl.BlockSpec(memory_space=pltpu.SMEM if arg.ndim == 1 else pltpu.VMEM) for arg in args
        ],
        out_specs=jax.tree.map(lambda _: pl.BlockSpec(memory_space=pltpu.VMEM), outs),
        scratch_shapes=list(scratch),
        compiler_params=pltpu.CompilerParams(vmem_limit_bytes=48 * 1024 * 1024),
        cost_estimate=pl.CostEstimate(
            flops=flops, bytes_accessed=megabytes * 1000000, transcendentals=0
        ),
        name=name,
    )(*args)


def struct(shape, dtype):
    return jax.ShapeDtypeStruct(shape, dtype)


def dispatch_kernel(feats_ref, owner_ref, cell_ref, send_ref, slot_ref, *, devices, cap):
    channels, points = feats_ref.shape
    owner = owner_ref[...]
    hot = iota((devices, points), 0) == owner
    block = min(256, points)
    upper = one_hot(iota((block, block), 0) < iota((block, block), 1))
    carry = jnp.zeros((devices, 1), F32)
    ranks = []
    for start in range(0, points, block):
        part = jnp.where(hot[:, start : start + block], 1.0, 0.0)
        before = mm(part.astype(BF16), upper) + carry
        ranks.append(jnp.sum(part * before, axis=0, keepdims=True))
        carry = carry + jnp.sum(part, axis=1, keepdims=True)
    rank = jnp.concatenate(ranks, axis=1).astype(jnp.int32)
    row = owner * (cap // PACK) + (rank >> 2)
    quarter = rank & 3
    slot_ref[0:1, :] = row
    slot_ref[1:2, :] = quarter
    cell = cell_ref[...]
    line = iota((LANE - channels, points), 0)
    extra = jnp.where(line == 0, cell >> 6, 0)
    extra = jnp.where(line == 1, (cell >> 1) & 31, extra)
    extra = jnp.where(line == 2, cell & 1, extra)
    whole = jnp.concatenate([feats_ref[...], extra.astype(F32).astype(BF16)], axis=0)
    spread = jnp.concatenate([whole * one_hot(quarter == q) for q in range(PACK)], axis=0)
    rows = send_ref.shape[0]
    step = min(256, rows)
    for start in range(0, rows, step):
        pick = one_hot(iota((step, points), 0) + start == row)
        send_ref[start : start + step, :] = mm(pick, spread, NT).astype(BF16)


def pool_kernel(
    place_ref, got_ref, coarse_ref, grid_ref, x_first, x_last, y_first, y_last,
    c_first_first, c_first_last, c_last_first, c_last_last, total_ref, *, channels, fields, counts,
):
    rows = got_ref.shape[0]
    pairs = grid_ref.shape[0]
    lane = iota((8, LANE), 1)
    weigh = jnp.where(lane == channels, 32.0, jnp.where(lane == channels + 1, 1.0, 0.0))
    weigh = weigh.astype(BF16)
    step = 256
    for q in range(PACK):
        block = got_ref[:, q * LANE : (q + 1) * LANE]
        place = mm(weigh, block, NT)[0:1].astype(jnp.int32)
        odd = block * block[:, channels + 2 : channels + 3]
        both = jnp.concatenate([block - odd, odd], axis=1)
        for start in range(0, pairs, step):
            pick = one_hot(iota((step, rows), 0) + start == place)
            part = mm(pick, both)
            if q:
                part = total_ref[start : start + step, :] + part
            total_ref[start : start + step, :] = part
    x_inner = [jnp.where(place_ref[0] == end, 0.0, 1.0) for end in (0, counts[0] - 1)]
    y_inner = [jnp.where(place_ref[1] == end, 0.0, 1.0) for end in (0, counts[1] - 1)]
    corners = ((c_first_first, c_first_last), (c_last_first, c_last_last))
    x_at, y_at, c_at = 0, 0, 0
    for ref, (ext_x, ext_y, half, rim) in zip((total_ref, coarse_ref), fields):
        field = as_field(ref[...], ext_x, ext_y, half)
        x_cuts = [slice(0, rim), slice(ext_x - rim, ext_x)]
        y_cuts = [slice(0, rim), slice(ext_y - rim, ext_y)]
        for i, x_ref in enumerate((x_first, x_last)):
            put_rows(x_ref, x_at, field[x_cuts[i]] * x_inner[i])
            put_rows((y_first, y_last)[i], y_at, field[:, y_cuts[i]] * y_inner[i])
            for k in range(2):
                part = field[x_cuts[i], y_cuts[k]] * (x_inner[i] * y_inner[k])
                put_rows(corners[i][k], c_at, part)
        x_at += rim * ext_y * half
        y_at += rim * ext_x * half
        c_at += rim * rim * half
    grid_ref[...] = total_ref[...].astype(BF16)


def as_field(rows, ext_x, ext_y, half):
    return rows.astype(F32).reshape(ext_x, ext_y, half, rows.shape[1])


def put_rows(ref, at, field):
    size = field.shape[0] * field.shape[1] * field.shape[2]
    ref[at : at + size, :] = field.reshape(size, field.shape[3]).astype(BF16)


def prepare_kernel(
    conv_ref, down_ref, cot_ref, occ_ref, conv_out, back_out, down_out, coarse_out, *, ext_y
):
    channels = conv_ref.shape[1]
    conv_out[...] = jnp.zeros(conv_out.shape, BF16)
    back_out[...] = jnp.zeros(back_out.shape, BF16)
    down_out[...] = jnp.zeros(down_out.shape, BF16)
    four = 4 * channels
    a, b = slice(0, channels), slice(LANE, LANE + channels)
    for j in range(9):
        for k in range(3):
            weight = conv_ref[3 * j + k]
            turned = weight.astype(F32).T.astype(BF16)
            for z in range(2):
                at, side = j * four + (k + z) * channels, (a, b)[z]
                conv_out[at : at + channels, side] = weight
                at = (8 - j) * four + (2 - k + z) * channels
                back_out[at : at + channels, side] = turned
    for j in range(4):
        down_out[j, a, :] = down_ref[2 * j]
        down_out[j, b, :] = down_ref[2 * j + 1]
    columns, depth = occ_ref.shape
    rows, coarse = cot_ref.shape
    half = depth // 2
    rest = WIDE - coarse
    occ = occ_ref[...].astype(F32).astype(BF16)
    row = iota((rows, columns), 0)
    place, column = row // half, iota((rows, columns), 1)
    base = place // (ext_y // 2) * 2 * ext_y + place % (ext_y // 2) * 2
    level = iota((rows, depth), 1) // 2 == iota((rows, depth), 0) % half
    total = jnp.zeros((rows, rest), F32)
    for j in range(4):
        pick = one_hot(base + j // 2 * ext_y + j % 2 == column)
        found = jnp.where(level, mm(pick, occ), 0.0).astype(BF16)
        spot = iota((depth, rest), 1) == 2 * j + iota((depth, rest), 0) % 2
        total = total + mm(found, one_hot(spot))
    coarse_out[:, :coarse] = cot_ref[...]
    coarse_out[:, coarse:] = total.astype(BF16)


def fill_four(pad_ref, four_ref, channels):
    ext_x, ext_y, half, wide = pad_ref.shape
    columns = ext_x * ext_y
    level = iota((columns, half, LANE), 1)
    even = pad_ref[:, :, :, :LANE].reshape(columns, half, LANE)
    odd = pad_ref[:, :, :, LANE:].reshape(columns, half, LANE)
    after = jnp.where(level == half - 1, 0.0, pltpu.roll(even, half - 1, 1))
    before = jnp.where(level == 0, 0.0, pltpu.roll(odd, 1, 1))
    parts = [part[:, :, :channels] for part in (before, even, odd, after)]
    four = jnp.concatenate(parts, axis=2)
    four_ref[...] = four.reshape(ext_x, ext_y, half, 4 * channels)


def windows(ref, first_x, count_x, first_y, count_y):
    parts = []
    for j in range(9):
        x, y = first_x + j // 3, first_y + j % 3
        part = ref[x : x + count_x, y : y + count_y]
        parts.append(part.reshape(count_x * count_y * part.shape[2], part.shape[3]).astype(BF16))
    return parts


def convolve(four_ref, weight_ref, boxes):
    rows = [jnp.concatenate(windows(four_ref, *box), axis=1) for box in boxes]
    return mm(rows[0] if len(rows) == 1 else jnp.concatenate(rows, axis=0), weight_ref[...])


def logistic(values):
    return 1.0 / (1.0 + jnp.exp(-values))


def silu_and_slope(pre):
    sigma = logistic(pre)
    return (pre * sigma).astype(BF16), sigma * (1.0 + pre * (1.0 - sigma))


def inner(field, rim):
    part = field[rim : field.shape[0] - rim, rim : field.shape[1] - rim]
    return part.reshape(part.shape[0] * part.shape[1] * part.shape[2], part.shape[3])


def column_kernel(
    grid_ref, x_low, x_high, conv_ref, silu_ref, slope_ref, pad_ref, four_ref, *, channels
):
    ext_x, ext_y, half = pad_ref.shape[0], pad_ref.shape[1], pad_ref.shape[2]
    rim = 3
    size = rim * ext_y * half
    pad_ref[:rim] = as_field(x_low[:size, :], rim, ext_y, half)
    pad_ref[rim : ext_x - rim] = as_field(grid_ref[...], ext_x - 2 * rim, ext_y, half)
    pad_ref[ext_x - rim :] = as_field(x_high[:size, :], rim, ext_y, half)
    fill_four(pad_ref, four_ref, channels)
    count = 4
    step = count * (ext_y - 2) * half
    for first in range(0, ext_x - 2, count):
        pre = convolve(four_ref, conv_ref, [(first, count, 0, ext_y - 2)])
        rows = slice(first // count * step, (first // count + 1) * step)
        silu_ref[rows, :], slope_ref[rows, :] = silu_and_slope(pre)


def level_kernel(
    grid_ref, coarse_ref, x_low, x_high, y_low, y_high, c_ll, c_lh, c_hl, c_hh, silu_ref, slope_ref,
    conv_ref, down_ref,
    features_ref, fine_ref, delta_coarse_ref, delta_ref,
    pad_ref, four_ref, coarse_s, mask_s, fine_s, slope_s, *, channels, fields,
):
    (ext_x, ext_y, half, rim), (coarse_x, coarse_y, _, _) = fields
    wide = WIDE
    slab, face, corner = rim * ext_y * half, ext_x * rim * half, rim * rim * half
    long = ext_x + 2 * rim
    grid = as_field(grid_ref[...], ext_x, ext_y, half)
    low = as_field(x_low[:slab, :], rim, ext_y, half)
    high = as_field(x_high[:slab, :], rim, ext_y, half)
    for s, (y_ref, c_low, c_high) in enumerate(((y_low, c_ll, c_hl), (y_high, c_lh, c_hh))):
        ours, here, there = ((0, 3, 0), (ext_y - 2, 0, 2))[s]
        base = s * long
        parts = (
            (low, as_field(c_low[:corner, :], rim, rim, half)),
            (grid, as_field(y_ref[:face, :], ext_x, rim, half)),
            (high, as_field(c_high[:corner, :], rim, rim, half)),
        )
        at = base
        for mine, theirs in parts:
            count = mine.shape[0]
            pad_ref[at : at + count, here : here + 2] = mine[:, ours : ours + 2]
            pad_ref[at : at + count, there : there + rim] = theirs
            at += count
    fill_four(pad_ref, four_ref, channels)
    coarse_s[1 : 1 + coarse_x, 1 : 1 + coarse_y] = as_field(
        coarse_ref[...], coarse_x, coarse_y, half
    )
    coarse_s[:1, 1 : 1 + coarse_y] = as_field(x_low[slab:, :], 1, coarse_y, half)
    coarse_s[1 + coarse_x :, 1 : 1 + coarse_y] = as_field(x_high[slab:, :], 1, coarse_y, half)
    for y, y_ref, c_low, c_high in ((0, y_low, c_ll, c_hl), (1 + coarse_y, y_high, c_lh, c_hh)):
        coarse_s[1 : 1 + coarse_x, y : y + 1] = as_field(y_ref[face:, :], coarse_x, 1, half)
        coarse_s[:1, y : y + 1] = as_field(c_low[corner:, :], 1, 1, half)
        coarse_s[1 + coarse_x :, y : y + 1] = as_field(c_high[corner:, :], 1, 1, half)
    wide_x, wide_y = coarse_x + 2, coarse_y + 2
    coarse_rows = wide_x * wide_y * half
    coarse = down_ref.shape[2]
    given = coarse_s[...].reshape(coarse_rows, wide).astype(BF16)
    largest = None
    for j in range(4):
        spot = iota((wide, wide), 0) == coarse + 2 * j + iota((wide, wide), 1) // LANE
        mask = mm(given, one_hot(spot))
        mask_s[:, j // 2, :, j % 2] = mask.reshape(wide_x, wide_y, half, wide)
        largest = mask if largest is None else jnp.maximum(largest, mask)
    largest = jnp.maximum(largest[:, :LANE], largest[:, LANE:])
    coarse_mask = jnp.concatenate([largest, largest[:, : coarse - LANE]], axis=1)

    out_x, out_y = 2 * wide_x, 2 * wide_y
    strip = 3
    boxes = [(0, out_x, 0, strip), (long, out_x, 0, strip)]
    silu, slope = silu_and_slope(convolve(four_ref, conv_ref, boxes))
    shape = (2, out_x, strip, half, wide)
    edge_silu, edge_slope = silu.astype(F32).reshape(shape), slope.reshape(shape)
    columns = out_y - 2 * strip
    mid_silu = as_field(silu_ref[...], out_x, columns, half)
    mid_slope = slope_ref[...].reshape(out_x, columns, half, wide)
    shape = (wide_x, 2, half, wide)
    for y in range(out_y):
        if y < strip:
            silu, slope = edge_silu[0, :, y], edge_slope[0, :, y]
        elif y >= out_y - strip:
            at = y - (out_y - strip)
            silu, slope = edge_silu[1, :, at], edge_slope[1, :, at]
        else:
            silu, slope = mid_silu[:, y - strip], mid_slope[:, y - strip]
        mask = mask_s[:, :, y // 2, y % 2]
        fine_s[:, :, y // 2, y % 2] = silu.reshape(shape) * mask
        slope_s[:, :, y // 2, y % 2] = slope.reshape(shape) * mask
    field = (out_x, out_y, half, wide)
    fine_ref[...] = inner(fine_s[...].reshape(field), 2).astype(BF16)

    pre = None
    for j in range(4):
        piece = fine_s[:, j // 2, :, j % 2].reshape(coarse_rows, wide).astype(BF16)
        part = mm(piece, down_ref[j])
        pre = part if pre is None else pre + part
    sigma = logistic(pre)
    coarse_field = (wide_x, wide_y, half, coarse)
    features = pre * sigma * coarse_mask
    features_ref[...] = inner(features.reshape(coarse_field), 1).astype(BF16)
    slope = sigma * (1.0 + pre * (1.0 - sigma))
    cot = coarse_s[:, :, :, :coarse].reshape(coarse_rows, coarse)
    delta = cot * coarse_mask * slope
    delta_coarse_ref[...] = inner(delta.reshape(coarse_field), 1).astype(BF16)
    delta = delta.astype(BF16)
    for j in range(4):
        back = mm(delta, down_ref[j], NT).reshape(wide_x, wide_y, half, wide)
        fine_s[:, j // 2, :, j % 2] = back * slope_s[:, j // 2, :, j % 2]
    delta_ref[...] = inner(fine_s[...].reshape(field), 1).astype(BF16)


def weight_grad_kernel(
    grid_ref, x_low, x_high, y_low, y_high, c_ll, c_lh, c_hl, c_hh, fine_ref, delta_coarse_ref,
    delta_ref,
    out_ref, pad_ref, four_ref, delta_s, fine_s, *, channels, fields, scale,
):
    (ext_x, ext_y, half, rim), _ = fields
    slab, face, corner = rim * ext_y * half, ext_x * rim * half, rim * rim * half
    pad_ref[1 : 1 + ext_x, 1 : 1 + ext_y] = as_field(grid_ref[...], ext_x, ext_y, half)
    near = (rim - 1, 0)
    for x, x_ref, at in ((0, x_low, near[0]), (1 + ext_x, x_high, near[1])):
        field = as_field(x_ref[:slab, :], rim, ext_y, half)
        pad_ref[x : x + 1, 1 : 1 + ext_y] = field[at : at + 1]
    ends = ((0, y_low, c_ll, c_hl, near[0]), (1 + ext_y, y_high, c_lh, c_hh, near[1]))
    for y, y_ref, c_low, c_high, at in ends:
        field = as_field(y_ref[:face, :], ext_x, rim, half)
        pad_ref[1 : 1 + ext_x, y : y + 1] = field[:, at : at + 1]
        field = as_field(c_low[:corner, :], rim, rim, half)
        pad_ref[:1, y : y + 1] = field[near[0] : near[0] + 1, at : at + 1]
        field = as_field(c_high[:corner, :], rim, rim, half)
        pad_ref[1 + ext_x :, y : y + 1] = field[near[1] : near[1] + 1, at : at + 1]
    fill_four(pad_ref, four_ref, channels)
    delta_s[...] = as_field(delta_ref[...], ext_x + 2, ext_y + 2, half)
    turned = inner(delta_s[...], 1).T.astype(BF16)
    three = 3 * channels
    for j, part in enumerate(windows(four_ref, 0, ext_x, 0, ext_y)):
        grad = mm(turned, part)
        grad = grad[:LANE, :three] + grad[LANE:, channels:]
        out_ref[j * three : (j + 1) * three, :] = (grad.T * scale).astype(BF16)
    fine_s[...] = fine_ref[...].astype(F32).reshape(fine_s.shape)
    coarse_rows = ext_x // 2 * (ext_y // 2) * half
    base = 27 * channels
    for j in range(4):
        piece = fine_s[:, j // 2, :, j % 2].reshape(coarse_rows, WIDE).astype(BF16)
        grad = mm(piece, delta_coarse_ref[...], TN) * scale
        first, second = grad[:channels], grad[LANE : LANE + channels]
        start = base + 2 * j * channels
        out_ref[start : start + channels, :] = first[:, :LANE].astype(BF16)
        out_ref[start + channels : start + 2 * channels, :] = second[:, :LANE].astype(BF16)
        start = base + (8 + j) * channels
        tail = jnp.concatenate([first[:, LANE:], second[:, LANE:]], axis=1)
        out_ref[start : start + channels, :] = tail.astype(BF16)
    end = base + 12 * channels
    out_ref[end:, :] = jnp.zeros((out_ref.shape[0] - end, LANE), BF16)


def input_grad_kernel(delta_ref, conv_ref, got_ref, back_ref, pad_ref, four_ref, grad_s, *, channels):
    ext_x, ext_y, half = pad_ref.shape[0] - 2, pad_ref.shape[1] - 2, pad_ref.shape[2]
    pad_ref[...] = as_field(delta_ref[...], ext_x + 2, ext_y + 2, half)
    fill_four(pad_ref, four_ref, channels)
    count = 4
    for first in range(0, ext_x, count):
        rows = slice(first * ext_y * half, (first + count) * ext_y * half)
        grad_s[rows, :] = convolve(four_ref, conv_ref, [(first, count, 0, ext_y)]).astype(BF16)
    grad = grad_s[...]
    pairs = grad.shape[0]
    rows = got_ref.shape[0]
    step = min(256, rows)
    for start in range(0, rows, step):
        found = []
        for q in range(PACK):
            info = got_ref[start : start + step, q * LANE : (q + 1) * LANE].astype(F32)
            place = info[:, channels : channels + 1] * 32.0 + info[:, channels + 1 : channels + 2]
            pick = one_hot(iota((step, pairs), 1) == place.astype(jnp.int32))
            both = mm(pick, grad)
            odd = info[:, channels + 2 : channels + 3] > 0.5
            found.append(jnp.where(odd, both[:, LANE:], both[:, :LANE])[:, :channels])
        back_ref[start : start + step, :] = jnp.concatenate(found, axis=1).astype(BF16)


def join_kernel(terms_ref, back_ref, out_ref, *, block, per_axis):
    total = jnp.sum(terms_ref[...].astype(F32), axis=0)
    rows, wide = back_ref.shape
    out_ref[:, :wide] = back_ref[...]
    lines = total.shape[0] // 2
    halves = []
    for h in range(2):
        parts = [total[h * lines + k : h * lines + k + block] for k in range(0, lines, block)]
        half = jnp.concatenate(parts, axis=1)
        halves.append(jnp.concatenate([half] * per_axis, axis=0).astype(BF16))
    step = block * per_axis
    for g in range(rows // step):
        out_ref[g * step : (g + 1) * step, wide:] = halves[g % 2]


def collect_kernel(back_ref, slot_ref, out_ref):
    channels, points = out_ref.shape
    rows = back_ref.shape[0]
    back = back_ref[:, : PACK * channels]
    step = min(512, points)
    for start in range(0, points, step):
        row = slot_ref[0:1, start : start + step]
        quarter = slot_ref[1:2, start : start + step]
        pick = one_hot(iota((rows, step), 0) == row)
        found = mm(back, pick, TN)
        total = jnp.zeros((channels, step), F32)
        for q in range(PACK):
            total = jnp.where(quarter == q, found[q * channels : (q + 1) * channels], total)
        out_ref[:, start : start + step] = total.astype(BF16)


def unpack_kernel(place_ref, mine_ref, theirs_ref, conv_ref, down_ref, all_s, *, block):
    channels = conv_ref.shape[1]
    devices, count = all_s.shape[0], all_s.shape[1] // 2
    skip = mine_ref.shape[1] - theirs_ref.shape[1]
    swap = place_ref[0] % 2 == 1
    for k in range(count):
        mine = mine_ref[:, skip + k * LANE : skip + (k + 1) * LANE].astype(F32)
        theirs = theirs_ref[:, k * LANE : (k + 1) * LANE].astype(F32)
        shape = (devices, block, LANE)
        all_s[:, k] = jnp.where(swap, theirs, mine).reshape(shape)
        all_s[:, count + k] = jnp.where(swap, mine, theirs).reshape(shape)
    whole = all_s[...].reshape(devices * 2 * count * block, LANE)
    base = 27 * channels
    for j in range(27):
        conv_ref[j] = whole[j * channels : (j + 1) * channels, :channels]
    rest = down_ref.shape[2] - LANE
    for j in range(8):
        start = base + j * channels
        down_ref[j, :, :LANE] = whole[start : start + channels]
        start = base + (8 + j // 2) * channels
        tail = whole[start : start + channels]
        down_ref[j, :, LANE:] = tail[:, (j % 2) * rest : (j % 2 + 1) * rest]


def shift(block, step_x, step_y):
    count_x, count_y = lax.axis_size("gx"), lax.axis_size("gy")
    pairs = []
    for x in range(count_x):
        for y in range(count_y):
            to = (x + step_x) % count_x * count_y + (y + step_y) % count_y
            pairs.append((x * count_y + y, to))
    return lax.ppermute(block, AXES, pairs)


def exchange(blocks):
    return lax.all_to_all(blocks, AXES, split_axis=0, concat_axis=0, tiled=True)


def shards(point_feats, point_owner, point_cell, occupancy, w_conv, w_down, cotangent):
    points, channels = point_feats.shape
    count_x, count_y = lax.axis_size("gx"), lax.axis_size("gy")
    devices = count_x * count_y
    cap = 32
    block = cap // PACK
    ext_x, ext_y, ext_z = occupancy.shape
    half = ext_z // 2
    pairs = ext_x * ext_y * half
    coarse = w_down.shape[2]
    coarse_x, coarse_y = ext_x // 2, ext_y // 2
    coarse_rows = coarse_x * coarse_y * half
    slot_rows = devices * block
    scale = 1.0 / math.sqrt(float(ext_x * ext_y * ext_z * devices))
    four = 4 * channels
    conv_flops = 2 * pairs * 9 * four * WIDE
    pick_flops = 2 * pairs * slot_rows * PACK * WIDE
    rim = 3
    fields = ((ext_x, ext_y, half, rim), (coarse_x, coarse_y, half, 1))

    send, slot = call(
        functools.partial(dispatch_kernel, devices=devices, cap=cap),
        (struct((slot_rows, PACK * LANE), BF16), struct((2, points), jnp.int32)),
        (point_feats.T, point_owner.reshape(1, points), point_cell.reshape(1, points)),
        "dispatch",
        flops=2 * points * slot_rows * PACK * LANE,
    )
    got = exchange(send.reshape(devices, block, PACK * LANE)).reshape(slot_rows, PACK * LANE)
    conv_blocks, back_blocks, down_blocks, given = call(
        functools.partial(prepare_kernel, ext_y=ext_y),
        (
            struct((9 * four, WIDE), BF16),
            struct((9 * four, WIDE), BF16),
            struct((4, WIDE, coarse), BF16),
            struct((coarse_rows, WIDE), BF16),
        ),
        (w_conv, w_down, cotangent.reshape(coarse_rows, coarse),
         occupancy.reshape(ext_x * ext_y, ext_z)),
        "prepare",
        flops=1000000000,
    )
    x_rows = sum(e[3] * e[1] * e[2] for e in fields)
    y_rows = sum(e[3] * e[0] * e[2] for e in fields)
    c_rows = sum(e[3] * e[3] * e[2] for e in fields)
    place = jnp.stack([lax.axis_index("gx"), lax.axis_index("gy")]).astype(jnp.int32)
    sizes = (pairs, x_rows, x_rows, y_rows, y_rows, c_rows, c_rows, c_rows, c_rows)
    grid, x_first, x_last, y_first, y_last, *corners = call(
        functools.partial(
            pool_kernel, channels=channels, fields=fields, counts=(count_x, count_y)
        ),
        tuple(struct((n, WIDE), BF16) for n in sizes),
        (place, got, given),
        "pool",
        scratch=[pltpu.VMEM((pairs, WIDE), F32)],
        flops=pick_flops,
    )
    x_low, x_high = shift(x_last, 1, 0), shift(x_first, -1, 0)
    y_low, y_high = shift(y_last, 0, 1), shift(y_first, 0, -1)
    steps = ((-1, -1), (-1, 1), (1, -1), (1, 1))
    c_hh, c_hl, c_lh, c_ll = [shift(part, *step) for part, step in zip(corners, steps)]
    long = ext_x + 2 * rim
    mid_rows = (ext_x + 4) * (ext_y - 2) * half
    silu, slope = call(
        functools.partial(column_kernel, channels=channels),
        (struct((mid_rows, WIDE), BF16), struct((mid_rows, WIDE), F32)),
        (grid, x_low, x_high, conv_blocks),
        "column",
        scratch=[
            pltpu.VMEM((long, ext_y, half, WIDE), F32),
            pltpu.VMEM((long, ext_y, half, four), F32),
        ],
        flops=2 * conv_flops,
    )
    near = (ext_x + 2, ext_y + 2, half)
    near_rows = near[0] * near[1] * half
    split = (coarse_x + 2, 2, coarse_y + 2, 2, half, WIDE)
    faces = (x_low, x_high, y_low, y_high, c_ll, c_lh, c_hl, c_hh)
    features, fine, delta_coarse, delta = call(
        functools.partial(level_kernel, channels=channels, fields=fields),
        (
            struct((coarse_rows, coarse), BF16),
            struct((pairs, WIDE), BF16),
            struct((coarse_rows, coarse), BF16),
            struct((near_rows, WIDE), BF16),
        ),
        (grid, given, *faces, silu, slope, conv_blocks, down_blocks),
        "level",
        scratch=[
            pltpu.VMEM((2 * long, 5, half, WIDE), F32),
            pltpu.VMEM((2 * long, 5, half, four), F32),
            pltpu.VMEM((coarse_x + 2, coarse_y + 2, half, WIDE), F32),
            pltpu.VMEM(split, F32),
            pltpu.VMEM(split, F32),
            pltpu.VMEM(split, F32),
        ],
        flops=conv_flops,
        megabytes=8,
    )
    used = 39 * channels
    chunk = -(-used // (32 * devices)) * 32
    packed = call(
        functools.partial(weight_grad_kernel, channels=channels, fields=fields, scale=scale),
        struct((devices * chunk, LANE), BF16),
        (grid, *faces, fine, delta_coarse, delta),
        "weight_grad",
        scratch=[
            pltpu.VMEM((*near, WIDE), F32),
            pltpu.VMEM((*near, four), F32),
            pltpu.VMEM((*near, WIDE), F32),
            pltpu.VMEM((coarse_x, 2, coarse_y, 2, half, WIDE), F32),
        ],
        flops=conv_flops,
        megabytes=8,
    )
    terms = exchange(packed.reshape(devices, chunk, LANE))
    back = call(
        functools.partial(input_grad_kernel, channels=channels),
        struct((slot_rows, PACK * channels), BF16),
        (delta, back_blocks, got),
        "input_grad",
        scratch=[
            pltpu.VMEM((*near, WIDE), F32),
            pltpu.VMEM((*near, four), F32),
            pltpu.VMEM((pairs, WIDE), BF16),
        ],
        flops=conv_flops + pick_flops,
        megabytes=8,
    )
    half_lanes = chunk // 2 // block * LANE
    joined_lanes = PACK * channels + half_lanes
    joined = call(
        functools.partial(join_kernel, block=block, per_axis=count_y),
        struct((slot_rows, joined_lanes), BF16),
        (terms, back),
        "join",
        flops=devices * chunk * LANE,
    )
    returned = exchange(joined.reshape(devices, block, joined_lanes)).reshape(
        slot_rows, joined_lanes
    )
    theirs = lax.ppermute(
        returned[:, PACK * channels :], "gx", [(i, i ^ 1) for i in range(count_x)]
    )
    grad_points = call(
        collect_kernel,
        struct((channels, points), BF16),
        (returned, slot),
        "collect",
        flops=2 * points * slot_rows * PACK * LANE,
    ).T
    grad_conv, grad_down = call(
        functools.partial(unpack_kernel, block=block),
        (struct(w_conv.shape, F32), struct(w_down.shape, F32)),
        (place, returned, theirs),
        "unpack",
        scratch=[pltpu.VMEM((devices, chunk // block, block, LANE), F32)],
    )
    return (
        features.reshape(coarse_x, coarse_y, half, coarse),
        grad_points,
        grad_conv,
        grad_down,
    )


def solution(mesh):
    placed = (
        P(("gx", "gy"), None),
        P(("gx", "gy"), None),
        P(("gx", "gy")),
        P("gx", "gy", None),
        P(),
        P(),
        P("gx", "gy", None, None),
    )
    return jax.shard_map(
        shards,
        mesh=mesh,
        in_specs=placed,
        out_specs=(P("gx", "gy", None, None), P(("gx", "gy"), None), P(), P()),
        check_vma=False,
    )
```

```python
import functools
import math

import jax
import jax.numpy as jnp
from jax import lax
from jax.experimental import pallas as pl
from jax.experimental.pallas import tpu as pltpu
from jax.sharding import PartitionSpec as P

F32 = jnp.float32
BF16 = jnp.bfloat16
LANE = 128
WIDE = 256
PACK = 4
AXES = ("gx", "gy")
NT = (((1,), (1,)), ((), ()))
NN = (((1,), (0,)), ((), ()))
TN = (((0,), (0,)), ((), ()))


def iota(shape, dim):
    return lax.broadcasted_iota(jnp.int32, shape, dim)


def mm(a, b, dims=NN):
    return lax.dot_general(a, b, dims, preferred_element_type=F32)


def one_hot(mask):
    return jnp.where(mask, 1.0, 0.0).astype(BF16)


def call(kernel, outs, args, name, scratch=(), flops=0, megabytes=4):
    return pl.pallas_call(
        kernel,
        out_shape=outs,
        in_specs=[
            pl.BlockSpec(memory_space=pltpu.SMEM if arg.ndim == 1 else pltpu.VMEM) for arg in args
        ],
        out_specs=jax.tree.map(lambda _: pl.BlockSpec(memory_space=pltpu.VMEM), outs),
        scratch_shapes=list(scratch),
        compiler_params=pltpu.CompilerParams(vmem_limit_bytes=48 * 1024 * 1024),
        cost_estimate=pl.CostEstimate(
            flops=flops, bytes_accessed=megabytes * 1000000, transcendentals=0
        ),
        name=name,
    )(*args)


def struct(shape, dtype):
    return jax.ShapeDtypeStruct(shape, dtype)


def dispatch_kernel(feats_ref, owner_ref, cell_ref, send_ref, slot_ref, *, devices, cap):
    channels, points = feats_ref.shape
    owner = owner_ref[...]
    hot = iota((devices, points), 0) == owner
    block = min(256, points)
    upper = one_hot(iota((block, block), 0) < iota((block, block), 1))
    carry = jnp.zeros((devices, 1), F32)
    ranks = []
    for start in range(0, points, block):
        part = jnp.where(hot[:, start : start + block], 1.0, 0.0)
        before = mm(part.astype(BF16), upper) + carry
        ranks.append(jnp.sum(part * before, axis=0, keepdims=True))
        carry = carry + jnp.sum(part, axis=1, keepdims=True)
    rank = jnp.concatenate(ranks, axis=1).astype(jnp.int32)
    row = owner * (cap // PACK) + (rank >> 2)
    quarter = rank & 3
    slot_ref[0:1, :] = row
    slot_ref[1:2, :] = quarter
    cell = cell_ref[...]
    line = iota((LANE - channels, points), 0)
    extra = jnp.where(line == 0, cell >> 6, 0)
    extra = jnp.where(line == 1, (cell >> 1) & 31, extra)
    extra = jnp.where(line == 2, cell & 1, extra)
    whole = jnp.concatenate([feats_ref[...], extra.astype(F32).astype(BF16)], axis=0)
    spread = jnp.concatenate([whole * one_hot(quarter == q) for q in range(PACK)], axis=0)
    rows = send_ref.shape[0]
    step = min(256, rows)
    for start in range(0, rows, step):
        pick = one_hot(iota((step, points), 0) + start == row)
        send_ref[start : start + step, :] = mm(pick, spread, NT).astype(BF16)


def pool_kernel(
    place_ref, got_ref, coarse_ref, grid_ref, first_ref, last_ref, total_ref,
    *, channels, fields, count,
):
    rows = got_ref.shape[0]
    pairs = grid_ref.shape[0]
    lane = iota((8, LANE), 1)
    weigh = jnp.where(lane == channels, 32.0, jnp.where(lane == channels + 1, 1.0, 0.0))
    weigh = weigh.astype(BF16)
    step = 256
    for q in range(PACK):
        block = got_ref[:, q * LANE : (q + 1) * LANE]
        place = mm(weigh, block, NT)[0:1].astype(jnp.int32)
        odd = block * block[:, channels + 2 : channels + 3]
        both = jnp.concatenate([block - odd, odd], axis=1)
        for start in range(0, pairs, step):
            pick = one_hot(iota((step, rows), 0) + start == place)
            part = mm(pick, both)
            if q:
                part = total_ref[start : start + step, :] + part
            total_ref[start : start + step, :] = part
    at = 0
    for ref, (ext_x, ext_y, half, rim) in zip((total_ref, coarse_ref), fields):
        field = as_field(ref[...], ext_x, ext_y, half)
        put_rows(first_ref, at, field[:rim] * inside(place_ref[0], 0))
        put_rows(last_ref, at, field[ext_x - rim :] * inside(place_ref[0], count - 1))
        at += rim * ext_y * half
    grid_ref[...] = total_ref[...].astype(BF16)


def as_field(rows, ext_x, ext_y, half):
    return rows.astype(F32).reshape(ext_x, ext_y, half, rows.shape[1])


def put_rows(ref, at, field):
    size = field.shape[0] * field.shape[1] * field.shape[2]
    ref[at : at + size, :] = field.reshape(size, field.shape[3]).astype(BF16)


def inside(place, end):
    return jnp.where(place == end, 0.0, 1.0)


def edge_kernel(
    place_ref, grid_ref, coarse_ref, low_ref, high_ref, first_ref, last_ref, *, fields, count
):
    start, at = 0, 0
    for ref, (ext_x, ext_y, half, rim) in zip((grid_ref, coarse_ref), fields):
        size = rim * ext_y * half
        parts = (
            as_field(low_ref[start : start + size, :], rim, ext_y, half),
            as_field(ref[...], ext_x, ext_y, half),
            as_field(high_ref[start : start + size, :], rim, ext_y, half),
        )
        for part in parts:
            put_rows(first_ref, at, part[:, :rim] * inside(place_ref[1], 0))
            put_rows(last_ref, at, part[:, ext_y - rim :] * inside(place_ref[1], count - 1))
            at += part.shape[0] * rim * half
        start += size


def prepare_kernel(
    conv_ref, down_ref, cot_ref, occ_ref, conv_out, back_out, down_out, coarse_out, *, ext_y
):
    channels = conv_ref.shape[1]
    conv_out[...] = jnp.zeros(conv_out.shape, BF16)
    back_out[...] = jnp.zeros(back_out.shape, BF16)
    down_out[...] = jnp.zeros(down_out.shape, BF16)
    four = 4 * channels
    a, b = slice(0, channels), slice(LANE, LANE + channels)
    for j in range(9):
        for k in range(3):
            weight = conv_ref[3 * j + k]
            turned = weight.astype(F32).T.astype(BF16)
            for z in range(2):
                at, side = j * four + (k + z) * channels, (a, b)[z]
                conv_out[at : at + channels, side] = weight
                at = (8 - j) * four + (2 - k + z) * channels
                back_out[at : at + channels, side] = turned
    for j in range(4):
        down_out[j, a, :] = down_ref[2 * j]
        down_out[j, b, :] = down_ref[2 * j + 1]
    columns, depth = occ_ref.shape
    rows, coarse = cot_ref.shape
    half = depth // 2
    rest = WIDE - coarse
    occ = occ_ref[...].astype(F32).astype(BF16)
    row = iota((rows, columns), 0)
    place, column = row // half, iota((rows, columns), 1)
    base = place // (ext_y // 2) * 2 * ext_y + place % (ext_y // 2) * 2
    level = iota((rows, depth), 1) // 2 == iota((rows, depth), 0) % half
    total = jnp.zeros((rows, rest), F32)
    for j in range(4):
        pick = one_hot(base + j // 2 * ext_y + j % 2 == column)
        found = jnp.where(level, mm(pick, occ), 0.0).astype(BF16)
        spot = iota((depth, rest), 1) == 2 * j + iota((depth, rest), 0) % 2
        total = total + mm(found, one_hot(spot))
    coarse_out[:, :coarse] = cot_ref[...]
    coarse_out[:, coarse:] = total.astype(BF16)


def fill_four(pad_ref, four_ref, channels):
    ext_x, ext_y, half, wide = pad_ref.shape
    columns = ext_x * ext_y
    level = iota((columns, half, LANE), 1)
    even = pad_ref[:, :, :, :LANE].reshape(columns, half, LANE)
    odd = pad_ref[:, :, :, LANE:].reshape(columns, half, LANE)
    after = jnp.where(level == half - 1, 0.0, pltpu.roll(even, half - 1, 1))
    before = jnp.where(level == 0, 0.0, pltpu.roll(odd, 1, 1))
    parts = [part[:, :, :channels] for part in (before, even, odd, after)]
    four = jnp.concatenate(parts, axis=2)
    four_ref[...] = four.reshape(ext_x, ext_y, half, 4 * channels)


def windows(ref, first_x, count_x, first_y, count_y):
    parts = []
    for j in range(9):
        x, y = first_x + j // 3, first_y + j % 3
        part = ref[x : x + count_x, y : y + count_y]
        parts.append(part.reshape(count_x * count_y * part.shape[2], part.shape[3]).astype(BF16))
    return parts


def convolve(four_ref, weight_ref, boxes):
    rows = [jnp.concatenate(windows(four_ref, *box), axis=1) for box in boxes]
    return mm(rows[0] if len(rows) == 1 else jnp.concatenate(rows, axis=0), weight_ref[...])


def logistic(values):
    return 1.0 / (1.0 + jnp.exp(-values))


def silu_and_slope(pre):
    sigma = logistic(pre)
    return (pre * sigma).astype(BF16), sigma * (1.0 + pre * (1.0 - sigma))


def inner(field, rim):
    part = field[rim : field.shape[0] - rim, rim : field.shape[1] - rim]
    return part.reshape(part.shape[0] * part.shape[1] * part.shape[2], part.shape[3])


def column_kernel(
    grid_ref, x_low, x_high, conv_ref, silu_ref, slope_ref, pad_ref, four_ref, *, channels
):
    ext_x, ext_y, half = pad_ref.shape[0], pad_ref.shape[1], pad_ref.shape[2]
    rim = 3
    size = rim * ext_y * half
    pad_ref[:rim] = as_field(x_low[:size, :], rim, ext_y, half)
    pad_ref[rim : ext_x - rim] = as_field(grid_ref[...], ext_x - 2 * rim, ext_y, half)
    pad_ref[ext_x - rim :] = as_field(x_high[:size, :], rim, ext_y, half)
    fill_four(pad_ref, four_ref, channels)
    count = 4
    step = count * (ext_y - 2) * half
    for first in range(0, ext_x - 2, count):
        pre = convolve(four_ref, conv_ref, [(first, count, 0, ext_y - 2)])
        rows = slice(first // count * step, (first // count + 1) * step)
        silu_ref[rows, :], slope_ref[rows, :] = silu_and_slope(pre)


def level_kernel(
    grid_ref, coarse_ref, x_low, x_high, y_low, y_high, silu_ref, slope_ref,
    conv_ref, down_ref,
    features_ref, fine_ref, delta_coarse_ref, delta_ref,
    pad_ref, four_ref, coarse_s, mask_s, fine_s, slope_s, *, channels, fields,
):
    (ext_x, ext_y, half, rim), (coarse_x, coarse_y, _, _) = fields
    wide = WIDE
    long = ext_x + 2 * rim
    slab, face = rim * ext_y * half, long * rim * half
    parts = (
        as_field(x_low[:slab, :], rim, ext_y, half),
        as_field(grid_ref[...], ext_x, ext_y, half),
        as_field(x_high[:slab, :], rim, ext_y, half),
    )
    for side, y_ref in enumerate((y_low, y_high)):
        ours, here, there = ((0, rim, 0), (ext_y - 2, 0, 2))[side]
        at = side * long
        pad_ref[at : at + long, there : there + rim] = as_field(y_ref[:face, :], long, rim, half)
        for part in parts:
            count = part.shape[0]
            pad_ref[at : at + count, here : here + 2] = part[:, ours : ours + 2]
            at += count
    fill_four(pad_ref, four_ref, channels)
    coarse_s[1 : 1 + coarse_x, 1 : 1 + coarse_y] = as_field(
        coarse_ref[...], coarse_x, coarse_y, half
    )
    coarse_s[:1, 1 : 1 + coarse_y] = as_field(x_low[slab:, :], 1, coarse_y, half)
    coarse_s[1 + coarse_x :, 1 : 1 + coarse_y] = as_field(x_high[slab:, :], 1, coarse_y, half)
    for y, y_ref in ((0, y_low), (1 + coarse_y, y_high)):
        coarse_s[:, y : y + 1] = as_field(y_ref[face:, :], coarse_x + 2, 1, half)
    wide_x, wide_y = coarse_x + 2, coarse_y + 2
    coarse_rows = wide_x * wide_y * half
    coarse = down_ref.shape[2]
    given = coarse_s[...].reshape(coarse_rows, wide).astype(BF16)
    largest = None
    for j in range(4):
        spot = iota((wide, wide), 0) == coarse + 2 * j + iota((wide, wide), 1) // LANE
        mask = mm(given, one_hot(spot))
        mask_s[:, j // 2, :, j % 2] = mask.reshape(wide_x, wide_y, half, wide)
        largest = mask if largest is None else jnp.maximum(largest, mask)
    largest = jnp.maximum(largest[:, :LANE], largest[:, LANE:])
    coarse_mask = jnp.concatenate([largest, largest[:, : coarse - LANE]], axis=1)

    out_x, out_y = 2 * wide_x, 2 * wide_y
    strip = 3
    boxes = [(0, out_x, 0, strip), (long, out_x, 0, strip)]
    silu, slope = silu_and_slope(convolve(four_ref, conv_ref, boxes))
    shape = (2, out_x, strip, half, wide)
    edge_silu, edge_slope = silu.astype(F32).reshape(shape), slope.reshape(shape)
    columns = out_y - 2 * strip
    mid_silu = as_field(silu_ref[...], out_x, columns, half)
    mid_slope = slope_ref[...].reshape(out_x, columns, half, wide)
    shape = (wide_x, 2, half, wide)
    for y in range(out_y):
        if y < strip:
            silu, slope = edge_silu[0, :, y], edge_slope[0, :, y]
        elif y >= out_y - strip:
            at = y - (out_y - strip)
            silu, slope = edge_silu[1, :, at], edge_slope[1, :, at]
        else:
            silu, slope = mid_silu[:, y - strip], mid_slope[:, y - strip]
        mask = mask_s[:, :, y // 2, y % 2]
        fine_s[:, :, y // 2, y % 2] = silu.reshape(shape) * mask
        slope_s[:, :, y // 2, y % 2] = slope.reshape(shape) * mask
    field = (out_x, out_y, half, wide)
    fine_ref[...] = inner(fine_s[...].reshape(field), 2).astype(BF16)

    pre = None
    for j in range(4):
        piece = fine_s[:, j // 2, :, j % 2].reshape(coarse_rows, wide).astype(BF16)
        part = mm(piece, down_ref[j])
        pre = part if pre is None else pre + part
    sigma = logistic(pre)
    coarse_field = (wide_x, wide_y, half, coarse)
    features = pre * sigma * coarse_mask
    features_ref[...] = inner(features.reshape(coarse_field), 1).astype(BF16)
    slope = sigma * (1.0 + pre * (1.0 - sigma))
    cot = coarse_s[:, :, :, :coarse].reshape(coarse_rows, coarse)
    delta = cot * coarse_mask * slope
    delta_coarse_ref[...] = inner(delta.reshape(coarse_field), 1).astype(BF16)
    delta = delta.astype(BF16)
    for j in range(4):
        back = mm(delta, down_ref[j], NT).reshape(wide_x, wide_y, half, wide)
        fine_s[:, j // 2, :, j % 2] = back * slope_s[:, j // 2, :, j % 2]
    delta_ref[...] = inner(fine_s[...].reshape(field), 1).astype(BF16)


def weight_grad_kernel(
    grid_ref, x_low, x_high, y_low, y_high, fine_ref, delta_coarse_ref, delta_ref,
    out_ref, pad_ref, four_ref, delta_s, fine_s, *, channels, fields, scale,
):
    (ext_x, ext_y, half, rim), _ = fields
    long = ext_x + 2 * rim
    slab, face = rim * ext_y * half, long * rim * half
    pad_ref[1 : 1 + ext_x, 1 : 1 + ext_y] = as_field(grid_ref[...], ext_x, ext_y, half)
    for x, x_ref, at in ((0, x_low, rim - 1), (1 + ext_x, x_high, 0)):
        field = as_field(x_ref[:slab, :], rim, ext_y, half)
        pad_ref[x : x + 1, 1 : 1 + ext_y] = field[at : at + 1]
    for y, y_ref, at in ((0, y_low, rim - 1), (1 + ext_y, y_high, 0)):
        field = as_field(y_ref[:face, :], long, rim, half)
        pad_ref[:, y : y + 1] = field[rim - 1 : long - rim + 1, at : at + 1]
    fill_four(pad_ref, four_ref, channels)
    delta_s[...] = as_field(delta_ref[...], ext_x + 2, ext_y + 2, half)
    turned = inner(delta_s[...], 1).T.astype(BF16)
    three = 3 * channels
    for j, part in enumerate(windows(four_ref, 0, ext_x, 0, ext_y)):
        grad = mm(turned, part)
        grad = grad[:LANE, :three] + grad[LANE:, channels:]
        out_ref[j * three : (j + 1) * three, :] = (grad.T * scale).astype(BF16)
    fine_s[...] = fine_ref[...].astype(F32).reshape(fine_s.shape)
    coarse_rows = ext_x // 2 * (ext_y // 2) * half
    base = 27 * channels
    for j in range(4):
        piece = fine_s[:, j // 2, :, j % 2].reshape(coarse_rows, WIDE).astype(BF16)
        grad = mm(piece, delta_coarse_ref[...], TN) * scale
        first, second = grad[:channels], grad[LANE : LANE + channels]
        start = base + 2 * j * channels
        out_ref[start : start + channels, :] = first[:, :LANE].astype(BF16)
        out_ref[start + channels : start + 2 * channels, :] = second[:, :LANE].astype(BF16)
        start = base + (8 + j) * channels
        tail = jnp.concatenate([first[:, LANE:], second[:, LANE:]], axis=1)
        out_ref[start : start + channels, :] = tail.astype(BF16)
    end = base + 12 * channels
    out_ref[end:, :] = jnp.zeros((out_ref.shape[0] - end, LANE), BF16)


def input_grad_kernel(delta_ref, conv_ref, got_ref, back_ref, pad_ref, four_ref, grad_s, *, channels):
    ext_x, ext_y, half = pad_ref.shape[0] - 2, pad_ref.shape[1] - 2, pad_ref.shape[2]
    pad_ref[...] = as_field(delta_ref[...], ext_x + 2, ext_y + 2, half)
    fill_four(pad_ref, four_ref, channels)
    count = 4
    for first in range(0, ext_x, count):
        rows = slice(first * ext_y * half, (first + count) * ext_y * half)
        grad_s[rows, :] = convolve(four_ref, conv_ref, [(first, count, 0, ext_y)]).astype(BF16)
    grad = grad_s[...]
    pairs = grad.shape[0]
    rows = got_ref.shape[0]
    step = min(256, rows)
    for start in range(0, rows, step):
        found = []
        for q in range(PACK):
            info = got_ref[start : start + step, q * LANE : (q + 1) * LANE].astype(F32)
            place = info[:, channels : channels + 1] * 32.0 + info[:, channels + 1 : channels + 2]
            pick = one_hot(iota((step, pairs), 1) == place.astype(jnp.int32))
            both = mm(pick, grad)
            odd = info[:, channels + 2 : channels + 3] > 0.5
            found.append(jnp.where(odd, both[:, LANE:], both[:, :LANE])[:, :channels])
        back_ref[start : start + step, :] = jnp.concatenate(found, axis=1).astype(BF16)


def join_kernel(terms_ref, back_ref, out_ref, *, block, per_axis):
    total = jnp.sum(terms_ref[...].astype(F32), axis=0)
    rows, wide = back_ref.shape
    out_ref[:, :wide] = back_ref[...]
    lines = total.shape[0] // 2
    halves = []
    for h in range(2):
        parts = [total[h * lines + k : h * lines + k + block] for k in range(0, lines, block)]
        half = jnp.concatenate(parts, axis=1)
        halves.append(jnp.concatenate([half] * per_axis, axis=0).astype(BF16))
    step = block * per_axis
    for g in range(rows // step):
        out_ref[g * step : (g + 1) * step, wide:] = halves[g % 2]


def collect_kernel(back_ref, slot_ref, out_ref):
    channels, points = out_ref.shape
    rows = back_ref.shape[0]
    back = back_ref[:, : PACK * channels]
    step = min(512, points)
    for start in range(0, points, step):
        row = slot_ref[0:1, start : start + step]
        quarter = slot_ref[1:2, start : start + step]
        pick = one_hot(iota((rows, step), 0) == row)
        found = mm(back, pick, TN)
        total = jnp.zeros((channels, step), F32)
        for q in range(PACK):
            total = jnp.where(quarter == q, found[q * channels : (q + 1) * channels], total)
        out_ref[:, start : start + step] = total.astype(BF16)


def unpack_kernel(place_ref, mine_ref, theirs_ref, conv_ref, down_ref, all_s, *, block):
    channels = conv_ref.shape[1]
    devices, count = all_s.shape[0], all_s.shape[1] // 2
    skip = mine_ref.shape[1] - theirs_ref.shape[1]
    swap = place_ref[0] % 2 == 1
    for k in range(count):
        mine = mine_ref[:, skip + k * LANE : skip + (k + 1) * LANE].astype(F32)
        theirs = theirs_ref[:, k * LANE : (k + 1) * LANE].astype(F32)
        shape = (devices, block, LANE)
        all_s[:, k] = jnp.where(swap, theirs, mine).reshape(shape)
        all_s[:, count + k] = jnp.where(swap, mine, theirs).reshape(shape)
    whole = all_s[...].reshape(devices * 2 * count * block, LANE)
    base = 27 * channels
    for j in range(27):
        conv_ref[j] = whole[j * channels : (j + 1) * channels, :channels]
    rest = down_ref.shape[2] - LANE
    for j in range(8):
        start = base + j * channels
        down_ref[j, :, :LANE] = whole[start : start + channels]
        start = base + (8 + j // 2) * channels
        tail = whole[start : start + channels]
        down_ref[j, :, LANE:] = tail[:, (j % 2) * rest : (j % 2 + 1) * rest]


def shift(block, axis, step):
    count = lax.axis_size(axis)
    return lax.ppermute(block, axis, [(i, (i + step) % count) for i in range(count)])


def exchange(blocks):
    return lax.all_to_all(blocks, AXES, split_axis=0, concat_axis=0, tiled=True)


def shards(point_feats, point_owner, point_cell, occupancy, w_conv, w_down, cotangent):
    points, channels = point_feats.shape
    count_x, count_y = lax.axis_size("gx"), lax.axis_size("gy")
    devices = count_x * count_y
    cap = 32
    block = cap // PACK
    ext_x, ext_y, ext_z = occupancy.shape
    half = ext_z // 2
    pairs = ext_x * ext_y * half
    coarse = w_down.shape[2]
    coarse_x, coarse_y = ext_x // 2, ext_y // 2
    coarse_rows = coarse_x * coarse_y * half
    slot_rows = devices * block
    scale = 1.0 / math.sqrt(float(ext_x * ext_y * ext_z * devices))
    four = 4 * channels
    conv_flops = 2 * pairs * 9 * four * WIDE
    pick_flops = 2 * pairs * slot_rows * PACK * WIDE
    rim = 3
    fields = ((ext_x, ext_y, half, rim), (coarse_x, coarse_y, half, 1))

    send, slot = call(
        functools.partial(dispatch_kernel, devices=devices, cap=cap),
        (struct((slot_rows, PACK * LANE), BF16), struct((2, points), jnp.int32)),
        (point_feats.T, point_owner.reshape(1, points), point_cell.reshape(1, points)),
        "dispatch",
        flops=2 * points * slot_rows * PACK * LANE,
    )
    got = exchange(send.reshape(devices, block, PACK * LANE)).reshape(slot_rows, PACK * LANE)
    conv_blocks, back_blocks, down_blocks, given = call(
        functools.partial(prepare_kernel, ext_y=ext_y),
        (
            struct((9 * four, WIDE), BF16),
            struct((9 * four, WIDE), BF16),
            struct((4, WIDE, coarse), BF16),
            struct((coarse_rows, WIDE), BF16),
        ),
        (w_conv, w_down, cotangent.reshape(coarse_rows, coarse),
         occupancy.reshape(ext_x * ext_y, ext_z)),
        "prepare",
        flops=1000000000,
    )
    x_rows = sum(e[3] * e[1] * e[2] for e in fields)
    y_rows = sum(e[3] * (e[0] + 2 * e[3]) * e[2] for e in fields)
    place = jnp.stack([lax.axis_index("gx"), lax.axis_index("gy")]).astype(jnp.int32)
    grid, x_first, x_last = call(
        functools.partial(pool_kernel, channels=channels, fields=fields, count=count_x),
        tuple(struct((n, WIDE), BF16) for n in (pairs, x_rows, x_rows)),
        (place, got, given),
        "pool",
        scratch=[pltpu.VMEM((pairs, WIDE), F32)],
        flops=pick_flops,
    )
    x_low, x_high = shift(x_last, "gx", 1), shift(x_first, "gx", -1)
    y_first, y_last = call(
        functools.partial(edge_kernel, fields=fields, count=count_y),
        tuple(struct((n, WIDE), BF16) for n in (y_rows, y_rows)),
        (place, grid, given, x_low, x_high),
        "edge",
    )
    y_low, y_high = shift(y_last, "gy", 1), shift(y_first, "gy", -1)
    long = ext_x + 2 * rim
    mid_rows = (ext_x + 4) * (ext_y - 2) * half
    silu, slope = call(
        functools.partial(column_kernel, channels=channels),
        (struct((mid_rows, WIDE), BF16), struct((mid_rows, WIDE), F32)),
        (grid, x_low, x_high, conv_blocks),
        "column",
        scratch=[
            pltpu.VMEM((long, ext_y, half, WIDE), F32),
            pltpu.VMEM((long, ext_y, half, four), F32),
        ],
        flops=2 * conv_flops,
    )
    near = (ext_x + 2, ext_y + 2, half)
    near_rows = near[0] * near[1] * half
    split = (coarse_x + 2, 2, coarse_y + 2, 2, half, WIDE)
    faces = (x_low, x_high, y_low, y_high)
    features, fine, delta_coarse, delta = call(
        functools.partial(level_kernel, channels=channels, fields=fields),
        (
            struct((coarse_rows, coarse), BF16),
            struct((pairs, WIDE), BF16),
            struct((coarse_rows, coarse), BF16),
            struct((near_rows, WIDE), BF16),
        ),
        (grid, given, *faces, silu, slope, conv_blocks, down_blocks),
        "level",
        scratch=[
            pltpu.VMEM((2 * long, 5, half, WIDE), F32),
            pltpu.VMEM((2 * long, 5, half, four), F32),
            pltpu.VMEM((coarse_x + 2, coarse_y + 2, half, WIDE), F32),
            pltpu.VMEM(split, F32),
            pltpu.VMEM(split, F32),
            pltpu.VMEM(split, F32),
        ],
        flops=conv_flops,
        megabytes=8,
    )
    used = 39 * channels
    chunk = -(-used // (32 * devices)) * 32
    packed = call(
        functools.partial(weight_grad_kernel, channels=channels, fields=fields, scale=scale),
        struct((devices * chunk, LANE), BF16),
        (grid, *faces, fine, delta_coarse, delta),
        "weight_grad",
        scratch=[
            pltpu.VMEM((*near, WIDE), F32),
            pltpu.VMEM((*near, four), F32),
            pltpu.VMEM((*near, WIDE), F32),
            pltpu.VMEM((coarse_x, 2, coarse_y, 2, half, WIDE), F32),
        ],
        flops=conv_flops,
        megabytes=8,
    )
    terms = exchange(packed.reshape(devices, chunk, LANE))
    back = call(
        functools.partial(input_grad_kernel, channels=channels),
        struct((slot_rows, PACK * channels), BF16),
        (delta, back_blocks, got),
        "input_grad",
        scratch=[
            pltpu.VMEM((*near, WIDE), F32),
            pltpu.VMEM((*near, four), F32),
            pltpu.VMEM((pairs, WIDE), BF16),
        ],
        flops=conv_flops + pick_flops,
        megabytes=8,
    )
    half_lanes = chunk // 2 // block * LANE
    joined_lanes = PACK * channels + half_lanes
    joined = call(
        functools.partial(join_kernel, block=block, per_axis=count_y),
        struct((slot_rows, joined_lanes), BF16),
        (terms, back),
        "join",
        flops=devices * chunk * LANE,
    )
    returned = exchange(joined.reshape(devices, block, joined_lanes)).reshape(
        slot_rows, joined_lanes
    )
    theirs = lax.ppermute(
        returned[:, PACK * channels :], "gx", [(i, i ^ 1) for i in range(count_x)]
    )
    grad_points = call(
        collect_kernel,
        struct((channels, points), BF16),
        (returned, slot),
        "collect",
        flops=2 * points * slot_rows * PACK * LANE,
    ).T
    grad_conv, grad_down = call(
        functools.partial(unpack_kernel, block=block),
        (struct(w_conv.shape, F32), struct(w_down.shape, F32)),
        (place, returned, theirs),
        "unpack",
        scratch=[pltpu.VMEM((devices, chunk // block, block, LANE), F32)],
    )
    return (
        features.reshape(coarse_x, coarse_y, half, coarse),
        grad_points,
        grad_conv,
        grad_down,
    )


def solution(mesh):
    placed = (
        P(("gx", "gy"), None),
        P(("gx", "gy"), None),
        P(("gx", "gy")),
        P("gx", "gy", None),
        P(),
        P(),
        P("gx", "gy", None, None),
    )
    return jax.shard_map(
        shards,
        mesh=mesh,
        in_specs=placed,
        out_specs=(P("gx", "gy", None, None), P(("gx", "gy"), None), P(), P()),
        check_vma=False,
    )
```

```python
import functools
import math

import jax
import jax.numpy as jnp
from jax import lax
from jax.experimental import pallas as pl
from jax.experimental.pallas import tpu as pltpu
from jax.sharding import PartitionSpec as P

F32 = jnp.float32
BF16 = jnp.bfloat16
LANE = 128
WIDE = 256
PACK = 4
AXES = ("gx", "gy")
NT = (((1,), (1,)), ((), ()))
NN = (((1,), (0,)), ((), ()))
TN = (((0,), (0,)), ((), ()))


def iota(shape, dim):
    return lax.broadcasted_iota(jnp.int32, shape, dim)


def mm(a, b, dims=NN):
    return lax.dot_general(a, b, dims, preferred_element_type=F32)


def one_hot(mask):
    return jnp.where(mask, 1.0, 0.0).astype(BF16)


def call(kernel, outs, args, name, scratch=(), flops=0, megabytes=4):
    return pl.pallas_call(
        kernel,
        out_shape=outs,
        in_specs=[
            pl.BlockSpec(memory_space=pltpu.SMEM if arg.ndim == 1 else pltpu.VMEM) for arg in args
        ],
        out_specs=jax.tree.map(lambda _: pl.BlockSpec(memory_space=pltpu.VMEM), outs),
        scratch_shapes=list(scratch),
        compiler_params=pltpu.CompilerParams(vmem_limit_bytes=24 * 1024 * 1024),
        cost_estimate=pl.CostEstimate(
            flops=flops, bytes_accessed=megabytes * 1000000, transcendentals=0
        ),
        name=name,
    )(*args)


def struct(shape, dtype):
    return jax.ShapeDtypeStruct(shape, dtype)


def dispatch_kernel(feats_ref, owner_ref, cell_ref, send_ref, slot_ref, *, devices, cap):
    channels, points = feats_ref.shape
    owner = owner_ref[...]
    hot = iota((devices, points), 0) == owner
    block = min(256, points)
    upper = one_hot(iota((block, block), 0) < iota((block, block), 1))
    carry = jnp.zeros((devices, 1), F32)
    ranks = []
    for start in range(0, points, block):
        part = jnp.where(hot[:, start : start + block], 1.0, 0.0)
        before = mm(part.astype(BF16), upper) + carry
        ranks.append(jnp.sum(part * before, axis=0, keepdims=True))
        carry = carry + jnp.sum(part, axis=1, keepdims=True)
    rank = jnp.concatenate(ranks, axis=1).astype(jnp.int32)
    row = owner * (cap // PACK) + (rank >> 2)
    quarter = rank & 3
    slot_ref[0:1, :] = row
    slot_ref[1:2, :] = quarter
    cell = cell_ref[...]
    line = iota((LANE - channels, points), 0)
    extra = jnp.where(line == 0, cell >> 6, 0)
    extra = jnp.where(line == 1, (cell >> 1) & 31, extra)
    extra = jnp.where(line == 2, cell & 1, extra)
    whole = jnp.concatenate([feats_ref[...], extra.astype(F32).astype(BF16)], axis=0)
    spread = jnp.concatenate([whole * one_hot(quarter == q) for q in range(PACK)], axis=0)
    rows = send_ref.shape[0]
    step = min(256, rows)
    for start in range(0, rows, step):
        pick = one_hot(iota((step, points), 0) + start == row)
        send_ref[start : start + step, :] = mm(pick, spread, NT).astype(BF16)


def pool_kernel(
    place_ref, got_ref, coarse_ref, grid_ref, first_ref, last_ref, total_ref,
    *, channels, fields, count,
):
    rows = got_ref.shape[0]
    pairs = grid_ref.shape[0]
    lane = iota((8, LANE), 1)
    weigh = jnp.where(lane == channels, 32.0, jnp.where(lane == channels + 1, 1.0, 0.0))
    weigh = weigh.astype(BF16)
    step = 256
    for q in range(PACK):
        block = got_ref[:, q * LANE : (q + 1) * LANE]
        place = mm(weigh, block, NT)[0:1].astype(jnp.int32)
        odd = block * block[:, channels + 2 : channels + 3]
        both = jnp.concatenate([block - odd, odd], axis=1)
        for start in range(0, pairs, step):
            pick = one_hot(iota((step, rows), 0) + start == place)
            part = mm(pick, both)
            if q:
                part = total_ref[start : start + step, :] + part
            total_ref[start : start + step, :] = part
    at = 0
    for ref, (ext_x, ext_y, half, rim) in zip((total_ref, coarse_ref), fields):
        field = as_field(ref[...], ext_x, ext_y, half)
        put_rows(first_ref, at, field[:rim] * inside(place_ref[0], 0))
        put_rows(last_ref, at, field[ext_x - rim :] * inside(place_ref[0], count - 1))
        at += rim * ext_y * half
    grid_ref[...] = total_ref[...].astype(BF16)


def as_field(rows, ext_x, ext_y, half):
    return rows.astype(F32).reshape(ext_x, ext_y, half, rows.shape[1])


def put_rows(ref, at, field):
    size = field.shape[0] * field.shape[1] * field.shape[2]
    ref[at : at + size, :] = field.reshape(size, field.shape[3]).astype(BF16)


def inside(place, end):
    return jnp.where(place == end, 0.0, 1.0)


def edge_kernel(
    place_ref, grid_ref, coarse_ref, low_ref, high_ref, first_ref, last_ref, *, fields, count
):
    start, at = 0, 0
    for ref, (ext_x, ext_y, half, rim) in zip((grid_ref, coarse_ref), fields):
        size = rim * ext_y * half
        parts = (
            as_field(low_ref[start : start + size, :], rim, ext_y, half),
            as_field(ref[...], ext_x, ext_y, half),
            as_field(high_ref[start : start + size, :], rim, ext_y, half),
        )
        for part in parts:
            put_rows(first_ref, at, part[:, :rim] * inside(place_ref[1], 0))
            put_rows(last_ref, at, part[:, ext_y - rim :] * inside(place_ref[1], count - 1))
            at += part.shape[0] * rim * half
        start += size


def prepare_kernel(
    conv_ref, down_ref, cot_ref, occ_ref, conv_out, back_out, down_out, coarse_out, *, ext_y
):
    channels = conv_ref.shape[1]
    conv_out[...] = jnp.zeros(conv_out.shape, BF16)
    back_out[...] = jnp.zeros(back_out.shape, BF16)
    down_out[...] = jnp.zeros(down_out.shape, BF16)
    four = 4 * channels
    a, b = slice(0, channels), slice(LANE, LANE + channels)
    for j in range(9):
        for k in range(3):
            weight = conv_ref[3 * j + k]
            turned = weight.astype(F32).T.astype(BF16)
            for z in range(2):
                at, side = j * four + (k + z) * channels, (a, b)[z]
                conv_out[at : at + channels, side] = weight
                at = (8 - j) * four + (2 - k + z) * channels
                back_out[at : at + channels, side] = turned
    for j in range(4):
        down_out[j, a, :] = down_ref[2 * j]
        down_out[j, b, :] = down_ref[2 * j + 1]
    columns, depth = occ_ref.shape
    rows, coarse = cot_ref.shape
    half = depth // 2
    rest = WIDE - coarse
    occ = occ_ref[...].astype(F32).astype(BF16)
    row = iota((rows, columns), 0)
    place, column = row // half, iota((rows, columns), 1)
    base = place // (ext_y // 2) * 2 * ext_y + place % (ext_y // 2) * 2
    level = iota((rows, depth), 1) // 2 == iota((rows, depth), 0) % half
    total = jnp.zeros((rows, rest), F32)
    for j in range(4):
        pick = one_hot(base + j // 2 * ext_y + j % 2 == column)
        found = jnp.where(level, mm(pick, occ), 0.0).astype(BF16)
        spot = iota((depth, rest), 1) == 2 * j + iota((depth, rest), 0) % 2
        total = total + mm(found, one_hot(spot))
    coarse_out[:, :coarse] = cot_ref[...]
    coarse_out[:, coarse:] = total.astype(BF16)


def fill_four(pad_ref, four_ref, channels):
    ext_x, ext_y, half, wide = pad_ref.shape
    columns = ext_x * ext_y
    level = iota((columns, half, LANE), 1)
    even = pad_ref[:, :, :, :LANE].reshape(columns, half, LANE)
    odd = pad_ref[:, :, :, LANE:].reshape(columns, half, LANE)
    after = jnp.where(level == half - 1, 0.0, pltpu.roll(even, half - 1, 1))
    before = jnp.where(level == 0, 0.0, pltpu.roll(odd, 1, 1))
    parts = [part[:, :, :channels] for part in (before, even, odd, after)]
    four = jnp.concatenate(parts, axis=2)
    four_ref[...] = four.reshape(ext_x, ext_y, half, 4 * channels)


def windows(ref, first_x, count_x, first_y, count_y):
    parts = []
    for j in range(9):
        x, y = first_x + j // 3, first_y + j % 3
        part = ref[x : x + count_x, y : y + count_y]
        parts.append(part.reshape(count_x * count_y * part.shape[2], part.shape[3]).astype(BF16))
    return parts


def convolve(four_ref, weight_ref, boxes):
    rows = [jnp.concatenate(windows(four_ref, *box), axis=1) for box in boxes]
    return mm(rows[0] if len(rows) == 1 else jnp.concatenate(rows, axis=0), weight_ref[...])


def logistic(values):
    return 1.0 / (1.0 + jnp.exp(-values))


def silu_and_slope(pre):
    sigma = logistic(pre)
    return (pre * sigma).astype(BF16), sigma * (1.0 + pre * (1.0 - sigma))


def inner(field, rim):
    part = field[rim : field.shape[0] - rim, rim : field.shape[1] - rim]
    return part.reshape(part.shape[0] * part.shape[1] * part.shape[2], part.shape[3])


def column_kernel(
    grid_ref, x_low, x_high, conv_ref, silu_ref, slope_ref, pad_ref, four_ref, *, channels
):
    ext_x, ext_y, half = pad_ref.shape[0], pad_ref.shape[1], pad_ref.shape[2]
    rim = 3
    size = rim * ext_y * half
    pad_ref[:rim] = as_field(x_low[:size, :], rim, ext_y, half)
    pad_ref[rim : ext_x - rim] = as_field(grid_ref[...], ext_x - 2 * rim, ext_y, half)
    pad_ref[ext_x - rim :] = as_field(x_high[:size, :], rim, ext_y, half)
    fill_four(pad_ref, four_ref, channels)
    count = 4
    step = count * (ext_y - 2) * half
    for first in range(0, ext_x - 2, count):
        pre = convolve(four_ref, conv_ref, [(first, count, 0, ext_y - 2)])
        rows = slice(first // count * step, (first // count + 1) * step)
        silu_ref[rows, :], slope_ref[rows, :] = silu_and_slope(pre)


def level_kernel(
    grid_ref, coarse_ref, x_low, x_high, y_low, y_high, silu_ref, slope_ref,
    conv_ref, down_ref,
    features_ref, fine_ref, delta_coarse_ref, delta_ref,
    pad_ref, four_ref, coarse_s, mask_s, fine_s, slope_s, *, channels, fields,
):
    (ext_x, ext_y, half, rim), (coarse_x, coarse_y, _, _) = fields
    wide = WIDE
    long = ext_x + 2 * rim
    slab, face = rim * ext_y * half, long * rim * half
    parts = (
        as_field(x_low[:slab, :], rim, ext_y, half),
        as_field(grid_ref[...], ext_x, ext_y, half),
        as_field(x_high[:slab, :], rim, ext_y, half),
    )
    for side, y_ref in enumerate((y_low, y_high)):
        ours, here, there = ((0, rim, 0), (ext_y - 2, 0, 2))[side]
        at = side * long
        pad_ref[at : at + long, there : there + rim] = as_field(y_ref[:face, :], long, rim, half)
        for part in parts:
            count = part.shape[0]
            pad_ref[at : at + count, here : here + 2] = part[:, ours : ours + 2]
            at += count
    fill_four(pad_ref, four_ref, channels)
    coarse_s[1 : 1 + coarse_x, 1 : 1 + coarse_y] = as_field(
        coarse_ref[...], coarse_x, coarse_y, half
    )
    coarse_s[:1, 1 : 1 + coarse_y] = as_field(x_low[slab:, :], 1, coarse_y, half)
    coarse_s[1 + coarse_x :, 1 : 1 + coarse_y] = as_field(x_high[slab:, :], 1, coarse_y, half)
    for y, y_ref in ((0, y_low), (1 + coarse_y, y_high)):
        coarse_s[:, y : y + 1] = as_field(y_ref[face:, :], coarse_x + 2, 1, half)
    wide_x, wide_y = coarse_x + 2, coarse_y + 2
    coarse_rows = wide_x * wide_y * half
    coarse = down_ref.shape[2]
    given = coarse_s[...].reshape(coarse_rows, wide).astype(BF16)
    largest = None
    for j in range(4):
        spot = iota((wide, wide), 0) == coarse + 2 * j + iota((wide, wide), 1) // LANE
        mask = mm(given, one_hot(spot))
        mask_s[:, j // 2, :, j % 2] = mask.reshape(wide_x, wide_y, half, wide)
        largest = mask if largest is None else jnp.maximum(largest, mask)
    largest = jnp.maximum(largest[:, :LANE], largest[:, LANE:])
    coarse_mask = jnp.concatenate([largest, largest[:, : coarse - LANE]], axis=1)

    out_x, out_y = 2 * wide_x, 2 * wide_y
    strip = 3
    boxes = [(0, out_x, 0, strip), (long, out_x, 0, strip)]
    silu, slope = silu_and_slope(convolve(four_ref, conv_ref, boxes))
    shape = (2, out_x, strip, half, wide)
    edge_silu, edge_slope = silu.astype(F32).reshape(shape), slope.reshape(shape)
    columns = out_y - 2 * strip
    mid_silu = as_field(silu_ref[...], out_x, columns, half)
    mid_slope = slope_ref[...].reshape(out_x, columns, half, wide)
    shape = (wide_x, 2, half, wide)
    for y in range(out_y):
        if y < strip:
            silu, slope = edge_silu[0, :, y], edge_slope[0, :, y]
        elif y >= out_y - strip:
            at = y - (out_y - strip)
            silu, slope = edge_silu[1, :, at], edge_slope[1, :, at]
        else:
            silu, slope = mid_silu[:, y - strip], mid_slope[:, y - strip]
        mask = mask_s[:, :, y // 2, y % 2]
        fine_s[:, :, y // 2, y % 2] = silu.reshape(shape) * mask
        slope_s[:, :, y // 2, y % 2] = slope.reshape(shape) * mask
    field = (out_x, out_y, half, wide)
    fine_ref[...] = inner(fine_s[...].reshape(field), 2).astype(BF16)

    pre = None
    for j in range(4):
        piece = fine_s[:, j // 2, :, j % 2].reshape(coarse_rows, wide).astype(BF16)
        part = mm(piece, down_ref[j])
        pre = part if pre is None else pre + part
    sigma = logistic(pre)
    coarse_field = (wide_x, wide_y, half, coarse)
    features = pre * sigma * coarse_mask
    features_ref[...] = inner(features.reshape(coarse_field), 1).astype(BF16)
    slope = sigma * (1.0 + pre * (1.0 - sigma))
    cot = coarse_s[:, :, :, :coarse].reshape(coarse_rows, coarse)
    delta = cot * coarse_mask * slope
    delta_coarse_ref[...] = inner(delta.reshape(coarse_field), 1).astype(BF16)
    delta = delta.astype(BF16)
    for j in range(4):
        back = mm(delta, down_ref[j], NT).reshape(wide_x, wide_y, half, wide)
        fine_s[:, j // 2, :, j % 2] = back * slope_s[:, j // 2, :, j % 2]
    delta_ref[...] = inner(fine_s[...].reshape(field), 1).astype(BF16)


def weight_grad_kernel(
    place_ref, grid_ref, x_low, x_high, y_low, y_high, fine_ref, delta_coarse_ref, delta_ref,
    keep_ref, give_ref, pad_ref, four_ref, delta_s, fine_s, out_ref, *, channels, fields, scale,
):
    (ext_x, ext_y, half, rim), _ = fields
    long = ext_x + 2 * rim
    slab, face = rim * ext_y * half, long * rim * half
    pad_ref[1 : 1 + ext_x, 1 : 1 + ext_y] = as_field(grid_ref[...], ext_x, ext_y, half)
    for x, x_ref, at in ((0, x_low, rim - 1), (1 + ext_x, x_high, 0)):
        field = as_field(x_ref[:slab, :], rim, ext_y, half)
        pad_ref[x : x + 1, 1 : 1 + ext_y] = field[at : at + 1]
    for y, y_ref, at in ((0, y_low, rim - 1), (1 + ext_y, y_high, 0)):
        field = as_field(y_ref[:face, :], long, rim, half)
        pad_ref[:, y : y + 1] = field[rim - 1 : long - rim + 1, at : at + 1]
    fill_four(pad_ref, four_ref, channels)
    delta_s[...] = as_field(delta_ref[...], ext_x + 2, ext_y + 2, half)
    turned = inner(delta_s[...], 1).T.astype(BF16)
    three = 3 * channels
    for j, part in enumerate(windows(four_ref, 0, ext_x, 0, ext_y)):
        grad = mm(turned, part)
        grad = grad[:LANE, :three] + grad[LANE:, channels:]
        out_ref[j * three : (j + 1) * three, :] = grad.T * scale
    fine_s[...] = fine_ref[...].astype(F32).reshape(fine_s.shape)
    coarse_rows = ext_x // 2 * (ext_y // 2) * half
    base = 27 * channels
    for j in range(4):
        piece = fine_s[:, j // 2, :, j % 2].reshape(coarse_rows, WIDE).astype(BF16)
        grad = mm(piece, delta_coarse_ref[...], TN) * scale
        first, second = grad[:channels], grad[LANE : LANE + channels]
        start = base + 2 * j * channels
        out_ref[start : start + channels, :] = first[:, :LANE]
        out_ref[start + channels : start + 2 * channels, :] = second[:, :LANE]
        start = base + (8 + j) * channels
        tail = jnp.concatenate([first[:, LANE:], second[:, LANE:]], axis=1)
        out_ref[start : start + channels, :] = tail
    end = base + 12 * channels
    out_ref[end:, :] = jnp.zeros((out_ref.shape[0] - end, LANE), F32)
    size = keep_ref.shape[0]
    core = place_ref[0] % 2
    keep_ref[...] = out_ref[pl.ds(pl.multiple_of(core * size, size), size), :]
    give = out_ref[pl.ds(pl.multiple_of((1 - core) * size, size), size), :]
    give_ref[...] = give.astype(BF16)


def pair_kernel(keep_ref, other_ref, out_ref):
    out_ref[...] = (keep_ref[...] + other_ref[...].astype(F32)).astype(BF16)


def input_grad_kernel(delta_ref, conv_ref, got_ref, back_ref, pad_ref, four_ref, grad_s, *, channels):
    ext_x, ext_y, half = pad_ref.shape[0] - 2, pad_ref.shape[1] - 2, pad_ref.shape[2]
    pad_ref[...] = as_field(delta_ref[...], ext_x + 2, ext_y + 2, half)
    fill_four(pad_ref, four_ref, channels)
    count = 4
    for first in range(0, ext_x, count):
        rows = slice(first * ext_y * half, (first + count) * ext_y * half)
        grad_s[rows, :] = convolve(four_ref, conv_ref, [(first, count, 0, ext_y)]).astype(BF16)
    grad = grad_s[...]
    pairs = grad.shape[0]
    rows = got_ref.shape[0]
    step = min(256, rows)
    for start in range(0, rows, step):
        found = []
        for q in range(PACK):
            info = got_ref[start : start + step, q * LANE : (q + 1) * LANE].astype(F32)
            place = info[:, channels : channels + 1] * 32.0 + info[:, channels + 1 : channels + 2]
            pick = one_hot(iota((step, pairs), 1) == place.astype(jnp.int32))
            both = mm(pick, grad)
            odd = info[:, channels + 2 : channels + 3] > 0.5
            found.append(jnp.where(odd, both[:, LANE:], both[:, :LANE])[:, :channels])
        back_ref[start : start + step, :] = jnp.concatenate(found, axis=1).astype(BF16)


def join_kernel(terms_ref, back_ref, out_ref, *, block, per_axis):
    total = jnp.sum(terms_ref[...].astype(F32), axis=0)
    rows, wide = back_ref.shape
    out_ref[:, :wide] = back_ref[...]
    lines = total.shape[0] // 2
    halves = []
    for h in range(2):
        parts = [total[h * lines + k : h * lines + k + block] for k in range(0, lines, block)]
        half = jnp.concatenate(parts, axis=1)
        halves.append(jnp.concatenate([half] * per_axis, axis=0).astype(BF16))
    step = block * per_axis
    for g in range(rows // step):
        out_ref[g * step : (g + 1) * step, wide:] = halves[g % 2]


def collect_kernel(back_ref, slot_ref, out_ref):
    channels, points = out_ref.shape
    rows = back_ref.shape[0]
    back = back_ref[:, : PACK * channels]
    step = min(512, points)
    for start in range(0, points, step):
        row = slot_ref[0:1, start : start + step]
        quarter = slot_ref[1:2, start : start + step]
        pick = one_hot(iota((rows, step), 0) == row)
        found = mm(back, pick, TN)
        total = jnp.zeros((channels, step), F32)
        for q in range(PACK):
            total = jnp.where(quarter == q, found[q * channels : (q + 1) * channels], total)
        out_ref[:, start : start + step] = total.astype(BF16)


def unpack_kernel(place_ref, mine_ref, theirs_ref, conv_ref, down_ref, all_s, *, block, per_axis):
    channels = conv_ref.shape[1]
    count = all_s.shape[2] // 2
    skip = mine_ref.shape[1] - theirs_ref.shape[1]
    swap = place_ref[0] % 2 == 1
    step = block * per_axis
    for g in range(mine_ref.shape[0] // step):
        rows = slice(g * step, (g + 1) * step)
        chips = slice(g // 2 * per_axis, (g // 2 + 1) * per_axis)
        for k in range(count):
            mine = mine_ref[rows, skip + k * LANE : skip + (k + 1) * LANE].astype(F32)
            theirs = theirs_ref[rows, k * LANE : (k + 1) * LANE].astype(F32)
            shape = (per_axis, block, LANE)
            all_s[g % 2, chips, k] = jnp.where(swap, theirs, mine).reshape(shape)
            all_s[g % 2, chips, count + k] = jnp.where(swap, mine, theirs).reshape(shape)
    whole = all_s[...].reshape(mine_ref.shape[0] // block * 2 * count * block, LANE)
    base = 27 * channels
    for j in range(27):
        conv_ref[j] = whole[j * channels : (j + 1) * channels, :channels]
    rest = down_ref.shape[2] - LANE
    for j in range(8):
        start = base + j * channels
        down_ref[j, :, :LANE] = whole[start : start + channels]
        start = base + (8 + j // 2) * channels
        tail = whole[start : start + channels]
        down_ref[j, :, LANE:] = tail[:, (j % 2) * rest : (j % 2 + 1) * rest]


def shift(block, axis, step):
    count = lax.axis_size(axis)
    return lax.ppermute(block, axis, [(i, (i + step) % count) for i in range(count)])


def to_other_core(block):
    return lax.ppermute(block, "gx", [(i, i ^ 1) for i in range(lax.axis_size("gx"))])


def exchange(blocks, **groups):
    return lax.all_to_all(blocks, AXES, split_axis=0, concat_axis=0, tiled=True, **groups)


def shards(point_feats, point_owner, point_cell, occupancy, w_conv, w_down, cotangent):
    points, channels = point_feats.shape
    count_x, count_y = lax.axis_size("gx"), lax.axis_size("gy")
    devices = count_x * count_y
    cap = 32
    block = cap // PACK
    ext_x, ext_y, ext_z = occupancy.shape
    half = ext_z // 2
    pairs = ext_x * ext_y * half
    coarse = w_down.shape[2]
    coarse_x, coarse_y = ext_x // 2, ext_y // 2
    coarse_rows = coarse_x * coarse_y * half
    slot_rows = devices * block
    scale = 1.0 / math.sqrt(float(ext_x * ext_y * ext_z * devices))
    four = 4 * channels
    conv_flops = 2 * pairs * 9 * four * WIDE
    pick_flops = 2 * pairs * slot_rows * PACK * WIDE
    rim = 3
    fields = ((ext_x, ext_y, half, rim), (coarse_x, coarse_y, half, 1))

    send, slot = call(
        functools.partial(dispatch_kernel, devices=devices, cap=cap),
        (struct((slot_rows, PACK * LANE), BF16), struct((2, points), jnp.int32)),
        (point_feats.T, point_owner.reshape(1, points), point_cell.reshape(1, points)),
        "dispatch",
        flops=2 * points * slot_rows * PACK * LANE,
    )
    got = exchange(send.reshape(devices, block, PACK * LANE)).reshape(slot_rows, PACK * LANE)
    conv_blocks, back_blocks, down_blocks, given = call(
        functools.partial(prepare_kernel, ext_y=ext_y),
        (
            struct((9 * four, WIDE), BF16),
            struct((9 * four, WIDE), BF16),
            struct((4, WIDE, coarse), BF16),
            struct((coarse_rows, WIDE), BF16),
        ),
        (w_conv, w_down, cotangent.reshape(coarse_rows, coarse),
         occupancy.reshape(ext_x * ext_y, ext_z)),
        "prepare",
        flops=1000000000,
    )
    x_rows = sum(e[3] * e[1] * e[2] for e in fields)
    y_rows = sum(e[3] * (e[0] + 2 * e[3]) * e[2] for e in fields)
    place = jnp.stack([lax.axis_index("gx"), lax.axis_index("gy")]).astype(jnp.int32)
    grid, x_first, x_last = call(
        functools.partial(pool_kernel, channels=channels, fields=fields, count=count_x),
        tuple(struct((n, WIDE), BF16) for n in (pairs, x_rows, x_rows)),
        (place, got, given),
        "pool",
        scratch=[pltpu.VMEM((pairs, WIDE), F32)],
        flops=pick_flops,
    )
    x_low, x_high = shift(x_last, "gx", 1), shift(x_first, "gx", -1)
    y_first, y_last = call(
        functools.partial(edge_kernel, fields=fields, count=count_y),
        tuple(struct((n, WIDE), BF16) for n in (y_rows, y_rows)),
        (place, grid, given, x_low, x_high),
        "edge",
    )
    y_low, y_high = shift(y_last, "gy", 1), shift(y_first, "gy", -1)
    long = ext_x + 2 * rim
    mid_rows = (ext_x + 4) * (ext_y - 2) * half
    silu, slope = call(
        functools.partial(column_kernel, channels=channels),
        (struct((mid_rows, WIDE), BF16), struct((mid_rows, WIDE), F32)),
        (grid, x_low, x_high, conv_blocks),
        "column",
        scratch=[
            pltpu.VMEM((long, ext_y, half, WIDE), F32),
            pltpu.VMEM((long, ext_y, half, four), F32),
        ],
        flops=2 * conv_flops,
    )
    near = (ext_x + 2, ext_y + 2, half)
    near_rows = near[0] * near[1] * half
    split = (coarse_x + 2, 2, coarse_y + 2, 2, half, WIDE)
    faces = (x_low, x_high, y_low, y_high)
    features, fine, delta_coarse, delta = call(
        functools.partial(level_kernel, channels=channels, fields=fields),
        (
            struct((coarse_rows, coarse), BF16),
            struct((pairs, WIDE), BF16),
            struct((coarse_rows, coarse), BF16),
            struct((near_rows, WIDE), BF16),
        ),
        (grid, given, *faces, silu, slope, conv_blocks, down_blocks),
        "level",
        scratch=[
            pltpu.VMEM((2 * long, 5, half, WIDE), F32),
            pltpu.VMEM((2 * long, 5, half, four), F32),
            pltpu.VMEM((coarse_x + 2, coarse_y + 2, half, WIDE), F32),
            pltpu.VMEM(split, F32),
            pltpu.VMEM(split, F32),
            pltpu.VMEM(split, F32),
        ],
        flops=conv_flops,
        megabytes=8,
    )
    used = 39 * channels
    chunk = -(-used // (32 * devices)) * 32
    half_rows = devices // 2 * chunk
    keep, give = call(
        functools.partial(weight_grad_kernel, channels=channels, fields=fields, scale=scale),
        (struct((half_rows, LANE), F32), struct((half_rows, LANE), BF16)),
        (place, grid, *faces, fine, delta_coarse, delta),
        "weight_grad",
        scratch=[
            pltpu.VMEM((*near, WIDE), F32),
            pltpu.VMEM((*near, four), F32),
            pltpu.VMEM((*near, WIDE), F32),
            pltpu.VMEM((coarse_x, 2, coarse_y, 2, half, WIDE), F32),
            pltpu.VMEM((2 * half_rows, LANE), F32),
        ],
        flops=conv_flops,
        megabytes=8,
    )
    both = call(
        pair_kernel, struct((half_rows, LANE), BF16), (keep, to_other_core(give)), "pair"
    )
    terms = exchange(
        both.reshape(devices // 2, chunk, LANE),
        axis_index_groups=[
            [x * count_y + y for x in range(core, count_x, 2) for y in range(count_y)]
            for core in range(2)
        ],
    )
    back = call(
        functools.partial(input_grad_kernel, channels=channels),
        struct((slot_rows, PACK * channels), BF16),
        (delta, back_blocks, got),
        "input_grad",
        scratch=[
            pltpu.VMEM((*near, WIDE), F32),
            pltpu.VMEM((*near, four), F32),
            pltpu.VMEM((pairs, WIDE), BF16),
        ],
        flops=conv_flops + pick_flops,
        megabytes=8,
    )
    half_lanes = chunk // 2 // block * LANE
    joined_lanes = PACK * channels + half_lanes
    joined = call(
        functools.partial(join_kernel, block=block, per_axis=count_y),
        struct((slot_rows, joined_lanes), BF16),
        (terms, back),
        "join",
        flops=devices * chunk * LANE,
    )
    returned = exchange(joined.reshape(devices, block, joined_lanes)).reshape(
        slot_rows, joined_lanes
    )
    theirs = to_other_core(returned[:, PACK * channels :])
    grad_points = call(
        collect_kernel,
        struct((channels, points), BF16),
        (returned, slot),
        "collect",
        flops=2 * points * slot_rows * PACK * LANE,
    ).T
    grad_conv, grad_down = call(
        functools.partial(unpack_kernel, block=block, per_axis=count_y),
        (struct(w_conv.shape, F32), struct(w_down.shape, F32)),
        (place, returned, theirs),
        "unpack",
        scratch=[pltpu.VMEM((2, devices // 2, chunk // block, block, LANE), F32)],
    )
    return (
        features.reshape(coarse_x, coarse_y, half, coarse),
        grad_points,
        grad_conv,
        grad_down,
    )


def solution(mesh):
    placed = (
        P(("gx", "gy"), None),
        P(("gx", "gy"), None),
        P(("gx", "gy")),
        P("gx", "gy", None),
        P(),
        P(),
        P("gx", "gy", None, None),
    )
    return jax.shard_map(
        shards,
        mesh=mesh,
        in_specs=placed,
        out_specs=(P("gx", "gy", None, None), P(("gx", "gy"), None), P(), P()),
        check_vma=False,
    )
```

```python
import functools
import math

import jax
import jax.numpy as jnp
from jax import lax
from jax.experimental import pallas as pl
from jax.experimental.pallas import tpu as pltpu
from jax.sharding import PartitionSpec as P

F32 = jnp.float32
BF16 = jnp.bfloat16
LANE = 128
WIDE = 256
PACK = 4
AXES = ("gx", "gy")
NT = (((1,), (1,)), ((), ()))
NN = (((1,), (0,)), ((), ()))
TN = (((0,), (0,)), ((), ()))


def iota(shape, dim):
    return lax.broadcasted_iota(jnp.int32, shape, dim)


def mm(a, b, dims=NN):
    return lax.dot_general(a, b, dims, preferred_element_type=F32)


def one_hot(mask):
    return jnp.where(mask, 1.0, 0.0).astype(BF16)


def call(
    kernel, outs, args, name, scratch=(), flops=0, megabytes=4, far=(), far_outs=(), grant=24
):
    def spec(index, array, group):
        if index in group:
            return pl.BlockSpec(memory_space=pl.ANY)
        scalars = array.ndim == 1
        return pl.BlockSpec(memory_space=pltpu.SMEM if scalars else pltpu.VMEM)

    single = not isinstance(outs, tuple)
    out_specs = [spec(i, out, far_outs) for i, out in enumerate((outs,) if single else outs)]
    return pl.pallas_call(
        kernel,
        out_shape=outs,
        in_specs=[spec(i, arg, far) for i, arg in enumerate(args)],
        out_specs=out_specs[0] if single else tuple(out_specs),
        scratch_shapes=list(scratch),
        compiler_params=pltpu.CompilerParams(vmem_limit_bytes=grant * 1024 * 1024),
        cost_estimate=pl.CostEstimate(
            flops=flops, bytes_accessed=megabytes * 1000000, transcendentals=0
        ),
        name=name,
    )(*args)


def struct(shape, dtype):
    return jax.ShapeDtypeStruct(shape, dtype)


def dispatch_kernel(
    feats_in, owner_in, cell_in, send_out, slot_ref,
    feats_ref, owner_ref, cell_ref, send_ref, in_sems, out_sems, *, devices, cap,
):
    loads = [
        pltpu.make_async_copy(source, target, in_sems.at[i])
        for i, (source, target) in enumerate(
            ((owner_in, owner_ref), (cell_in, cell_ref), (feats_in, feats_ref))
        )
    ]
    for load in loads:
        load.start()
    channels, points = feats_ref.shape
    loads[0].wait()
    owner = owner_ref[...]
    hot = iota((devices, points), 0) == owner
    block = min(256, points)
    upper = one_hot(iota((block, block), 0) < iota((block, block), 1))
    carry = jnp.zeros((devices, 1), F32)
    ranks = []
    for start in range(0, points, block):
        part = jnp.where(hot[:, start : start + block], 1.0, 0.0)
        before = mm(part.astype(BF16), upper) + carry
        ranks.append(jnp.sum(part * before, axis=0, keepdims=True))
        carry = carry + jnp.sum(part, axis=1, keepdims=True)
    rank = jnp.concatenate(ranks, axis=1).astype(jnp.int32)
    row = owner * (cap // PACK) + (rank >> 2)
    quarter = rank & 3
    slot_ref[0:1, :] = row
    slot_ref[1:2, :] = quarter
    loads[1].wait()
    cell = cell_ref[...]
    line = iota((LANE - channels, points), 0)
    extra = jnp.where(line == 0, cell >> 6, 0)
    extra = jnp.where(line == 1, (cell >> 1) & 31, extra)
    extra = jnp.where(line == 2, cell & 1, extra)
    loads[2].wait()
    whole = jnp.concatenate([feats_ref[...], extra.astype(F32).astype(BF16)], axis=0)
    spread = jnp.concatenate([whole * one_hot(quarter == q) for q in range(PACK)], axis=0)
    rows = send_ref.shape[0]
    step = min(256, rows)
    stores = []
    for start in range(0, rows, step):
        pick = one_hot(iota((step, points), 0) + start == row)
        part = slice(start, start + step)
        send_ref[part, :] = mm(pick, spread, NT).astype(BF16)
        store = pltpu.make_async_copy(
            send_ref.at[part], send_out.at[part], out_sems.at[start // step]
        )
        store.start()
        stores.append(store)
    for store in stores:
        store.wait()


def pool_kernel(
    place_ref, got_ref, coarse_ref, grid_ref, first_ref, last_ref, total_ref,
    *, channels, fields, count,
):
    rows = got_ref.shape[0]
    pairs = grid_ref.shape[0]
    lane = iota((8, LANE), 1)
    weigh = jnp.where(lane == channels, 32.0, jnp.where(lane == channels + 1, 1.0, 0.0))
    weigh = weigh.astype(BF16)
    step = 256
    for q in range(PACK):
        block = got_ref[:, q * LANE : (q + 1) * LANE]
        place = mm(weigh, block, NT)[0:1].astype(jnp.int32)
        odd = block * block[:, channels + 2 : channels + 3]
        both = jnp.concatenate([block - odd, odd], axis=1)
        for start in range(0, pairs, step):
            pick = one_hot(iota((step, rows), 0) + start == place)
            part = mm(pick, both)
            if q:
                part = total_ref[start : start + step, :] + part
            total_ref[start : start + step, :] = part
    at = 0
    for ref, (ext_x, ext_y, half, rim) in zip((total_ref, coarse_ref), fields):
        field = as_field(ref[...], ext_x, ext_y, half)
        put_rows(first_ref, at, field[:rim] * inside(place_ref[0], 0))
        put_rows(last_ref, at, field[ext_x - rim :] * inside(place_ref[0], count - 1))
        at += rim * ext_y * half
    grid_ref[...] = total_ref[...].astype(BF16)


def as_field(rows, ext_x, ext_y, half):
    return rows.astype(F32).reshape(ext_x, ext_y, half, rows.shape[1])


def put_rows(ref, at, field):
    size = field.shape[0] * field.shape[1] * field.shape[2]
    ref[at : at + size, :] = field.reshape(size, field.shape[3]).astype(BF16)


def inside(place, end):
    return jnp.where(place == end, 0.0, 1.0)


def edge_kernel(
    place_ref, grid_ref, coarse_ref, low_ref, high_ref, first_ref, last_ref, *, fields, count
):
    start, at = 0, 0
    for ref, (ext_x, ext_y, half, rim) in zip((grid_ref, coarse_ref), fields):
        size = rim * ext_y * half
        parts = (
            as_field(low_ref[start : start + size, :], rim, ext_y, half),
            as_field(ref[...], ext_x, ext_y, half),
            as_field(high_ref[start : start + size, :], rim, ext_y, half),
        )
        for part in parts:
            put_rows(first_ref, at, part[:, :rim] * inside(place_ref[1], 0))
            put_rows(last_ref, at, part[:, ext_y - rim :] * inside(place_ref[1], count - 1))
            at += part.shape[0] * rim * half
        start += size


def prepare_kernel(
    conv_ref, down_ref, cot_ref, occ_ref, conv_out, back_out, down_out, coarse_out, *, ext_y
):
    channels = conv_ref.shape[1]
    conv_out[...] = jnp.zeros(conv_out.shape, BF16)
    back_out[...] = jnp.zeros(back_out.shape, BF16)
    down_out[...] = jnp.zeros(down_out.shape, BF16)
    four = 4 * channels
    a, b = slice(0, channels), slice(LANE, LANE + channels)
    for j in range(9):
        for k in range(3):
            weight = conv_ref[3 * j + k]
            turned = weight.astype(F32).T.astype(BF16)
            for z in range(2):
                at, side = j * four + (k + z) * channels, (a, b)[z]
                conv_out[at : at + channels, side] = weight
                at = (8 - j) * four + (2 - k + z) * channels
                back_out[at : at + channels, side] = turned
    for j in range(4):
        down_out[j, a, :] = down_ref[2 * j]
        down_out[j, b, :] = down_ref[2 * j + 1]
    columns, depth = occ_ref.shape
    rows, coarse = cot_ref.shape
    half = depth // 2
    rest = WIDE - coarse
    occ = occ_ref[...].astype(F32).astype(BF16)
    row = iota((rows, columns), 0)
    place, column = row // half, iota((rows, columns), 1)
    base = place // (ext_y // 2) * 2 * ext_y + place % (ext_y // 2) * 2
    level = iota((rows, depth), 1) // 2 == iota((rows, depth), 0) % half
    total = jnp.zeros((rows, rest), F32)
    for j in range(4):
        pick = one_hot(base + j // 2 * ext_y + j % 2 == column)
        found = jnp.where(level, mm(pick, occ), 0.0).astype(BF16)
        spot = iota((depth, rest), 1) == 2 * j + iota((depth, rest), 0) % 2
        total = total + mm(found, one_hot(spot))
    coarse_out[:, :coarse] = cot_ref[...]
    coarse_out[:, coarse:] = total.astype(BF16)


def fill_four(pad_ref, four_ref, channels):
    ext_x, ext_y, half, wide = pad_ref.shape
    columns = ext_x * ext_y
    level = iota((columns, half, LANE), 1)
    even = pad_ref[:, :, :, :LANE].reshape(columns, half, LANE)
    odd = pad_ref[:, :, :, LANE:].reshape(columns, half, LANE)
    after = jnp.where(level == half - 1, 0.0, pltpu.roll(even, half - 1, 1))
    before = jnp.where(level == 0, 0.0, pltpu.roll(odd, 1, 1))
    parts = [part[:, :, :channels] for part in (before, even, odd, after)]
    four = jnp.concatenate(parts, axis=2)
    four_ref[...] = four.reshape(ext_x, ext_y, half, 4 * channels)


def windows(ref, first_x, count_x, first_y, count_y):
    parts = []
    for j in range(9):
        x, y = first_x + j // 3, first_y + j % 3
        part = ref[x : x + count_x, y : y + count_y]
        parts.append(part.reshape(count_x * count_y * part.shape[2], part.shape[3]).astype(BF16))
    return parts


def convolve(four_ref, weight_ref, boxes):
    rows = [jnp.concatenate(windows(four_ref, *box), axis=1) for box in boxes]
    return mm(rows[0] if len(rows) == 1 else jnp.concatenate(rows, axis=0), weight_ref[...])


def logistic(values):
    return 1.0 / (1.0 + jnp.exp(-values))


def silu_and_slope(pre):
    sigma = logistic(pre)
    return (pre * sigma).astype(BF16), sigma * (1.0 + pre * (1.0 - sigma))


def inner(field, rim):
    part = field[rim : field.shape[0] - rim, rim : field.shape[1] - rim]
    return part.reshape(part.shape[0] * part.shape[1] * part.shape[2], part.shape[3])


def column_kernel(
    grid_ref, x_low, x_high, conv_ref, silu_ref, slope_ref, pad_ref, four_ref, *, channels
):
    ext_x, ext_y, half = pad_ref.shape[0], pad_ref.shape[1], pad_ref.shape[2]
    rim = 3
    size = rim * ext_y * half
    pad_ref[:rim] = as_field(x_low[:size, :], rim, ext_y, half)
    pad_ref[rim : ext_x - rim] = as_field(grid_ref[...], ext_x - 2 * rim, ext_y, half)
    pad_ref[ext_x - rim :] = as_field(x_high[:size, :], rim, ext_y, half)
    fill_four(pad_ref, four_ref, channels)
    count = 4
    step = count * (ext_y - 2) * half
    for first in range(0, ext_x - 2, count):
        pre = convolve(four_ref, conv_ref, [(first, count, 0, ext_y - 2)])
        rows = slice(first // count * step, (first // count + 1) * step)
        silu_ref[rows, :], slope_ref[rows, :] = silu_and_slope(pre)


def level_kernel(
    grid_ref, coarse_ref, x_low, x_high, y_low, y_high, silu_ref, slope_ref,
    conv_ref, down_ref,
    features_ref, fine_ref, delta_coarse_ref, delta_ref,
    pad_ref, four_ref, coarse_s, mask_s, fine_s, slope_s, *, channels, fields,
):
    (ext_x, ext_y, half, rim), (coarse_x, coarse_y, _, _) = fields
    wide = WIDE
    long = ext_x + 2 * rim
    slab, face = rim * ext_y * half, long * rim * half
    parts = (
        as_field(x_low[:slab, :], rim, ext_y, half),
        as_field(grid_ref[...], ext_x, ext_y, half),
        as_field(x_high[:slab, :], rim, ext_y, half),
    )
    for side, y_ref in enumerate((y_low, y_high)):
        ours, here, there = ((0, rim, 0), (ext_y - 2, 0, 2))[side]
        at = side * long
        pad_ref[at : at + long, there : there + rim] = as_field(y_ref[:face, :], long, rim, half)
        for part in parts:
            count = part.shape[0]
            pad_ref[at : at + count, here : here + 2] = part[:, ours : ours + 2]
            at += count
    fill_four(pad_ref, four_ref, channels)
    coarse_s[1 : 1 + coarse_x, 1 : 1 + coarse_y] = as_field(
        coarse_ref[...], coarse_x, coarse_y, half
    )
    coarse_s[:1, 1 : 1 + coarse_y] = as_field(x_low[slab:, :], 1, coarse_y, half)
    coarse_s[1 + coarse_x :, 1 : 1 + coarse_y] = as_field(x_high[slab:, :], 1, coarse_y, half)
    for y, y_ref in ((0, y_low), (1 + coarse_y, y_high)):
        coarse_s[:, y : y + 1] = as_field(y_ref[face:, :], coarse_x + 2, 1, half)
    wide_x, wide_y = coarse_x + 2, coarse_y + 2
    coarse_rows = wide_x * wide_y * half
    coarse = down_ref.shape[2]
    given = coarse_s[...].reshape(coarse_rows, wide).astype(BF16)
    largest = None
    for j in range(4):
        spot = iota((wide, wide), 0) == coarse + 2 * j + iota((wide, wide), 1) // LANE
        mask = mm(given, one_hot(spot))
        mask_s[:, j // 2, :, j % 2] = mask.reshape(wide_x, wide_y, half, wide)
        largest = mask if largest is None else jnp.maximum(largest, mask)
    largest = jnp.maximum(largest[:, :LANE], largest[:, LANE:])
    coarse_mask = jnp.concatenate([largest, largest[:, : coarse - LANE]], axis=1)

    out_x, out_y = 2 * wide_x, 2 * wide_y
    strip = 3
    boxes = [(0, out_x, 0, strip), (long, out_x, 0, strip)]
    silu, slope = silu_and_slope(convolve(four_ref, conv_ref, boxes))
    shape = (2, out_x, strip, half, wide)
    edge_silu, edge_slope = silu.astype(F32).reshape(shape), slope.reshape(shape)
    columns = out_y - 2 * strip
    mid_silu = as_field(silu_ref[...], out_x, columns, half)
    mid_slope = slope_ref[...].reshape(out_x, columns, half, wide)
    shape = (wide_x, 2, half, wide)
    for y in range(out_y):
        if y < strip:
            silu, slope = edge_silu[0, :, y], edge_slope[0, :, y]
        elif y >= out_y - strip:
            at = y - (out_y - strip)
            silu, slope = edge_silu[1, :, at], edge_slope[1, :, at]
        else:
            silu, slope = mid_silu[:, y - strip], mid_slope[:, y - strip]
        mask = mask_s[:, :, y // 2, y % 2]
        fine_s[:, :, y // 2, y % 2] = silu.reshape(shape) * mask
        slope_s[:, :, y // 2, y % 2] = slope.reshape(shape) * mask
    field = (out_x, out_y, half, wide)
    fine_ref[...] = inner(fine_s[...].reshape(field), 2).astype(BF16)

    pre = None
    for j in range(4):
        piece = fine_s[:, j // 2, :, j % 2].reshape(coarse_rows, wide).astype(BF16)
        part = mm(piece, down_ref[j])
        pre = part if pre is None else pre + part
    sigma = logistic(pre)
    coarse_field = (wide_x, wide_y, half, coarse)
    features = pre * sigma * coarse_mask
    features_ref[...] = inner(features.reshape(coarse_field), 1).astype(BF16)
    slope = sigma * (1.0 + pre * (1.0 - sigma))
    cot = coarse_s[:, :, :, :coarse].reshape(coarse_rows, coarse)
    delta = cot * coarse_mask * slope
    delta_coarse_ref[...] = inner(delta.reshape(coarse_field), 1).astype(BF16)
    delta = delta.astype(BF16)
    for j in range(4):
        back = mm(delta, down_ref[j], NT).reshape(wide_x, wide_y, half, wide)
        fine_s[:, j // 2, :, j % 2] = back * slope_s[:, j // 2, :, j % 2]
    delta_ref[...] = inner(fine_s[...].reshape(field), 1).astype(BF16)


def weight_grad_kernel(
    place_ref, grid_ref, x_low, x_high, y_low, y_high, fine_ref, delta_coarse_ref, delta_ref,
    keep_ref, give_ref, pad_ref, four_ref, delta_s, fine_s, out_ref, *, channels, fields, scale,
):
    (ext_x, ext_y, half, rim), _ = fields
    long = ext_x + 2 * rim
    slab, face = rim * ext_y * half, long * rim * half
    pad_ref[1 : 1 + ext_x, 1 : 1 + ext_y] = as_field(grid_ref[...], ext_x, ext_y, half)
    for x, x_ref, at in ((0, x_low, rim - 1), (1 + ext_x, x_high, 0)):
        field = as_field(x_ref[:slab, :], rim, ext_y, half)
        pad_ref[x : x + 1, 1 : 1 + ext_y] = field[at : at + 1]
    for y, y_ref, at in ((0, y_low, rim - 1), (1 + ext_y, y_high, 0)):
        field = as_field(y_ref[:face, :], long, rim, half)
        pad_ref[:, y : y + 1] = field[rim - 1 : long - rim + 1, at : at + 1]
    fill_four(pad_ref, four_ref, channels)
    delta_s[...] = as_field(delta_ref[...], ext_x + 2, ext_y + 2, half)
    turned = inner(delta_s[...], 1).T.astype(BF16)
    three = 3 * channels
    for j, part in enumerate(windows(four_ref, 0, ext_x, 0, ext_y)):
        grad = mm(turned, part)
        grad = grad[:LANE, :three] + grad[LANE:, channels:]
        out_ref[j * three : (j + 1) * three, :] = grad.T * scale
    fine_s[...] = fine_ref[...].astype(F32).reshape(fine_s.shape)
    coarse_rows = ext_x // 2 * (ext_y // 2) * half
    base = 27 * channels
    for j in range(4):
        piece = fine_s[:, j // 2, :, j % 2].reshape(coarse_rows, WIDE).astype(BF16)
        grad = mm(piece, delta_coarse_ref[...], TN) * scale
        first, second = grad[:channels], grad[LANE : LANE + channels]
        start = base + 2 * j * channels
        out_ref[start : start + channels, :] = first[:, :LANE]
        out_ref[start + channels : start + 2 * channels, :] = second[:, :LANE]
        start = base + (8 + j) * channels
        tail = jnp.concatenate([first[:, LANE:], second[:, LANE:]], axis=1)
        out_ref[start : start + channels, :] = tail
    end = base + 12 * channels
    out_ref[end:, :] = jnp.zeros((out_ref.shape[0] - end, LANE), F32)
    size = keep_ref.shape[0]
    core = place_ref[0] % 2
    keep_ref[...] = out_ref[pl.ds(pl.multiple_of(core * size, size), size), :]
    give = out_ref[pl.ds(pl.multiple_of((1 - core) * size, size), size), :]
    give_ref[...] = give.astype(BF16)


def pair_kernel(keep_ref, other_ref, out_ref):
    out_ref[...] = (keep_ref[...] + other_ref[...].astype(F32)).astype(BF16)


def input_grad_kernel(delta_ref, conv_ref, got_ref, back_ref, pad_ref, four_ref, grad_s, *, channels):
    ext_x, ext_y, half = pad_ref.shape[0] - 2, pad_ref.shape[1] - 2, pad_ref.shape[2]
    pad_ref[...] = as_field(delta_ref[...], ext_x + 2, ext_y + 2, half)
    fill_four(pad_ref, four_ref, channels)
    count = 4
    for first in range(0, ext_x, count):
        rows = slice(first * ext_y * half, (first + count) * ext_y * half)
        grad_s[rows, :] = convolve(four_ref, conv_ref, [(first, count, 0, ext_y)]).astype(BF16)
    grad = grad_s[...]
    pairs = grad.shape[0]
    rows = got_ref.shape[0]
    step = min(256, rows)
    for start in range(0, rows, step):
        found = []
        for q in range(PACK):
            info = got_ref[start : start + step, q * LANE : (q + 1) * LANE].astype(F32)
            place = info[:, channels : channels + 1] * 32.0 + info[:, channels + 1 : channels + 2]
            pick = one_hot(iota((step, pairs), 1) == place.astype(jnp.int32))
            both = mm(pick, grad)
            odd = info[:, channels + 2 : channels + 3] > 0.5
            found.append(jnp.where(odd, both[:, LANE:], both[:, :LANE])[:, :channels])
        back_ref[start : start + step, :] = jnp.concatenate(found, axis=1).astype(BF16)


def join_kernel(terms_ref, back_ref, out_ref, *, block, per_axis):
    total = jnp.sum(terms_ref[...].astype(F32), axis=0)
    rows, wide = back_ref.shape
    out_ref[:, :wide] = back_ref[...]
    lines = total.shape[0] // 2
    halves = []
    for h in range(2):
        parts = [total[h * lines + k : h * lines + k + block] for k in range(0, lines, block)]
        half = jnp.concatenate(parts, axis=1)
        halves.append(jnp.concatenate([half] * per_axis, axis=0).astype(BF16))
    step = block * per_axis
    for g in range(rows // step):
        out_ref[g * step : (g + 1) * step, wide:] = halves[g % 2]


def collect_kernel(back_ref, slot_ref, out_ref):
    channels, points = out_ref.shape
    rows = back_ref.shape[0]
    back = back_ref[:, : PACK * channels]
    step = min(512, points)
    for start in range(0, points, step):
        row = slot_ref[0:1, start : start + step]
        quarter = slot_ref[1:2, start : start + step]
        pick = one_hot(iota((rows, step), 0) == row)
        found = mm(back, pick, TN)
        total = jnp.zeros((channels, step), F32)
        for q in range(PACK):
            total = jnp.where(quarter == q, found[q * channels : (q + 1) * channels], total)
        out_ref[:, start : start + step] = total.astype(BF16)


def unpack_kernel(place_ref, mine_ref, theirs_ref, conv_ref, down_ref, all_s, *, block, per_axis):
    channels = conv_ref.shape[1]
    count = all_s.shape[2] // 2
    skip = mine_ref.shape[1] - theirs_ref.shape[1]
    swap = place_ref[0] % 2 == 1
    step = block * per_axis
    for g in range(mine_ref.shape[0] // step):
        rows = slice(g * step, (g + 1) * step)
        chips = slice(g // 2 * per_axis, (g // 2 + 1) * per_axis)
        for k in range(count):
            mine = mine_ref[rows, skip + k * LANE : skip + (k + 1) * LANE].astype(F32)
            theirs = theirs_ref[rows, k * LANE : (k + 1) * LANE].astype(F32)
            shape = (per_axis, block, LANE)
            all_s[g % 2, chips, k] = jnp.where(swap, theirs, mine).reshape(shape)
            all_s[g % 2, chips, count + k] = jnp.where(swap, mine, theirs).reshape(shape)
    whole = all_s[...].reshape(mine_ref.shape[0] // block * 2 * count * block, LANE)
    base = 27 * channels
    for j in range(27):
        conv_ref[j] = whole[j * channels : (j + 1) * channels, :channels]
    rest = down_ref.shape[2] - LANE
    for j in range(8):
        start = base + j * channels
        down_ref[j, :, :LANE] = whole[start : start + channels]
        start = base + (8 + j // 2) * channels
        tail = whole[start : start + channels]
        down_ref[j, :, LANE:] = tail[:, (j % 2) * rest : (j % 2 + 1) * rest]


def shift(block, axis, step):
    count = lax.axis_size(axis)
    return lax.ppermute(block, axis, [(i, (i + step) % count) for i in range(count)])


def to_other_core(block):
    return lax.ppermute(block, "gx", [(i, i ^ 1) for i in range(lax.axis_size("gx"))])


def exchange(blocks, **groups):
    return lax.all_to_all(blocks, AXES, split_axis=0, concat_axis=0, tiled=True, **groups)


def shards(point_feats, point_owner, point_cell, occupancy, w_conv, w_down, cotangent):
    points, channels = point_feats.shape
    count_x, count_y = lax.axis_size("gx"), lax.axis_size("gy")
    devices = count_x * count_y
    cap = 32
    block = cap // PACK
    ext_x, ext_y, ext_z = occupancy.shape
    half = ext_z // 2
    pairs = ext_x * ext_y * half
    coarse = w_down.shape[2]
    coarse_x, coarse_y = ext_x // 2, ext_y // 2
    coarse_rows = coarse_x * coarse_y * half
    slot_rows = devices * block
    scale = 1.0 / math.sqrt(float(ext_x * ext_y * ext_z * devices))
    four = 4 * channels
    conv_flops = 2 * pairs * 9 * four * WIDE
    pick_flops = 2 * pairs * slot_rows * PACK * WIDE
    rim = 3
    fields = ((ext_x, ext_y, half, rim), (coarse_x, coarse_y, half, 1))

    send, slot = call(
        functools.partial(dispatch_kernel, devices=devices, cap=cap),
        (struct((slot_rows, PACK * LANE), BF16), struct((2, points), jnp.int32)),
        (point_feats.T, point_owner.reshape(1, points), point_cell.reshape(1, points)),
        "dispatch",
        scratch=[
            pltpu.VMEM((channels, points), BF16),
            pltpu.VMEM((1, points), jnp.int32),
            pltpu.VMEM((1, points), jnp.int32),
            pltpu.VMEM((slot_rows, PACK * LANE), BF16),
            pltpu.SemaphoreType.DMA((3,)),
            pltpu.SemaphoreType.DMA((-(-slot_rows // 256),)),
        ],
        flops=2 * points * slot_rows * PACK * LANE,
        far=(0, 1, 2),
        far_outs=(0,),
        grant=56,
    )
    got = exchange(send.reshape(devices, block, PACK * LANE)).reshape(slot_rows, PACK * LANE)
    conv_blocks, back_blocks, down_blocks, given = call(
        functools.partial(prepare_kernel, ext_y=ext_y),
        (
            struct((9 * four, WIDE), BF16),
            struct((9 * four, WIDE), BF16),
            struct((4, WIDE, coarse), BF16),
            struct((coarse_rows, WIDE), BF16),
        ),
        (w_conv, w_down, cotangent.reshape(coarse_rows, coarse),
         occupancy.reshape(ext_x * ext_y, ext_z)),
        "prepare",
        flops=1000000000,
    )
    x_rows = sum(e[3] * e[1] * e[2] for e in fields)
    y_rows = sum(e[3] * (e[0] + 2 * e[3]) * e[2] for e in fields)
    place = jnp.stack([lax.axis_index("gx"), lax.axis_index("gy")]).astype(jnp.int32)
    grid, x_first, x_last = call(
        functools.partial(pool_kernel, channels=channels, fields=fields, count=count_x),
        tuple(struct((n, WIDE), BF16) for n in (pairs, x_rows, x_rows)),
        (place, got, given),
        "pool",
        scratch=[pltpu.VMEM((pairs, WIDE), F32)],
        flops=pick_flops,
    )
    x_low, x_high = shift(x_last, "gx", 1), shift(x_first, "gx", -1)
    y_first, y_last = call(
        functools.partial(edge_kernel, fields=fields, count=count_y),
        tuple(struct((n, WIDE), BF16) for n in (y_rows, y_rows)),
        (place, grid, given, x_low, x_high),
        "edge",
    )
    y_low, y_high = shift(y_last, "gy", 1), shift(y_first, "gy", -1)
    long = ext_x + 2 * rim
    mid_rows = (ext_x + 4) * (ext_y - 2) * half
    silu, slope = call(
        functools.partial(column_kernel, channels=channels),
        (struct((mid_rows, WIDE), BF16), struct((mid_rows, WIDE), F32)),
        (grid, x_low, x_high, conv_blocks),
        "column",
        scratch=[
            pltpu.VMEM((long, ext_y, half, WIDE), F32),
            pltpu.VMEM((long, ext_y, half, four), F32),
        ],
        flops=2 * conv_flops,
    )
    near = (ext_x + 2, ext_y + 2, half)
    near_rows = near[0] * near[1] * half
    split = (coarse_x + 2, 2, coarse_y + 2, 2, half, WIDE)
    faces = (x_low, x_high, y_low, y_high)
    features, fine, delta_coarse, delta = call(
        functools.partial(level_kernel, channels=channels, fields=fields),
        (
            struct((coarse_rows, coarse), BF16),
            struct((pairs, WIDE), BF16),
            struct((coarse_rows, coarse), BF16),
            struct((near_rows, WIDE), BF16),
        ),
        (grid, given, *faces, silu, slope, conv_blocks, down_blocks),
        "level",
        scratch=[
            pltpu.VMEM((2 * long, 5, half, WIDE), F32),
            pltpu.VMEM((2 * long, 5, half, four), F32),
            pltpu.VMEM((coarse_x + 2, coarse_y + 2, half, WIDE), F32),
            pltpu.VMEM(split, F32),
            pltpu.VMEM(split, F32),
            pltpu.VMEM(split, F32),
        ],
        flops=conv_flops,
        megabytes=8,
    )
    used = 39 * channels
    chunk = -(-used // (32 * devices)) * 32
    half_rows = devices // 2 * chunk
    keep, give = call(
        functools.partial(weight_grad_kernel, channels=channels, fields=fields, scale=scale),
        (struct((half_rows, LANE), F32), struct((half_rows, LANE), BF16)),
        (place, grid, *faces, fine, delta_coarse, delta),
        "weight_grad",
        scratch=[
            pltpu.VMEM((*near, WIDE), F32),
            pltpu.VMEM((*near, four), F32),
            pltpu.VMEM((*near, WIDE), F32),
            pltpu.VMEM((coarse_x, 2, coarse_y, 2, half, WIDE), F32),
            pltpu.VMEM((2 * half_rows, LANE), F32),
        ],
        flops=conv_flops,
        megabytes=8,
    )
    both = call(
        pair_kernel, struct((half_rows, LANE), BF16), (keep, to_other_core(give)), "pair"
    )
    terms = exchange(
        both.reshape(devices // 2, chunk, LANE),
        axis_index_groups=[
            [x * count_y + y for x in range(core, count_x, 2) for y in range(count_y)]
            for core in range(2)
        ],
    )
    back = call(
        functools.partial(input_grad_kernel, channels=channels),
        struct((slot_rows, PACK * channels), BF16),
        (delta, back_blocks, got),
        "input_grad",
        scratch=[
            pltpu.VMEM((*near, WIDE), F32),
            pltpu.VMEM((*near, four), F32),
            pltpu.VMEM((pairs, WIDE), BF16),
        ],
        flops=conv_flops + pick_flops,
        megabytes=8,
    )
    half_lanes = chunk // 2 // block * LANE
    joined_lanes = PACK * channels + half_lanes
    joined = call(
        functools.partial(join_kernel, block=block, per_axis=count_y),
        struct((slot_rows, joined_lanes), BF16),
        (terms, back),
        "join",
        flops=devices * chunk * LANE,
    )
    returned = exchange(joined.reshape(devices, block, joined_lanes)).reshape(
        slot_rows, joined_lanes
    )
    theirs = to_other_core(returned[:, PACK * channels :])
    grad_points = call(
        collect_kernel,
        struct((channels, points), BF16),
        (returned, slot),
        "collect",
        flops=2 * points * slot_rows * PACK * LANE,
    ).T
    grad_conv, grad_down = call(
        functools.partial(unpack_kernel, block=block, per_axis=count_y),
        (struct(w_conv.shape, F32), struct(w_down.shape, F32)),
        (place, returned, theirs),
        "unpack",
        scratch=[pltpu.VMEM((2, devices // 2, chunk // block, block, LANE), F32)],
    )
    return (
        features.reshape(coarse_x, coarse_y, half, coarse),
        grad_points,
        grad_conv,
        grad_down,
    )


def solution(mesh):
    placed = (
        P(("gx", "gy"), None),
        P(("gx", "gy"), None),
        P(("gx", "gy")),
        P("gx", "gy", None),
        P(),
        P(),
        P("gx", "gy", None, None),
    )
    return jax.shard_map(
        shards,
        mesh=mesh,
        in_specs=placed,
        out_specs=(P("gx", "gy", None, None), P(("gx", "gy"), None), P(), P()),
        check_vma=False,
    )
```

```python
import functools
import math

import jax
import jax.numpy as jnp
from jax import lax
from jax.experimental import pallas as pl
from jax.experimental.pallas import tpu as pltpu
from jax.sharding import PartitionSpec as P

F32 = jnp.float32
BF16 = jnp.bfloat16
LANE = 128
WIDE = 256
PACK = 4
AXES = ("gx", "gy")
NT = (((1,), (1,)), ((), ()))
NN = (((1,), (0,)), ((), ()))
TN = (((0,), (0,)), ((), ()))


def iota(shape, dim):
    return lax.broadcasted_iota(jnp.int32, shape, dim)


def mm(a, b, dims=NN):
    return lax.dot_general(a, b, dims, preferred_element_type=F32)


def one_hot(mask):
    return jnp.where(mask, 1.0, 0.0).astype(BF16)


def call(
    kernel, outs, args, name, scratch=(), flops=0, megabytes=4, far=(), far_outs=(), grant=24
):
    def spec(index, array, group):
        if index in group:
            return pl.BlockSpec(memory_space=pl.ANY)
        scalars = array.ndim == 1
        return pl.BlockSpec(memory_space=pltpu.SMEM if scalars else pltpu.VMEM)

    single = not isinstance(outs, tuple)
    out_specs = [spec(i, out, far_outs) for i, out in enumerate((outs,) if single else outs)]
    return pl.pallas_call(
        kernel,
        out_shape=outs,
        in_specs=[spec(i, arg, far) for i, arg in enumerate(args)],
        out_specs=out_specs[0] if single else tuple(out_specs),
        scratch_shapes=list(scratch),
        compiler_params=pltpu.CompilerParams(vmem_limit_bytes=grant * 1024 * 1024),
        cost_estimate=pl.CostEstimate(
            flops=flops, bytes_accessed=megabytes * 1000000, transcendentals=0
        ),
        name=name,
    )(*args)


def struct(shape, dtype):
    return jax.ShapeDtypeStruct(shape, dtype)


def dispatch_kernel(
    feats_in, owner_in, cell_in, send_out, slot_ref,
    feats_ref, owner_ref, cell_ref, send_ref, in_sems, out_sems, *, devices, cap,
):
    loads = [
        pltpu.make_async_copy(source, target, in_sems.at[i])
        for i, (source, target) in enumerate(
            ((owner_in, owner_ref), (cell_in, cell_ref), (feats_in, feats_ref))
        )
    ]
    for load in loads:
        load.start()
    channels, points = feats_ref.shape
    loads[0].wait()
    owner = owner_ref[...]
    hot = iota((devices, points), 0) == owner
    block = min(256, points)
    upper = one_hot(iota((block, block), 0) < iota((block, block), 1))
    carry = jnp.zeros((devices, 1), F32)
    ranks = []
    for start in range(0, points, block):
        part = jnp.where(hot[:, start : start + block], 1.0, 0.0)
        before = mm(part.astype(BF16), upper) + carry
        ranks.append(jnp.sum(part * before, axis=0, keepdims=True))
        carry = carry + jnp.sum(part, axis=1, keepdims=True)
    rank = jnp.concatenate(ranks, axis=1).astype(jnp.int32)
    row = owner * (cap // PACK) + (rank >> 2)
    quarter = rank & 3
    slot_ref[0:1, :] = row
    slot_ref[1:2, :] = quarter
    loads[1].wait()
    cell = cell_ref[...]
    line = iota((LANE - channels, points), 0)
    extra = jnp.where(line == 0, cell >> 6, 0)
    extra = jnp.where(line == 1, (cell >> 1) & 31, extra)
    extra = jnp.where(line == 2, cell & 1, extra)
    loads[2].wait()
    whole = jnp.concatenate([feats_ref[...], extra.astype(F32).astype(BF16)], axis=0)
    spread = jnp.concatenate([whole * one_hot(quarter == q) for q in range(PACK)], axis=0)
    rows = send_ref.shape[0]
    step = min(256, rows)
    stores = []
    for start in range(0, rows, step):
        pick = one_hot(iota((step, points), 0) + start == row)
        part = slice(start, start + step)
        send_ref[part, :] = mm(pick, spread, NT).astype(BF16)
        store = pltpu.make_async_copy(
            send_ref.at[part], send_out.at[part], out_sems.at[start // step]
        )
        store.start()
        stores.append(store)
    for store in stores:
        store.wait()


def pool_kernel(
    place_ref, got_ref, coarse_ref, grid_ref, first_ref, last_ref, total_ref,
    *, channels, fields, count,
):
    rows = got_ref.shape[0]
    pairs = grid_ref.shape[0]
    lane = iota((8, LANE), 1)
    weigh = jnp.where(lane == channels, 32.0, jnp.where(lane == channels + 1, 1.0, 0.0))
    weigh = weigh.astype(BF16)
    step = 256
    places, parts = [], []
    for q in range(PACK):
        block = got_ref[:, q * LANE : (q + 1) * LANE]
        places.append(mm(weigh, block, NT)[0:1].astype(jnp.int32))
        odd = block * block[:, channels + 2 : channels + 3]
        parts.append(jnp.concatenate([block - odd, odd], axis=1))
    place = jnp.concatenate(places, axis=1)
    both = jnp.concatenate(parts, axis=0)
    for start in range(0, pairs, step):
        pick = one_hot(iota((step, PACK * rows), 0) + start == place)
        total_ref[start : start + step, :] = mm(pick, both)
    at = 0
    for ref, (ext_x, ext_y, half, rim) in zip((total_ref, coarse_ref), fields):
        field = as_field(ref[...], ext_x, ext_y, half)
        put_rows(first_ref, at, field[:rim] * inside(place_ref[0], 0))
        put_rows(last_ref, at, field[ext_x - rim :] * inside(place_ref[0], count - 1))
        at += rim * ext_y * half
    grid_ref[...] = total_ref[...].astype(BF16)


def as_field(rows, ext_x, ext_y, half):
    return rows.astype(F32).reshape(ext_x, ext_y, half, rows.shape[1])


def put_rows(ref, at, field):
    size = field.shape[0] * field.shape[1] * field.shape[2]
    ref[at : at + size, :] = field.reshape(size, field.shape[3]).astype(BF16)


def inside(place, end):
    return jnp.where(place == end, 0.0, 1.0)


def edge_kernel(
    place_ref, grid_ref, coarse_ref, low_ref, high_ref, first_ref, last_ref, *, fields, count
):
    start, at = 0, 0
    for ref, (ext_x, ext_y, half, rim) in zip((grid_ref, coarse_ref), fields):
        size = rim * ext_y * half
        parts = (
            as_field(low_ref[start : start + size, :], rim, ext_y, half),
            as_field(ref[...], ext_x, ext_y, half),
            as_field(high_ref[start : start + size, :], rim, ext_y, half),
        )
        for part in parts:
            put_rows(first_ref, at, part[:, :rim] * inside(place_ref[1], 0))
            put_rows(last_ref, at, part[:, ext_y - rim :] * inside(place_ref[1], count - 1))
            at += part.shape[0] * rim * half
        start += size


def prepare_kernel(
    conv_ref, down_ref, cot_ref, occ_ref,
    conv_out, back_out, down_out, down_back_out, coarse_out, *, ext_y
):
    channels = conv_ref.shape[1]
    conv_out[...] = jnp.zeros(conv_out.shape, BF16)
    back_out[...] = jnp.zeros(back_out.shape, BF16)
    down_out[...] = jnp.zeros(down_out.shape, BF16)
    down_back_out[...] = jnp.zeros(down_back_out.shape, BF16)
    four = 4 * channels
    a, b = slice(0, channels), slice(LANE, LANE + channels)
    for j in range(9):
        for k in range(3):
            weight = conv_ref[3 * j + k]
            turned = weight.astype(F32).T.astype(BF16)
            for z in range(2):
                at, side = j * four + (k + z) * channels, (a, b)[z]
                conv_out[at : at + channels, side] = weight
                at = (8 - j) * four + (2 - k + z) * channels
                back_out[at : at + channels, side] = turned
    for j in range(8):
        part = slice(j * LANE, j * LANE + channels)
        down_out[part, :] = down_ref[j]
        down_back_out[:, part] = down_ref[j].astype(F32).T.astype(BF16)
    columns, depth = occ_ref.shape
    rows, coarse = cot_ref.shape
    half = depth // 2
    rest = WIDE - coarse
    occ = occ_ref[...].astype(F32).astype(BF16)
    row = iota((rows, columns), 0)
    place, column = row // half, iota((rows, columns), 1)
    base = place // (ext_y // 2) * 2 * ext_y + place % (ext_y // 2) * 2
    level = iota((rows, depth), 1) // 2 == iota((rows, depth), 0) % half
    total = jnp.zeros((rows, rest), F32)
    for j in range(4):
        pick = one_hot(base + j // 2 * ext_y + j % 2 == column)
        found = jnp.where(level, mm(pick, occ), 0.0).astype(BF16)
        spot = iota((depth, rest), 1) == 2 * j + iota((depth, rest), 0) % 2
        total = total + mm(found, one_hot(spot))
    coarse_out[:, :coarse] = cot_ref[...]
    coarse_out[:, coarse:] = total.astype(BF16)


def fill_four(pad_ref, four_ref, channels):
    ext_x, ext_y, half, wide = pad_ref.shape
    columns = ext_x * ext_y
    level = iota((columns, half, LANE), 1)
    even = pad_ref[:, :, :, :LANE].reshape(columns, half, LANE)
    odd = pad_ref[:, :, :, LANE:].reshape(columns, half, LANE)
    after = jnp.where(level == half - 1, 0.0, pltpu.roll(even, half - 1, 1))
    before = jnp.where(level == 0, 0.0, pltpu.roll(odd, 1, 1))
    parts = [part[:, :, :channels] for part in (before, even, odd, after)]
    four = jnp.concatenate(parts, axis=2)
    four_ref[...] = four.reshape(ext_x, ext_y, half, 4 * channels)


def windows(ref, first_x, count_x, first_y, count_y):
    parts = []
    for j in range(9):
        x, y = first_x + j // 3, first_y + j % 3
        part = ref[x : x + count_x, y : y + count_y]
        parts.append(part.reshape(count_x * count_y * part.shape[2], part.shape[3]).astype(BF16))
    return parts


def convolve(four_ref, weight_ref, boxes):
    weight = weight_ref[...]
    return [mm(jnp.concatenate(windows(four_ref, *box), axis=1), weight) for box in boxes]


def logistic(values):
    return 1.0 / (1.0 + jnp.exp(-values))


def silu_and_slope(pre):
    sigma = logistic(pre)
    return (pre * sigma).astype(BF16), sigma * (1.0 + pre * (1.0 - sigma))


def rows_of(field):
    return field.reshape(field.shape[0] * field.shape[1] * field.shape[2], field.shape[3])


def child_masks(coarse_s, mask_s, coarse):
    count_x, count_y, half, wide = coarse_s.shape
    given = rows_of(coarse_s[:, :, :, LANE:]).astype(BF16)
    spot = iota((LANE, 4 * wide), 0) == coarse - LANE + iota((LANE, 4 * wide), 1) // LANE
    masks = mm(given, one_hot(spot))
    largest = None
    for j in range(4):
        mask = masks[:, j * wide : (j + 1) * wide]
        mask_s[:, j // 2, :, j % 2] = mask.reshape(count_x, count_y, half, wide)
        largest = mask if largest is None else jnp.maximum(largest, mask)
    largest = jnp.maximum(largest[:, :LANE], largest[:, LANE:])
    largest = jnp.concatenate([largest, largest[:, : coarse - LANE]], axis=1)
    return largest.reshape(count_x, count_y, half, coarse)


def coarse_pass(
    fine_s, slope_s, delta_s, coarse_s, coarse_mask, down_ref, down_back_ref, first, count
):
    coarse = down_ref.shape[1]
    columns = slice(first, first + count)
    pieces = [rows_of(fine_s[:, j // 2, columns, j % 2]).astype(BF16) for j in range(4)]
    pre = mm(jnp.concatenate(pieces, axis=1), down_ref[...])
    sigma = logistic(pre)
    shape = (coarse_s.shape[0], count, coarse_s.shape[2], coarse)
    mask = rows_of(coarse_mask[:, columns])
    features = (pre * sigma * mask).reshape(shape)
    slope = sigma * (1.0 + pre * (1.0 - sigma))
    delta = (rows_of(coarse_s[:, columns, :, :coarse]) * mask * slope).astype(BF16)
    back = mm(delta, down_back_ref[...])
    for j in range(4):
        part = back[:, j * WIDE : (j + 1) * WIDE].reshape(*shape[:3], WIDE)
        delta_s[:, j // 2, :, j % 2] = part * slope_s[:, j // 2, columns, j % 2]
    return features, delta.astype(F32).reshape(shape)


def as_columns(ref):
    count_x, _, count_y, _, half, wide = ref.shape
    return ref[...].reshape(2 * count_x, 2 * count_y, half, wide)


def middle_kernel(
    grid_ref, coarse_ref, x_low, x_high, conv_ref, down_ref, down_back_ref,
    fine_ref, slope_ref, features_ref, delta_ref, conv_grad_ref, down_grad_ref,
    pad_ref, four_ref, coarse_s, mask_s, fine_s, slope_s, delta_s, *, channels, rim,
):
    ext_x, ext_y, half = pad_ref.shape[0], pad_ref.shape[1], pad_ref.shape[2]
    size = rim * ext_y * half
    pad_ref[:rim] = as_field(x_low[:size, :], rim, ext_y, half)
    pad_ref[rim : ext_x - rim] = as_field(grid_ref[...], ext_x - 2 * rim, ext_y, half)
    pad_ref[ext_x - rim :] = as_field(x_high[:size, :], rim, ext_y, half)
    fill_four(pad_ref, four_ref, channels)
    coarse_x, coarse_y = coarse_s.shape[0], coarse_s.shape[1]
    coarse = down_ref.shape[1]
    coarse_s[:1] = as_field(x_low[size:, :], 1, coarse_y, half)
    coarse_s[1 : coarse_x - 1] = as_field(coarse_ref[...], coarse_x - 2, coarse_y, half)
    coarse_s[coarse_x - 1 :] = as_field(x_high[size:, :], 1, coarse_y, half)
    coarse_mask = child_masks(coarse_s, mask_s, coarse)
    count, inside_y = 4, ext_y - 2
    for first in range(0, ext_x - 2, count):
        (pre,) = convolve(four_ref, conv_ref, [(first, count, 0, inside_y)])
        silu, slope = silu_and_slope(pre)
        silu = as_field(silu, count, inside_y, half)
        slope = slope.reshape(silu.shape)
        part = slice(first // 2, (first + count) // 2)
        shape = (count // 2, 2, half, WIDE)
        for y in range(1, ext_y - 1):
            mask = mask_s[part, :, y // 2, y % 2]
            fine_s[part, :, y // 2, y % 2] = silu[:, y - 1].reshape(shape) * mask
            slope_s[part, :, y // 2, y % 2] = slope[:, y - 1].reshape(shape) * mask
    size = 2 * coarse_x * half
    for at, y in enumerate((1, ext_y - 2)):
        rows = slice(at * size, (at + 1) * size)
        fine_ref[rows, :] = fine_s[:, :, y // 2, y % 2].reshape(size, WIDE).astype(BF16)
        slope_ref[rows, :] = slope_s[:, :, y // 2, y % 2].reshape(size, WIDE)
    middle = coarse_y - 2
    features, delta_coarse = coarse_pass(
        fine_s, slope_s, delta_s, coarse_s, coarse_mask, down_ref, down_back_ref, 1, middle
    )
    features_ref[...] = rows_of(features[1 : coarse_x - 1]).astype(BF16)
    delta = as_columns(delta_s)
    delta_ref[...] = rows_of(delta[1 : 2 * coarse_x - 1]).astype(BF16)
    turned = rows_of(delta[2 : 2 * coarse_x - 2]).T.astype(BF16)
    box = (rim - 1, 2 * (coarse_x - 2), 1, 2 * middle)
    for j, part in enumerate(windows(four_ref, *box)):
        conv_grad_ref[j * LANE : (j + 1) * LANE, :] = fold(mm(turned, part), channels)
    ours = rows_of(delta_coarse[1 : coarse_x - 1]).astype(BF16)
    for j in range(4):
        piece = fine_s[1 : coarse_x - 1, j // 2, 1 : 1 + middle, j % 2]
        down_grad_ref[j * WIDE : (j + 1) * WIDE, :] = mm(rows_of(piece).astype(BF16), ours, TN)


def fold(grad, channels):
    return grad[:LANE, : 3 * channels] + grad[LANE:, channels:]


def strip_kernel(
    place_ref, grid_ref, coarse_ref, x_low, x_high, y_low, y_high, fine_ref, slope_ref,
    mid_features_ref, mid_delta_ref, conv_grad_ref, down_grad_ref, conv_ref, down_ref,
    down_back_ref, features_ref, delta_ref, keep_ref, give_ref,
    pad_ref, four_ref, coarse_s, mask_s, fine_s, slope_s, delta_s, sum_s,
    *, channels, fields, scale,
):
    (ext_x, ext_y, half, rim), (coarse_x, coarse_y, _, _) = fields
    long = ext_x + 2 * rim
    slab, face = rim * ext_y * half, long * rim * half
    parts = (
        as_field(x_low[:slab, :], rim, ext_y, half),
        as_field(grid_ref[...], ext_x, ext_y, half),
        as_field(x_high[:slab, :], rim, ext_y, half),
    )
    for side, y_ref in enumerate((y_low, y_high)):
        ours, here, there = ((0, rim, 0), (ext_y - rim, 0, rim))[side]
        at = side * long
        pad_ref[at : at + long, there : there + rim] = as_field(y_ref[:face, :], long, rim, half)
        for part in parts:
            count = part.shape[0]
            pad_ref[at : at + count, here : here + rim] = part[:, ours : ours + rim]
            at += count
    fill_four(pad_ref, four_ref, channels)
    parts = (
        as_field(x_low[slab:, :], 1, coarse_y, half),
        as_field(coarse_ref[...], coarse_x, coarse_y, half),
        as_field(x_high[slab:, :], 1, coarse_y, half),
    )
    for side, y_ref in enumerate((y_low, y_high)):
        y = side * (coarse_y - 1)
        theirs = 3 * side
        coarse_s[:, theirs : theirs + 1] = as_field(y_ref[face:, :], coarse_x + 2, 1, half)
        at = 0
        for part in parts:
            count = part.shape[0]
            coarse_s[at : at + count, 1 + side : 2 + side] = part[:, y : y + 1]
            at += count
    coarse = down_ref.shape[1]
    coarse_mask = child_masks(coarse_s, mask_s, coarse)
    out_x, strip = ext_x + 4, 3
    boxes = [(0, out_x, 0, strip), (long, out_x, 1, strip)]
    shape = (out_x, strip, half, WIDE)
    ends = [silu_and_slope(pre) for pre in convolve(four_ref, conv_ref, boxes)]
    ends = [(silu.astype(F32).reshape(shape), slope.reshape(shape)) for silu, slope in ends]
    shape = (coarse_x + 2, 2, half, WIDE)
    size = out_x * half
    for y in range(8):
        if y in (3, 4):
            rows = slice((y - 3) * size, (y - 2) * size)
            fine_s[:, :, y // 2, y % 2] = fine_ref[rows, :].astype(F32).reshape(shape)
            slope_s[:, :, y // 2, y % 2] = slope_ref[rows, :].reshape(shape)
        else:
            side, at = y // 5, y % 5
            mask = mask_s[:, :, y // 2, y % 2]
            silu, slope = ends[side]
            fine_s[:, :, y // 2, y % 2] = silu[:, at].reshape(shape) * mask
            slope_s[:, :, y // 2, y % 2] = slope[:, at].reshape(shape) * mask
    features, delta_coarse = coarse_pass(
        fine_s, slope_s, delta_s, coarse_s, coarse_mask, down_ref, down_back_ref, 0, 4
    )
    features = features[1 : 1 + coarse_x]
    mid = as_field(mid_features_ref[...], coarse_x, coarse_y - 2, half)
    features = jnp.concatenate([features[:, 1:2], mid, features[:, 2:3]], axis=1)
    features_ref[...] = rows_of(features).astype(BF16)
    delta = as_columns(delta_s)
    mid = as_field(mid_delta_ref[...], ext_x + 2, ext_y - 4, half)
    near = delta[1 : out_x - 1]
    near = jnp.concatenate([near[:, 1:4], mid, near[:, 4:7]], axis=1)
    delta_ref[...] = rows_of(near).astype(BF16)
    ours = delta[2 : 2 + ext_x]
    turned = jnp.concatenate([rows_of(ours[:, 2:4]), rows_of(ours[:, 4:6])], axis=0)
    turned = turned.T.astype(BF16)
    low = windows(four_ref, rim - 1, ext_x, rim - 1, 2)
    high = windows(four_ref, long + rim - 1, ext_x, 0, 2)
    three = 3 * channels
    for j in range(9):
        grad = fold(mm(turned, jnp.concatenate([low[j], high[j]], axis=0)), channels)
        grad = grad + conv_grad_ref[j * LANE : (j + 1) * LANE, :]
        sum_s[j * three : (j + 1) * three, :] = grad.T * scale
    ours = rows_of(delta_coarse[1 : 1 + coarse_x, 1:3]).astype(BF16)
    base = 27 * channels
    for j in range(4):
        piece = rows_of(fine_s[1 : 1 + coarse_x, j // 2, 1:3, j % 2]).astype(BF16)
        grad = (mm(piece, ours, TN) + down_grad_ref[j * WIDE : (j + 1) * WIDE, :]) * scale
        first, second = grad[:channels], grad[LANE : LANE + channels]
        start = base + 2 * j * channels
        sum_s[start : start + channels, :] = first[:, :LANE]
        sum_s[start + channels : start + 2 * channels, :] = second[:, :LANE]
        start = base + (8 + j) * channels
        sum_s[start : start + channels, :] = jnp.concatenate(
            [first[:, LANE:], second[:, LANE:]], axis=1
        )
    end = base + 12 * channels
    sum_s[end:, :] = jnp.zeros((sum_s.shape[0] - end, LANE), F32)
    size = keep_ref.shape[0]
    core = place_ref[0] % 2
    keep_ref[...] = sum_s[pl.ds(pl.multiple_of(core * size, size), size), :]
    give = sum_s[pl.ds(pl.multiple_of((1 - core) * size, size), size), :]
    give_ref[...] = give.astype(BF16)


def pair_kernel(keep_ref, other_ref, out_ref):
    out_ref[...] = (keep_ref[...] + other_ref[...].astype(F32)).astype(BF16)


def input_grad_kernel(delta_ref, conv_ref, got_ref, back_ref, pad_ref, four_ref, grad_s, *, channels):
    ext_x, ext_y, half = pad_ref.shape[0] - 2, pad_ref.shape[1] - 2, pad_ref.shape[2]
    pad_ref[...] = as_field(delta_ref[...], ext_x + 2, ext_y + 2, half)
    fill_four(pad_ref, four_ref, channels)
    count = 4
    for first in range(0, ext_x, count):
        rows = slice(first * ext_y * half, (first + count) * ext_y * half)
        (grad,) = convolve(four_ref, conv_ref, [(first, count, 0, ext_y)])
        grad_s[rows, :] = grad.astype(BF16)
    grad = grad_s[...]
    pairs = grad.shape[0]
    rows = got_ref.shape[0]
    step = min(256, rows)
    for start in range(0, rows, step):
        found = []
        for q in range(PACK):
            info = got_ref[start : start + step, q * LANE : (q + 1) * LANE].astype(F32)
            place = info[:, channels : channels + 1] * 32.0 + info[:, channels + 1 : channels + 2]
            pick = one_hot(iota((step, pairs), 1) == place.astype(jnp.int32))
            both = mm(pick, grad)
            odd = info[:, channels + 2 : channels + 3] > 0.5
            found.append(jnp.where(odd, both[:, LANE:], both[:, :LANE])[:, :channels])
        back_ref[start : start + step, :] = jnp.concatenate(found, axis=1).astype(BF16)


def join_kernel(terms_ref, back_ref, out_ref, *, block, per_axis):
    total = jnp.sum(terms_ref[...].astype(F32), axis=0)
    rows, wide = back_ref.shape
    out_ref[:, :wide] = back_ref[...]
    lines = total.shape[0] // 2
    halves = []
    for h in range(2):
        parts = [total[h * lines + k : h * lines + k + block] for k in range(0, lines, block)]
        half = jnp.concatenate(parts, axis=1)
        halves.append(jnp.concatenate([half] * per_axis, axis=0).astype(BF16))
    step = block * per_axis
    for g in range(rows // step):
        out_ref[g * step : (g + 1) * step, wide:] = halves[g % 2]


def collect_kernel(back_ref, slot_ref, out_ref):
    channels, points = out_ref.shape
    rows = back_ref.shape[0]
    back = back_ref[:, : PACK * channels]
    step = min(512, points)
    for start in range(0, points, step):
        row = slot_ref[0:1, start : start + step]
        quarter = slot_ref[1:2, start : start + step]
        pick = one_hot(iota((rows, step), 0) == row)
        found = mm(back, pick, TN)
        total = jnp.zeros((channels, step), F32)
        for q in range(PACK):
            total = jnp.where(quarter == q, found[q * channels : (q + 1) * channels], total)
        out_ref[:, start : start + step] = total.astype(BF16)


def unpack_kernel(place_ref, mine_ref, theirs_ref, conv_ref, down_ref, all_s, *, block, per_axis):
    channels = conv_ref.shape[1]
    count = all_s.shape[2] // 2
    skip = mine_ref.shape[1] - theirs_ref.shape[1]
    swap = place_ref[0] % 2 == 1
    step = block * per_axis
    for g in range(mine_ref.shape[0] // step):
        rows = slice(g * step, (g + 1) * step)
        chips = slice(g // 2 * per_axis, (g // 2 + 1) * per_axis)
        for k in range(count):
            mine = mine_ref[rows, skip + k * LANE : skip + (k + 1) * LANE].astype(F32)
            theirs = theirs_ref[rows, k * LANE : (k + 1) * LANE].astype(F32)
            shape = (per_axis, block, LANE)
            all_s[g % 2, chips, k] = jnp.where(swap, theirs, mine).reshape(shape)
            all_s[g % 2, chips, count + k] = jnp.where(swap, mine, theirs).reshape(shape)
    whole = all_s[...].reshape(mine_ref.shape[0] // block * 2 * count * block, LANE)
    base = 27 * channels
    for j in range(27):
        conv_ref[j] = whole[j * channels : (j + 1) * channels, :channels]
    rest = down_ref.shape[2] - LANE
    for j in range(8):
        start = base + j * channels
        down_ref[j, :, :LANE] = whole[start : start + channels]
        start = base + (8 + j // 2) * channels
        tail = whole[start : start + channels]
        down_ref[j, :, LANE:] = tail[:, (j % 2) * rest : (j % 2 + 1) * rest]


def shift(block, axis, step):
    count = lax.axis_size(axis)
    return lax.ppermute(block, axis, [(i, (i + step) % count) for i in range(count)])


def to_other_core(block):
    return lax.ppermute(block, "gx", [(i, i ^ 1) for i in range(lax.axis_size("gx"))])


def exchange(blocks, **groups):
    return lax.all_to_all(blocks, AXES, split_axis=0, concat_axis=0, tiled=True, **groups)


def shards(point_feats, point_owner, point_cell, occupancy, w_conv, w_down, cotangent):
    points, channels = point_feats.shape
    count_x, count_y = lax.axis_size("gx"), lax.axis_size("gy")
    devices = count_x * count_y
    cap = 32
    block = cap // PACK
    ext_x, ext_y, ext_z = occupancy.shape
    half = ext_z // 2
    pairs = ext_x * ext_y * half
    coarse = w_down.shape[2]
    coarse_x, coarse_y = ext_x // 2, ext_y // 2
    coarse_rows = coarse_x * coarse_y * half
    slot_rows = devices * block
    scale = 1.0 / math.sqrt(float(ext_x * ext_y * ext_z * devices))
    four = 4 * channels
    conv_flops = 2 * pairs * 9 * four * WIDE
    pick_flops = 2 * pairs * slot_rows * PACK * WIDE
    rim = 3
    fields = ((ext_x, ext_y, half, rim), (coarse_x, coarse_y, half, 1))

    send, slot = call(
        functools.partial(dispatch_kernel, devices=devices, cap=cap),
        (struct((slot_rows, PACK * LANE), BF16), struct((2, points), jnp.int32)),
        (point_feats.T, point_owner.reshape(1, points), point_cell.reshape(1, points)),
        "dispatch",
        scratch=[
            pltpu.VMEM((channels, points), BF16),
            pltpu.VMEM((1, points), jnp.int32),
            pltpu.VMEM((1, points), jnp.int32),
            pltpu.VMEM((slot_rows, PACK * LANE), BF16),
            pltpu.SemaphoreType.DMA((3,)),
            pltpu.SemaphoreType.DMA((-(-slot_rows // 256),)),
        ],
        flops=2 * points * slot_rows * PACK * LANE,
        far=(0, 1, 2),
        far_outs=(0,),
        grant=56,
    )
    got = exchange(send.reshape(devices, block, PACK * LANE)).reshape(slot_rows, PACK * LANE)
    conv_blocks, back_blocks, down_blocks, down_back, given = call(
        functools.partial(prepare_kernel, ext_y=ext_y),
        (
            struct((9 * four, WIDE), BF16),
            struct((9 * four, WIDE), BF16),
            struct((4 * WIDE, coarse), BF16),
            struct((coarse, 4 * WIDE), BF16),
            struct((coarse_rows, WIDE), BF16),
        ),
        (w_conv, w_down, cotangent.reshape(coarse_rows, coarse),
         occupancy.reshape(ext_x * ext_y, ext_z)),
        "prepare",
        flops=1000000000,
    )
    x_rows = sum(e[3] * e[1] * e[2] for e in fields)
    y_rows = sum(e[3] * (e[0] + 2 * e[3]) * e[2] for e in fields)
    place = jnp.stack([lax.axis_index("gx"), lax.axis_index("gy")]).astype(jnp.int32)
    grid, x_first, x_last = call(
        functools.partial(pool_kernel, channels=channels, fields=fields, count=count_x),
        tuple(struct((n, WIDE), BF16) for n in (pairs, x_rows, x_rows)),
        (place, got, given),
        "pool",
        scratch=[pltpu.VMEM((pairs, WIDE), F32)],
        flops=pick_flops,
    )
    x_low, x_high = shift(x_last, "gx", 1), shift(x_first, "gx", -1)
    y_first, y_last = call(
        functools.partial(edge_kernel, fields=fields, count=count_y),
        tuple(struct((n, WIDE), BF16) for n in (y_rows, y_rows)),
        (place, grid, given, x_low, x_high),
        "edge",
    )
    y_low, y_high = shift(y_last, "gy", 1), shift(y_first, "gy", -1)
    long = ext_x + 2 * rim
    near = (ext_x + 2, ext_y + 2, half)
    near_rows = near[0] * near[1] * half
    edge_rows = 2 * (ext_x + 4) * half

    def split(columns):
        return pltpu.VMEM((coarse_x + 2, 2, columns, 2, half, WIDE), F32)

    middle = call(
        functools.partial(middle_kernel, channels=channels, rim=rim),
        (
            struct((edge_rows, WIDE), BF16),
            struct((edge_rows, WIDE), F32),
            struct((coarse_x * (coarse_y - 2) * half, coarse), BF16),
            struct(((ext_x + 2) * (ext_y - 4) * half, WIDE), BF16),
            struct((9 * LANE, 3 * channels), F32),
            struct((4 * WIDE, coarse), F32),
        ),
        (grid, given, x_low, x_high, conv_blocks, down_blocks, down_back),
        "middle",
        scratch=[
            pltpu.VMEM((long, ext_y, half, WIDE), F32),
            pltpu.VMEM((long, ext_y, half, four), F32),
            pltpu.VMEM((coarse_x + 2, coarse_y, half, WIDE), F32),
            split(coarse_y),
            split(coarse_y),
            split(coarse_y),
            split(coarse_y - 2),
        ],
        flops=3 * conv_flops,
    )
    used = 39 * channels
    chunk = -(-used // (32 * devices)) * 32
    half_rows = devices // 2 * chunk
    features, delta, keep, give = call(
        functools.partial(strip_kernel, channels=channels, fields=fields, scale=scale),
        (
            struct((coarse_rows, coarse), BF16),
            struct((near_rows, WIDE), BF16),
            struct((half_rows, LANE), F32),
            struct((half_rows, LANE), BF16),
        ),
        (place, grid, given, x_low, x_high, y_low, y_high, *middle, conv_blocks, down_blocks,
         down_back),
        "strip",
        scratch=[
            pltpu.VMEM((2 * long, 2 * rim, half, WIDE), F32),
            pltpu.VMEM((2 * long, 2 * rim, half, four), F32),
            pltpu.VMEM((coarse_x + 2, 4, half, WIDE), F32),
            split(4),
            split(4),
            split(4),
            split(4),
            pltpu.VMEM((2 * half_rows, LANE), F32),
        ],
        flops=conv_flops,
        megabytes=8,
    )
    both = call(
        pair_kernel, struct((half_rows, LANE), BF16), (keep, to_other_core(give)), "pair"
    )
    terms = exchange(
        both.reshape(devices // 2, chunk, LANE),
        axis_index_groups=[
            [x * count_y + y for x in range(core, count_x, 2) for y in range(count_y)]
            for core in range(2)
        ],
    )
    back = call(
        functools.partial(input_grad_kernel, channels=channels),
        struct((slot_rows, PACK * channels), BF16),
        (delta, back_blocks, got),
        "input_grad",
        scratch=[
            pltpu.VMEM((*near, WIDE), F32),
            pltpu.VMEM((*near, four), F32),
            pltpu.VMEM((pairs, WIDE), BF16),
        ],
        flops=conv_flops + pick_flops,
        megabytes=8,
    )
    half_lanes = chunk // 2 // block * LANE
    joined_lanes = PACK * channels + half_lanes
    joined = call(
        functools.partial(join_kernel, block=block, per_axis=count_y),
        struct((slot_rows, joined_lanes), BF16),
        (terms, back),
        "join",
        flops=devices * chunk * LANE,
    )
    returned = exchange(joined.reshape(devices, block, joined_lanes)).reshape(
        slot_rows, joined_lanes
    )
    theirs = to_other_core(returned[:, PACK * channels :])
    grad_points = call(
        collect_kernel,
        struct((channels, points), BF16),
        (returned, slot),
        "collect",
        flops=2 * points * slot_rows * PACK * LANE,
    ).T
    grad_conv, grad_down = call(
        functools.partial(unpack_kernel, block=block, per_axis=count_y),
        (struct(w_conv.shape, F32), struct(w_down.shape, F32)),
        (place, returned, theirs),
        "unpack",
        scratch=[pltpu.VMEM((2, devices // 2, chunk // block, block, LANE), F32)],
    )
    return (
        features.reshape(coarse_x, coarse_y, half, coarse),
        grad_points,
        grad_conv,
        grad_down,
    )


def solution(mesh):
    placed = (
        P(("gx", "gy"), None),
        P(("gx", "gy"), None),
        P(("gx", "gy")),
        P("gx", "gy", None),
        P(),
        P(),
        P("gx", "gy", None, None),
    )
    return jax.shard_map(
        shards,
        mesh=mesh,
        in_specs=placed,
        out_specs=(P("gx", "gy", None, None), P(("gx", "gy"), None), P(), P()),
        check_vma=False,
    )
```

```python
import functools
import math

import jax
import jax.numpy as jnp
from jax import lax
from jax.experimental import pallas as pl
from jax.experimental.pallas import tpu as pltpu
from jax.sharding import PartitionSpec as P

F32 = jnp.float32
BF16 = jnp.bfloat16
LANE = 128
WIDE = 256
PACK = 4
AXES = ("gx", "gy")
NT = (((1,), (1,)), ((), ()))
NN = (((1,), (0,)), ((), ()))
TN = (((0,), (0,)), ((), ()))


def iota(shape, dim):
    return lax.broadcasted_iota(jnp.int32, shape, dim)


def mm(a, b, dims=NN):
    return lax.dot_general(a, b, dims, preferred_element_type=F32)


def one_hot(mask):
    return jnp.where(mask, 1.0, 0.0).astype(BF16)


def call(
    kernel, outs, args, name, scratch=(), flops=0, megabytes=4, far=(), far_outs=(), grant=24
):
    def spec(index, array, group):
        if index in group:
            return pl.BlockSpec(memory_space=pl.ANY)
        scalars = array.ndim == 1
        return pl.BlockSpec(memory_space=pltpu.SMEM if scalars else pltpu.VMEM)

    single = not isinstance(outs, tuple)
    out_specs = [spec(i, out, far_outs) for i, out in enumerate((outs,) if single else outs)]
    return pl.pallas_call(
        kernel,
        out_shape=outs,
        in_specs=[spec(i, arg, far) for i, arg in enumerate(args)],
        out_specs=out_specs[0] if single else tuple(out_specs),
        scratch_shapes=list(scratch),
        compiler_params=pltpu.CompilerParams(vmem_limit_bytes=grant * 1024 * 1024),
        cost_estimate=pl.CostEstimate(
            flops=flops, bytes_accessed=megabytes * 1000000, transcendentals=0
        ),
        name=name,
    )(*args)


def struct(shape, dtype):
    return jax.ShapeDtypeStruct(shape, dtype)


def dispatch_kernel(
    feats_in, owner_in, cell_in, send_out, slot_ref,
    feats_ref, owner_ref, cell_ref, send_ref, in_sems, out_sems, *, devices, cap,
):
    loads = [
        pltpu.make_async_copy(source, target, in_sems.at[i])
        for i, (source, target) in enumerate(
            ((owner_in, owner_ref), (cell_in, cell_ref), (feats_in, feats_ref))
        )
    ]
    for load in loads:
        load.start()
    channels, points = feats_ref.shape
    loads[0].wait()
    owner = owner_ref[...]
    hot = iota((devices, points), 0) == owner
    block = min(256, points)
    upper = one_hot(iota((block, block), 0) < iota((block, block), 1))
    carry = jnp.zeros((devices, 1), F32)
    ranks = []
    for start in range(0, points, block):
        part = jnp.where(hot[:, start : start + block], 1.0, 0.0)
        before = mm(part.astype(BF16), upper) + carry
        ranks.append(jnp.sum(part * before, axis=0, keepdims=True))
        carry = carry + jnp.sum(part, axis=1, keepdims=True)
    rank = jnp.concatenate(ranks, axis=1).astype(jnp.int32)
    row = owner * (cap // PACK) + (rank >> 2)
    quarter = rank & 3
    slot_ref[0:1, :] = row
    slot_ref[1:2, :] = quarter
    loads[1].wait()
    cell = cell_ref[...]
    line = iota((LANE - channels, points), 0)
    extra = jnp.where(line == 0, cell >> 6, 0)
    extra = jnp.where(line == 1, (cell >> 1) & 31, extra)
    extra = jnp.where(line == 2, cell & 1, extra)
    loads[2].wait()
    whole = jnp.concatenate([feats_ref[...], extra.astype(F32).astype(BF16)], axis=0)
    spread = jnp.concatenate([whole * one_hot(quarter == q) for q in range(PACK)], axis=0)
    rows = send_ref.shape[0]
    step = min(256, rows)
    stores = []
    for start in range(0, rows, step):
        pick = one_hot(iota((step, points), 0) + start == row)
        part = slice(start, start + step)
        send_ref[part, :] = mm(pick, spread, NT).astype(BF16)
        store = pltpu.make_async_copy(
            send_ref.at[part], send_out.at[part], out_sems.at[start // step]
        )
        store.start()
        stores.append(store)
    for store in stores:
        store.wait()


def pool_kernel(
    place_ref, got_ref, coarse_ref, grid_ref, even_ref, odd_ref, total_ref,
    *, channels, fields, count,
):
    rows = got_ref.shape[0]
    pairs = grid_ref.shape[0]
    lane = iota((8, LANE), 1)
    weigh = jnp.where(lane == channels, 32.0, jnp.where(lane == channels + 1, 1.0, 0.0))
    weigh = weigh.astype(BF16)
    step = 256
    places, parts = [], []
    for q in range(PACK):
        block = got_ref[:, q * LANE : (q + 1) * LANE]
        places.append(mm(weigh, block, NT)[0:1].astype(jnp.int32))
        odd = block * block[:, channels + 2 : channels + 3]
        parts.append(jnp.concatenate([block - odd, odd], axis=1))
    place = jnp.concatenate(places, axis=1)
    both = jnp.concatenate(parts, axis=0)
    for start in range(0, pairs, step):
        pick = one_hot(iota((step, PACK * rows), 0) + start == place)
        total_ref[start : start + step, :] = mm(pick, both)
    at = 0
    for ref, (ext_x, ext_y, half, rim) in zip((total_ref, coarse_ref), fields):
        field = as_field(ref[...], ext_x, ext_y, half)
        first = field[:rim] * inside(place_ref[0], 0)
        last = field[ext_x - rim :] * inside(place_ref[0], count - 1)
        even, odd = by_parity(place_ref[0], first, last)
        put_rows(even_ref, at, even)
        put_rows(odd_ref, at, odd)
        at += rim * ext_y * half
    grid_ref[...] = total_ref[...].astype(BF16)


def as_field(rows, ext_x, ext_y, half):
    return rows.astype(F32).reshape(ext_x, ext_y, half, rows.shape[1])


def put_rows(ref, at, field):
    size = field.shape[0] * field.shape[1] * field.shape[2]
    ref[at : at + size, :] = field.reshape(size, field.shape[3]).astype(BF16)


def inside(place, end):
    return jnp.where(place == end, 0.0, 1.0)


def by_parity(place, one, other):
    swap = place % 2 == 1
    return jnp.where(swap, one, other), jnp.where(swap, other, one)


def edge_kernel(
    place_ref, grid_ref, coarse_ref, x_even, x_odd, even_ref, odd_ref, *, fields, count
):
    start, at = 0, 0
    for ref, (ext_x, ext_y, half, rim) in zip((grid_ref, coarse_ref), fields):
        size = rim * ext_y * half
        x_faces = [as_field(ref_x[start : start + size, :], rim, ext_y, half) for ref_x in (x_even, x_odd)]
        low, high = by_parity(place_ref[0], *x_faces)
        for part in (low, as_field(ref[...], ext_x, ext_y, half), high):
            first = part[:, :rim] * inside(place_ref[1], 0)
            last = part[:, ext_y - rim :] * inside(place_ref[1], count - 1)
            even, odd = by_parity(place_ref[1], first, last)
            put_rows(even_ref, at, even)
            put_rows(odd_ref, at, odd)
            at += part.shape[0] * rim * half
        start += size


def prepare_kernel(
    conv_ref, down_ref, cot_ref, occ_ref,
    conv_out, back_out, down_out, down_back_out, coarse_out, *, ext_y
):
    channels = conv_ref.shape[1]
    conv_out[...] = jnp.zeros(conv_out.shape, BF16)
    back_out[...] = jnp.zeros(back_out.shape, BF16)
    down_out[...] = jnp.zeros(down_out.shape, BF16)
    down_back_out[...] = jnp.zeros(down_back_out.shape, BF16)
    four = 4 * channels
    a, b = slice(0, channels), slice(LANE, LANE + channels)
    for j in range(9):
        for k in range(3):
            weight = conv_ref[3 * j + k]
            turned = weight.astype(F32).T.astype(BF16)
            for z in range(2):
                at, side = j * four + (k + z) * channels, (a, b)[z]
                conv_out[at : at + channels, side] = weight
                at = (8 - j) * four + (2 - k + z) * channels
                back_out[at : at + channels, side] = turned
    for j in range(8):
        part = slice(j * LANE, j * LANE + channels)
        down_out[part, :] = down_ref[j]
        down_back_out[:, part] = down_ref[j].astype(F32).T.astype(BF16)
    columns, depth = occ_ref.shape
    rows, coarse = cot_ref.shape
    half = depth // 2
    rest = WIDE - coarse
    occ = occ_ref[...].astype(F32).astype(BF16)
    row = iota((rows, columns), 0)
    place, column = row // half, iota((rows, columns), 1)
    base = place // (ext_y // 2) * 2 * ext_y + place % (ext_y // 2) * 2
    level = iota((rows, depth), 1) // 2 == iota((rows, depth), 0) % half
    total = jnp.zeros((rows, rest), F32)
    for j in range(4):
        pick = one_hot(base + j // 2 * ext_y + j % 2 == column)
        found = jnp.where(level, mm(pick, occ), 0.0).astype(BF16)
        spot = iota((depth, rest), 1) == 2 * j + iota((depth, rest), 0) % 2
        total = total + mm(found, one_hot(spot))
    coarse_out[:, :coarse] = cot_ref[...]
    coarse_out[:, coarse:] = total.astype(BF16)


def fill_four(pad_ref, four_ref, channels):
    ext_x, ext_y, half, wide = pad_ref.shape
    columns = ext_x * ext_y
    level = iota((columns, half, LANE), 1)
    even = pad_ref[:, :, :, :LANE].reshape(columns, half, LANE)
    odd = pad_ref[:, :, :, LANE:].reshape(columns, half, LANE)
    after = jnp.where(level == half - 1, 0.0, pltpu.roll(even, half - 1, 1))
    before = jnp.where(level == 0, 0.0, pltpu.roll(odd, 1, 1))
    parts = [part[:, :, :channels] for part in (before, even, odd, after)]
    four = jnp.concatenate(parts, axis=2)
    four_ref[...] = four.reshape(ext_x, ext_y, half, 4 * channels)


def windows(ref, first_x, count_x, first_y, count_y):
    parts = []
    for j in range(9):
        x, y = first_x + j // 3, first_y + j % 3
        part = ref[x : x + count_x, y : y + count_y]
        parts.append(part.reshape(count_x * count_y * part.shape[2], part.shape[3]).astype(BF16))
    return parts


def convolve(four_ref, weight_ref, boxes):
    weight = weight_ref[...]
    return [mm(jnp.concatenate(windows(four_ref, *box), axis=1), weight) for box in boxes]


def logistic(values):
    return 1.0 / (1.0 + jnp.exp(-values))


def silu_and_slope(pre):
    sigma = logistic(pre)
    return (pre * sigma).astype(BF16), sigma * (1.0 + pre * (1.0 - sigma))


def rows_of(field):
    return field.reshape(field.shape[0] * field.shape[1] * field.shape[2], field.shape[3])


def child_masks(coarse_s, mask_s, coarse):
    count_x, count_y, half, wide = coarse_s.shape
    given = rows_of(coarse_s[:, :, :, LANE:]).astype(BF16)
    spot = iota((LANE, 4 * wide), 0) == coarse - LANE + iota((LANE, 4 * wide), 1) // LANE
    masks = mm(given, one_hot(spot))
    largest = None
    for j in range(4):
        mask = masks[:, j * wide : (j + 1) * wide]
        mask_s[:, j // 2, :, j % 2] = mask.reshape(count_x, count_y, half, wide)
        largest = mask if largest is None else jnp.maximum(largest, mask)
    largest = jnp.maximum(largest[:, :LANE], largest[:, LANE:])
    largest = jnp.concatenate([largest, largest[:, : coarse - LANE]], axis=1)
    return largest.reshape(count_x, count_y, half, coarse)


def coarse_pass(
    fine_s, slope_s, delta_s, coarse_s, coarse_mask, down_ref, down_back_ref, first, count
):
    coarse = down_ref.shape[1]
    columns = slice(first, first + count)
    pieces = [rows_of(fine_s[:, j // 2, columns, j % 2]).astype(BF16) for j in range(4)]
    pre = mm(jnp.concatenate(pieces, axis=1), down_ref[...])
    sigma = logistic(pre)
    shape = (coarse_s.shape[0], count, coarse_s.shape[2], coarse)
    mask = rows_of(coarse_mask[:, columns])
    features = (pre * sigma * mask).reshape(shape)
    slope = sigma * (1.0 + pre * (1.0 - sigma))
    delta = (rows_of(coarse_s[:, columns, :, :coarse]) * mask * slope).astype(BF16)
    back = mm(delta, down_back_ref[...])
    for j in range(4):
        part = back[:, j * WIDE : (j + 1) * WIDE].reshape(*shape[:3], WIDE)
        delta_s[:, j // 2, :, j % 2] = part * slope_s[:, j // 2, columns, j % 2]
    return features, delta.astype(F32).reshape(shape)


def as_columns(ref):
    count_x, _, count_y, _, half, wide = ref.shape
    return ref[...].reshape(2 * count_x, 2 * count_y, half, wide)


def middle_kernel(
    place_ref, grid_ref, coarse_ref, x_even, x_odd, conv_ref, down_ref, down_back_ref,
    fine_ref, slope_ref, features_ref, delta_ref, conv_grad_ref, down_grad_ref,
    pad_ref, four_ref, coarse_s, mask_s, fine_s, slope_s, delta_s, *, channels, rim,
):
    ext_x, ext_y, half = pad_ref.shape[0], pad_ref.shape[1], pad_ref.shape[2]
    size = rim * ext_y * half
    x_faces = [as_field(ref[:size, :], rim, ext_y, half) for ref in (x_even, x_odd)]
    pad_ref[:rim], pad_ref[ext_x - rim :] = by_parity(place_ref[0], *x_faces)
    pad_ref[rim : ext_x - rim] = as_field(grid_ref[...], ext_x - 2 * rim, ext_y, half)
    fill_four(pad_ref, four_ref, channels)
    coarse_x, coarse_y = coarse_s.shape[0], coarse_s.shape[1]
    coarse = down_ref.shape[1]
    x_faces = [as_field(ref[size:, :], 1, coarse_y, half) for ref in (x_even, x_odd)]
    coarse_s[:1], coarse_s[coarse_x - 1 :] = by_parity(place_ref[0], *x_faces)
    coarse_s[1 : coarse_x - 1] = as_field(coarse_ref[...], coarse_x - 2, coarse_y, half)
    coarse_mask = child_masks(coarse_s, mask_s, coarse)
    count, inside_y = 4, ext_y - 2
    for first in range(0, ext_x - 2, count):
        (pre,) = convolve(four_ref, conv_ref, [(first, count, 0, inside_y)])
        silu, slope = silu_and_slope(pre)
        silu = as_field(silu, count, inside_y, half)
        slope = slope.reshape(silu.shape)
        part = slice(first // 2, (first + count) // 2)
        shape = (count // 2, 2, half, WIDE)
        for y in range(1, ext_y - 1):
            mask = mask_s[part, :, y // 2, y % 2]
            fine_s[part, :, y // 2, y % 2] = silu[:, y - 1].reshape(shape) * mask
            slope_s[part, :, y // 2, y % 2] = slope[:, y - 1].reshape(shape) * mask
    size = 2 * coarse_x * half
    for at, y in enumerate((1, ext_y - 2)):
        rows = slice(at * size, (at + 1) * size)
        fine_ref[rows, :] = fine_s[:, :, y // 2, y % 2].reshape(size, WIDE).astype(BF16)
        slope_ref[rows, :] = slope_s[:, :, y // 2, y % 2].reshape(size, WIDE)
    middle = coarse_y - 2
    features, delta_coarse = coarse_pass(
        fine_s, slope_s, delta_s, coarse_s, coarse_mask, down_ref, down_back_ref, 1, middle
    )
    features_ref[...] = rows_of(features[1 : coarse_x - 1]).astype(BF16)
    delta = as_columns(delta_s)
    delta_ref[...] = rows_of(delta[1 : 2 * coarse_x - 1]).astype(BF16)
    turned = rows_of(delta[2 : 2 * coarse_x - 2]).T.astype(BF16)
    box = (rim - 1, 2 * (coarse_x - 2), 1, 2 * middle)
    for j, part in enumerate(windows(four_ref, *box)):
        conv_grad_ref[j * LANE : (j + 1) * LANE, :] = fold(mm(turned, part), channels)
    ours = rows_of(delta_coarse[1 : coarse_x - 1]).astype(BF16)
    for j in range(4):
        piece = fine_s[1 : coarse_x - 1, j // 2, 1 : 1 + middle, j % 2]
        down_grad_ref[j * WIDE : (j + 1) * WIDE, :] = mm(rows_of(piece).astype(BF16), ours, TN)


def fold(grad, channels):
    return grad[:LANE, : 3 * channels] + grad[LANE:, channels:]


def strip_kernel(
    place_ref, grid_ref, coarse_ref, x_even, x_odd, y_even, y_odd, fine_ref, slope_ref,
    mid_features_ref, mid_delta_ref, conv_grad_ref, down_grad_ref, conv_ref, down_ref,
    down_back_ref, features_ref, delta_ref, keep_ref, give_ref,
    pad_ref, four_ref, coarse_s, mask_s, fine_s, slope_s, delta_s, sum_s,
    *, channels, fields, scale,
):
    (ext_x, ext_y, half, rim), (coarse_x, coarse_y, _, _) = fields
    long = ext_x + 2 * rim
    slab, face = rim * ext_y * half, long * rim * half
    x_faces = [as_field(ref[:slab, :], rim, ext_y, half) for ref in (x_even, x_odd)]
    low, high = by_parity(place_ref[0], *x_faces)
    parts = (low, as_field(grid_ref[...], ext_x, ext_y, half), high)
    y_faces = [as_field(ref[:face, :], long, rim, half) for ref in (y_even, y_odd)]
    for side, y_face in enumerate(by_parity(place_ref[1], *y_faces)):
        ours, here, there = ((0, rim, 0), (ext_y - rim, 0, rim))[side]
        at = side * long
        pad_ref[at : at + long, there : there + rim] = y_face
        for part in parts:
            count = part.shape[0]
            pad_ref[at : at + count, here : here + rim] = part[:, ours : ours + rim]
            at += count
    fill_four(pad_ref, four_ref, channels)
    x_faces = [as_field(ref[slab:, :], 1, coarse_y, half) for ref in (x_even, x_odd)]
    low, high = by_parity(place_ref[0], *x_faces)
    parts = (low, as_field(coarse_ref[...], coarse_x, coarse_y, half), high)
    y_faces = [as_field(ref[face:, :], coarse_x + 2, 1, half) for ref in (y_even, y_odd)]
    for side, y_face in enumerate(by_parity(place_ref[1], *y_faces)):
        y = side * (coarse_y - 1)
        theirs = 3 * side
        coarse_s[:, theirs : theirs + 1] = y_face
        at = 0
        for part in parts:
            count = part.shape[0]
            coarse_s[at : at + count, 1 + side : 2 + side] = part[:, y : y + 1]
            at += count
    coarse = down_ref.shape[1]
    coarse_mask = child_masks(coarse_s, mask_s, coarse)
    out_x, strip = ext_x + 4, 3
    boxes = [(0, out_x, 0, strip), (long, out_x, 1, strip)]
    shape = (out_x, strip, half, WIDE)
    ends = [silu_and_slope(pre) for pre in convolve(four_ref, conv_ref, boxes)]
    ends = [(silu.astype(F32).reshape(shape), slope.reshape(shape)) for silu, slope in ends]
    shape = (coarse_x + 2, 2, half, WIDE)
    size = out_x * half
    for y in range(8):
        if y in (3, 4):
            rows = slice((y - 3) * size, (y - 2) * size)
            fine_s[:, :, y // 2, y % 2] = fine_ref[rows, :].astype(F32).reshape(shape)
            slope_s[:, :, y // 2, y % 2] = slope_ref[rows, :].reshape(shape)
        else:
            side, at = y // 5, y % 5
            mask = mask_s[:, :, y // 2, y % 2]
            silu, slope = ends[side]
            fine_s[:, :, y // 2, y % 2] = silu[:, at].reshape(shape) * mask
            slope_s[:, :, y // 2, y % 2] = slope[:, at].reshape(shape) * mask
    features, delta_coarse = coarse_pass(
        fine_s, slope_s, delta_s, coarse_s, coarse_mask, down_ref, down_back_ref, 0, 4
    )
    features = features[1 : 1 + coarse_x]
    mid = as_field(mid_features_ref[...], coarse_x, coarse_y - 2, half)
    features = jnp.concatenate([features[:, 1:2], mid, features[:, 2:3]], axis=1)
    features_ref[...] = rows_of(features).astype(BF16)
    delta = as_columns(delta_s)
    mid = as_field(mid_delta_ref[...], ext_x + 2, ext_y - 4, half)
    near = delta[1 : out_x - 1]
    near = jnp.concatenate([near[:, 1:4], mid, near[:, 4:7]], axis=1)
    delta_ref[...] = rows_of(near).astype(BF16)
    ours = delta[2 : 2 + ext_x]
    turned = jnp.concatenate([rows_of(ours[:, 2:4]), rows_of(ours[:, 4:6])], axis=0)
    turned = turned.T.astype(BF16)
    low = windows(four_ref, rim - 1, ext_x, rim - 1, 2)
    high = windows(four_ref, long + rim - 1, ext_x, 0, 2)
    three = 3 * channels
    for j in range(9):
        grad = fold(mm(turned, jnp.concatenate([low[j], high[j]], axis=0)), channels)
        grad = grad + conv_grad_ref[j * LANE : (j + 1) * LANE, :]
        sum_s[j * three : (j + 1) * three, :] = (grad * scale).astype(BF16).T
    ours = rows_of(delta_coarse[1 : 1 + coarse_x, 1:3]).astype(BF16)
    base = 27 * channels
    for j in range(4):
        piece = rows_of(fine_s[1 : 1 + coarse_x, j // 2, 1:3, j % 2]).astype(BF16)
        grad = (mm(piece, ours, TN) + down_grad_ref[j * WIDE : (j + 1) * WIDE, :]) * scale
        grad = grad.astype(BF16)
        first, second = grad[:channels], grad[LANE : LANE + channels]
        start = base + 2 * j * channels
        sum_s[start : start + channels, :] = first[:, :LANE]
        sum_s[start + channels : start + 2 * channels, :] = second[:, :LANE]
        start = base + (8 + j) * channels
        sum_s[start : start + channels, :] = jnp.concatenate(
            [first[:, LANE:], second[:, LANE:]], axis=1
        )
    end = base + 12 * channels
    sum_s[end:, :] = jnp.zeros((sum_s.shape[0] - end, LANE), BF16)
    size = keep_ref.shape[0]
    core = place_ref[0] % 2
    keep_ref[...] = sum_s[pl.ds(pl.multiple_of(core * size, size), size), :]
    give_ref[...] = sum_s[pl.ds(pl.multiple_of((1 - core) * size, size), size), :]


def pair_kernel(keep_ref, other_ref, out_ref):
    out_ref[...] = (keep_ref[...].astype(F32) + other_ref[...].astype(F32)).astype(BF16)


def input_grad_kernel(delta_ref, conv_ref, got_ref, back_ref, pad_ref, four_ref, grad_s, *, channels):
    ext_x, ext_y, half = pad_ref.shape[0] - 2, pad_ref.shape[1] - 2, pad_ref.shape[2]
    pad_ref[...] = as_field(delta_ref[...], ext_x + 2, ext_y + 2, half)
    fill_four(pad_ref, four_ref, channels)
    count = 4
    for first in range(0, ext_x, count):
        rows = slice(first * ext_y * half, (first + count) * ext_y * half)
        (grad,) = convolve(four_ref, conv_ref, [(first, count, 0, ext_y)])
        grad_s[rows, :] = grad.astype(BF16)
    grad = grad_s[...]
    pairs = grad.shape[0]
    rows = got_ref.shape[0]
    step = min(256, rows)
    for start in range(0, rows, step):
        found = []
        for q in range(PACK):
            info = got_ref[start : start + step, q * LANE : (q + 1) * LANE].astype(F32)
            place = info[:, channels : channels + 1] * 32.0 + info[:, channels + 1 : channels + 2]
            pick = one_hot(iota((step, pairs), 1) == place.astype(jnp.int32))
            both = mm(pick, grad)
            odd = info[:, channels + 2 : channels + 3] > 0.5
            found.append(jnp.where(odd, both[:, LANE:], both[:, :LANE])[:, :channels])
        back_ref[start : start + step, :] = jnp.concatenate(found, axis=1).astype(BF16)


def join_kernel(terms_ref, back_ref, out_ref, *, block, per_axis):
    total = jnp.sum(terms_ref[...].astype(F32), axis=0)
    rows, wide = back_ref.shape
    out_ref[:, :wide] = back_ref[...]
    lines = total.shape[0] // 2
    halves = []
    for h in range(2):
        parts = [total[h * lines + k : h * lines + k + block] for k in range(0, lines, block)]
        half = jnp.concatenate(parts, axis=1)
        halves.append(jnp.concatenate([half] * per_axis, axis=0).astype(BF16))
    step = block * per_axis
    for g in range(rows // step):
        out_ref[g * step : (g + 1) * step, wide:] = halves[g % 2]


def collect_kernel(back_ref, slot_ref, out_ref):
    channels, points = out_ref.shape
    rows = back_ref.shape[0]
    back = back_ref[:, : PACK * channels]
    step = min(512, points)
    for start in range(0, points, step):
        row = slot_ref[0:1, start : start + step]
        quarter = slot_ref[1:2, start : start + step]
        pick = one_hot(iota((rows, step), 0) == row)
        found = mm(back, pick, TN)
        total = jnp.zeros((channels, step), F32)
        for q in range(PACK):
            total = jnp.where(quarter == q, found[q * channels : (q + 1) * channels], total)
        out_ref[:, start : start + step] = total.astype(BF16)


def unpack_kernel(place_ref, mine_ref, theirs_ref, conv_ref, down_ref, all_s, *, block, per_axis):
    channels = conv_ref.shape[1]
    count = all_s.shape[2] // 2
    skip = mine_ref.shape[1] - theirs_ref.shape[1]
    swap = place_ref[0] % 2 == 1
    step = block * per_axis
    for g in range(mine_ref.shape[0] // step):
        rows = slice(g * step, (g + 1) * step)
        chips = slice(g // 2 * per_axis, (g // 2 + 1) * per_axis)
        for k in range(count):
            mine = mine_ref[rows, skip + k * LANE : skip + (k + 1) * LANE].astype(F32)
            theirs = theirs_ref[rows, k * LANE : (k + 1) * LANE].astype(F32)
            shape = (per_axis, block, LANE)
            all_s[g % 2, chips, k] = jnp.where(swap, theirs, mine).reshape(shape)
            all_s[g % 2, chips, count + k] = jnp.where(swap, mine, theirs).reshape(shape)
    whole = all_s[...].reshape(mine_ref.shape[0] // block * 2 * count * block, LANE)
    base = 27 * channels
    for j in range(27):
        conv_ref[j] = whole[j * channels : (j + 1) * channels, :channels]
    rest = down_ref.shape[2] - LANE
    for j in range(8):
        start = base + j * channels
        down_ref[j, :, :LANE] = whole[start : start + channels]
        start = base + (8 + j // 2) * channels
        tail = whole[start : start + channels]
        down_ref[j, :, LANE:] = tail[:, (j % 2) * rest : (j % 2 + 1) * rest]


def swap_faces(even, odd, axis):
    count = lax.axis_size(axis)
    pairs = [
        [(i, (i + 1) % count) for i in range(start, count, 2)]
        + [((i + 1) % count, i) for i in range(start, count, 2)]
        for start in range(2)
    ]
    odd = lax.ppermute(odd, axis, pairs[1])
    return lax.ppermute(even, axis, pairs[0]), odd


def to_other_core(block):
    return lax.ppermute(block, "gx", [(i, i ^ 1) for i in range(lax.axis_size("gx"))])


def exchange(blocks, **groups):
    return lax.all_to_all(blocks, AXES, split_axis=0, concat_axis=0, tiled=True, **groups)


def shards(point_feats, point_owner, point_cell, occupancy, w_conv, w_down, cotangent):
    points, channels = point_feats.shape
    count_x, count_y = lax.axis_size("gx"), lax.axis_size("gy")
    devices = count_x * count_y
    cap = 32
    block = cap // PACK
    ext_x, ext_y, ext_z = occupancy.shape
    half = ext_z // 2
    pairs = ext_x * ext_y * half
    coarse = w_down.shape[2]
    coarse_x, coarse_y = ext_x // 2, ext_y // 2
    coarse_rows = coarse_x * coarse_y * half
    slot_rows = devices * block
    scale = 1.0 / math.sqrt(float(ext_x * ext_y * ext_z * devices))
    four = 4 * channels
    conv_flops = 2 * pairs * 9 * four * WIDE
    pick_flops = 2 * pairs * slot_rows * PACK * WIDE
    rim = 3
    fields = ((ext_x, ext_y, half, rim), (coarse_x, coarse_y, half, 1))

    send, slot = call(
        functools.partial(dispatch_kernel, devices=devices, cap=cap),
        (struct((slot_rows, PACK * LANE), BF16), struct((2, points), jnp.int32)),
        (point_feats.T, point_owner.reshape(1, points), point_cell.reshape(1, points)),
        "dispatch",
        scratch=[
            pltpu.VMEM((channels, points), BF16),
            pltpu.VMEM((1, points), jnp.int32),
            pltpu.VMEM((1, points), jnp.int32),
            pltpu.VMEM((slot_rows, PACK * LANE), BF16),
            pltpu.SemaphoreType.DMA((3,)),
            pltpu.SemaphoreType.DMA((-(-slot_rows // 256),)),
        ],
        flops=2 * points * slot_rows * PACK * LANE,
        far=(0, 1, 2),
        far_outs=(0,),
        grant=56,
    )
    got = exchange(send.reshape(devices, block, PACK * LANE)).reshape(slot_rows, PACK * LANE)
    conv_blocks, back_blocks, down_blocks, down_back, given = call(
        functools.partial(prepare_kernel, ext_y=ext_y),
        (
            struct((9 * four, WIDE), BF16),
            struct((9 * four, WIDE), BF16),
            struct((4 * WIDE, coarse), BF16),
            struct((coarse, 4 * WIDE), BF16),
            struct((coarse_rows, WIDE), BF16),
        ),
        (w_conv, w_down, cotangent.reshape(coarse_rows, coarse),
         occupancy.reshape(ext_x * ext_y, ext_z)),
        "prepare",
        flops=1000000000,
    )
    x_rows = sum(e[3] * e[1] * e[2] for e in fields)
    y_rows = sum(e[3] * (e[0] + 2 * e[3]) * e[2] for e in fields)
    place = jnp.stack([lax.axis_index("gx"), lax.axis_index("gy")]).astype(jnp.int32)
    grid, x_even, x_odd = call(
        functools.partial(pool_kernel, channels=channels, fields=fields, count=count_x),
        tuple(struct((n, WIDE), BF16) for n in (pairs, x_rows, x_rows)),
        (place, got, given),
        "pool",
        scratch=[pltpu.VMEM((pairs, WIDE), F32)],
        flops=pick_flops,
    )
    x_faces = swap_faces(x_even, x_odd, "gx")
    y_even, y_odd = call(
        functools.partial(edge_kernel, fields=fields, count=count_y),
        tuple(struct((n, WIDE), BF16) for n in (y_rows, y_rows)),
        (place, grid, given, *x_faces),
        "edge",
    )
    y_faces = swap_faces(y_even, y_odd, "gy")
    long = ext_x + 2 * rim
    near = (ext_x + 2, ext_y + 2, half)
    near_rows = near[0] * near[1] * half
    edge_rows = 2 * (ext_x + 4) * half

    def split(columns):
        return pltpu.VMEM((coarse_x + 2, 2, columns, 2, half, WIDE), F32)

    middle = call(
        functools.partial(middle_kernel, channels=channels, rim=rim),
        (
            struct((edge_rows, WIDE), BF16),
            struct((edge_rows, WIDE), F32),
            struct((coarse_x * (coarse_y - 2) * half, coarse), BF16),
            struct(((ext_x + 2) * (ext_y - 4) * half, WIDE), BF16),
            struct((9 * LANE, 3 * channels), F32),
            struct((4 * WIDE, coarse), F32),
        ),
        (place, grid, given, *x_faces, conv_blocks, down_blocks, down_back),
        "middle",
        scratch=[
            pltpu.VMEM((long, ext_y, half, WIDE), F32),
            pltpu.VMEM((long, ext_y, half, four), F32),
            pltpu.VMEM((coarse_x + 2, coarse_y, half, WIDE), F32),
            split(coarse_y),
            split(coarse_y),
            split(coarse_y),
            split(coarse_y - 2),
        ],
        flops=3 * conv_flops,
    )
    used = 39 * channels
    chunk = -(-used // (32 * devices)) * 32
    half_rows = devices // 2 * chunk
    features, delta, keep, give = call(
        functools.partial(strip_kernel, channels=channels, fields=fields, scale=scale),
        (
            struct((coarse_rows, coarse), BF16),
            struct((near_rows, WIDE), BF16),
            struct((half_rows, LANE), BF16),
            struct((half_rows, LANE), BF16),
        ),
        (place, grid, given, *x_faces, *y_faces, *middle, conv_blocks, down_blocks, down_back),
        "strip",
        scratch=[
            pltpu.VMEM((2 * long, 2 * rim, half, WIDE), F32),
            pltpu.VMEM((2 * long, 2 * rim, half, four), F32),
            pltpu.VMEM((coarse_x + 2, 4, half, WIDE), F32),
            split(4),
            split(4),
            split(4),
            split(4),
            pltpu.VMEM((2 * half_rows, LANE), BF16),
        ],
        flops=conv_flops,
        megabytes=8,
    )
    both = call(
        pair_kernel, struct((half_rows, LANE), BF16), (keep, to_other_core(give)), "pair"
    )
    terms = exchange(
        both.reshape(devices // 2, chunk, LANE),
        axis_index_groups=[
            [x * count_y + y for x in range(core, count_x, 2) for y in range(count_y)]
            for core in range(2)
        ],
    )
    back = call(
        functools.partial(input_grad_kernel, channels=channels),
        struct((slot_rows, PACK * channels), BF16),
        (delta, back_blocks, got),
        "input_grad",
        scratch=[
            pltpu.VMEM((*near, WIDE), F32),
            pltpu.VMEM((*near, four), F32),
            pltpu.VMEM((pairs, WIDE), BF16),
        ],
        flops=conv_flops + pick_flops,
        megabytes=8,
    )
    half_lanes = chunk // 2 // block * LANE
    joined_lanes = PACK * channels + half_lanes
    joined = call(
        functools.partial(join_kernel, block=block, per_axis=count_y),
        struct((slot_rows, joined_lanes), BF16),
        (terms, back),
        "join",
        flops=devices * chunk * LANE,
    )
    returned = exchange(joined.reshape(devices, block, joined_lanes)).reshape(
        slot_rows, joined_lanes
    )
    theirs = to_other_core(returned[:, PACK * channels :])
    grad_points = call(
        collect_kernel,
        struct((channels, points), BF16),
        (returned, slot),
        "collect",
        flops=2 * points * slot_rows * PACK * LANE,
    ).T
    grad_conv, grad_down = call(
        functools.partial(unpack_kernel, block=block, per_axis=count_y),
        (struct(w_conv.shape, F32), struct(w_down.shape, F32)),
        (place, returned, theirs),
        "unpack",
        scratch=[pltpu.VMEM((2, devices // 2, chunk // block, block, LANE), F32)],
    )
    return (
        features.reshape(coarse_x, coarse_y, half, coarse),
        grad_points,
        grad_conv,
        grad_down,
    )


def solution(mesh):
    placed = (
        P(("gx", "gy"), None),
        P(("gx", "gy"), None),
        P(("gx", "gy")),
        P("gx", "gy", None),
        P(),
        P(),
        P("gx", "gy", None, None),
    )
    return jax.shard_map(
        shards,
        mesh=mesh,
        in_specs=placed,
        out_specs=(P("gx", "gy", None, None), P(("gx", "gy"), None), P(), P()),
        check_vma=False,
    )
```

```python
import functools
import math

import jax
import jax.numpy as jnp
from jax import lax
from jax.experimental import pallas as pl
from jax.experimental.pallas import tpu as pltpu
from jax.sharding import PartitionSpec as P

F32 = jnp.float32
BF16 = jnp.bfloat16
LANE = 128
WIDE = 256
PACK = 4
AXES = ("gx", "gy")
NT = (((1,), (1,)), ((), ()))
NN = (((1,), (0,)), ((), ()))
TN = (((0,), (0,)), ((), ()))


def iota(shape, dim):
    return lax.broadcasted_iota(jnp.int32, shape, dim)


def mm(a, b, dims=NN):
    return lax.dot_general(a, b, dims, preferred_element_type=F32)


def one_hot(mask):
    return jnp.where(mask, 1.0, 0.0).astype(BF16)


def call(
    kernel, outs, args, name, scratch=(), flops=0, megabytes=4, far=(), far_outs=(), grant=24
):
    def spec(index, array, group):
        if index in group:
            return pl.BlockSpec(memory_space=pl.ANY)
        scalars = array.ndim == 1
        return pl.BlockSpec(memory_space=pltpu.SMEM if scalars else pltpu.VMEM)

    single = not isinstance(outs, tuple)
    out_specs = [spec(i, out, far_outs) for i, out in enumerate((outs,) if single else outs)]
    return pl.pallas_call(
        kernel,
        out_shape=outs,
        in_specs=[spec(i, arg, far) for i, arg in enumerate(args)],
        out_specs=out_specs[0] if single else tuple(out_specs),
        scratch_shapes=list(scratch),
        compiler_params=pltpu.CompilerParams(vmem_limit_bytes=grant * 1024 * 1024),
        cost_estimate=pl.CostEstimate(
            flops=flops, bytes_accessed=megabytes * 1000000, transcendentals=0
        ),
        name=name,
    )(*args)


def struct(shape, dtype):
    return jax.ShapeDtypeStruct(shape, dtype)


def dispatch_kernel(
    feats_in, owner_in, cell_in, send_out, slot_ref,
    feats_ref, owner_ref, cell_ref, send_ref, in_sems, out_sems, *, devices, cap,
):
    loads = [
        pltpu.make_async_copy(source, target, in_sems.at[i])
        for i, (source, target) in enumerate(
            ((owner_in, owner_ref), (cell_in, cell_ref), (feats_in, feats_ref))
        )
    ]
    for load in loads:
        load.start()
    channels, points = feats_ref.shape
    loads[0].wait()
    owner = owner_ref[...]
    hot = iota((devices, points), 0) == owner
    block = min(256, points)
    upper = one_hot(iota((block, block), 0) < iota((block, block), 1))
    carry = jnp.zeros((devices, 1), F32)
    ranks = []
    for start in range(0, points, block):
        part = jnp.where(hot[:, start : start + block], 1.0, 0.0)
        before = mm(part.astype(BF16), upper) + carry
        ranks.append(jnp.sum(part * before, axis=0, keepdims=True))
        carry = carry + jnp.sum(part, axis=1, keepdims=True)
    rank = jnp.concatenate(ranks, axis=1).astype(jnp.int32)
    row = owner * (cap // PACK) + (rank >> 2)
    quarter = rank & 3
    slot_ref[0:1, :] = row
    slot_ref[1:2, :] = quarter
    loads[1].wait()
    cell = cell_ref[...]
    line = iota((LANE - channels, points), 0)
    extra = jnp.where(line == 0, cell >> 6, 0)
    extra = jnp.where(line == 1, (cell >> 1) & 31, extra)
    extra = jnp.where(line == 2, cell & 1, extra)
    loads[2].wait()
    whole = jnp.concatenate([feats_ref[...], extra.astype(F32).astype(BF16)], axis=0)
    spread = jnp.concatenate([whole * one_hot(quarter == q) for q in range(PACK)], axis=0)
    rows = send_ref.shape[0]
    step = min(256, rows)
    stores = []
    for start in range(0, rows, step):
        pick = one_hot(iota((step, points), 0) + start == row)
        part = slice(start, start + step)
        send_ref[part, :] = mm(pick, spread, NT).astype(BF16)
        store = pltpu.make_async_copy(
            send_ref.at[part], send_out.at[part], out_sems.at[start // step]
        )
        store.start()
        stores.append(store)
    for store in stores:
        store.wait()


def pool_kernel(
    place_ref, got_ref, coarse_ref, grid_ref, even_ref, odd_ref, total_ref,
    *, channels, fields, count,
):
    rows = got_ref.shape[0]
    pairs = grid_ref.shape[0]
    lane = iota((8, LANE), 1)
    weigh = jnp.where(lane == channels, 32.0, jnp.where(lane == channels + 1, 1.0, 0.0))
    weigh = weigh.astype(BF16)
    step = 256
    places, parts = [], []
    for q in range(PACK):
        block = got_ref[:, q * LANE : (q + 1) * LANE]
        places.append(mm(weigh, block, NT)[0:1].astype(jnp.int32))
        odd = block * block[:, channels + 2 : channels + 3]
        parts.append(jnp.concatenate([block - odd, odd], axis=1))
    place = jnp.concatenate(places, axis=1)
    both = jnp.concatenate(parts, axis=0)
    for start in range(0, pairs, step):
        pick = one_hot(iota((step, PACK * rows), 0) + start == place)
        total_ref[start : start + step, :] = mm(pick, both)
    at = 0
    for ref, (ext_x, ext_y, half, rim) in zip((total_ref, coarse_ref), fields):
        field = as_field(ref[...], ext_x, ext_y, half)
        packed = ref is total_ref
        first = field[:rim] * inside(place_ref[0], 0)
        last = field[ext_x - rim :] * inside(place_ref[0], count - 1)
        at = put_faces(place_ref[0], (even_ref, odd_ref), at, first, last, packed)
    grid_ref[...] = total_ref[...].astype(BF16)


def as_field(rows, ext_x, ext_y, half):
    return rows.astype(F32).reshape(ext_x, ext_y, half, rows.shape[1])


def packed_size(size):
    return size - size // 64 * 16


def pack_rows(rows):
    quarter = rows.shape[0] // 64 * 16
    third = LANE // 4
    spare = iota((quarter, LANE), 1) >= 3 * third
    halves = []
    for lanes in (slice(0, LANE), slice(LANE, WIDE)):
        moved = rows[3 * quarter : 4 * quarter, lanes]
        parts = [
            jnp.where(
                spare,
                pltpu.roll(moved, (3 - k) * third, 1),
                rows[k * quarter : (k + 1) * quarter, lanes],
            )
            for k in range(3)
        ]
        if rows.shape[0] > 4 * quarter:
            parts.append(rows[4 * quarter :, lanes])
        halves.append(jnp.concatenate(parts, axis=0))
    return jnp.concatenate(halves, axis=1)


def unpack_rows(rows, size):
    quarter = size // 64 * 16
    third = LANE // 4
    lane = iota((quarter, LANE), 1)
    halves = []
    for lanes in (slice(0, LANE), slice(LANE, WIDE)):
        parts = [rows[k * quarter : (k + 1) * quarter, lanes] for k in range(3)]
        back = [pltpu.roll(part, (k + 1) * third, 1) for k, part in enumerate(parts)]
        moved = jnp.where(lane < third, back[0], jnp.where(lane < 2 * third, back[1], back[2]))
        parts.append(moved)
        if size > 4 * quarter:
            parts.append(rows[3 * quarter :, lanes])
        halves.append(jnp.concatenate(parts, axis=0))
    return jnp.concatenate(halves, axis=1)


def faces_of(place, refs, start, shape, packed):
    count_x, count_y, half = shape
    size = count_x * count_y * half
    length = packed_size(size) if packed else size
    both = by_parity(place, *[ref[start : start + length, :].astype(F32) for ref in refs])
    if packed:
        both = [unpack_rows(rows, size) for rows in both]
    return [as_field(rows, count_x, count_y, half) for rows in both], start + length


def put_faces(place, refs, at, first, last, packed):
    for ref, field in zip(refs, by_parity(place, first, last)):
        rows = rows_of(field)
        rows = pack_rows(rows) if packed else rows
        ref[at : at + rows.shape[0], :] = rows.astype(BF16)
    return at + rows.shape[0]


def inside(place, end):
    return jnp.where(place == end, 0.0, 1.0)


def by_parity(place, one, other):
    swap = place % 2 == 1
    return jnp.where(swap, one, other), jnp.where(swap, other, one)


def edge_kernel(
    place_ref, grid_ref, coarse_ref, x_even, x_odd, even_ref, odd_ref, *, fields, count
):
    start, at = 0, 0
    for ref, (ext_x, ext_y, half, rim) in zip((grid_ref, coarse_ref), fields):
        packed = ref is grid_ref
        (low, high), start = faces_of(
            place_ref[0], (x_even, x_odd), start, (rim, ext_y, half), packed
        )
        field = jnp.concatenate([low, as_field(ref[...], ext_x, ext_y, half), high], axis=0)
        first = field[:, :rim] * inside(place_ref[1], 0)
        last = field[:, ext_y - rim :] * inside(place_ref[1], count - 1)
        at = put_faces(place_ref[1], (even_ref, odd_ref), at, first, last, packed)


def prepare_kernel(
    conv_ref, down_ref, cot_ref, occ_ref,
    conv_out, back_out, down_out, down_back_out, coarse_out, *, ext_y
):
    channels = conv_ref.shape[1]
    conv_out[...] = jnp.zeros(conv_out.shape, BF16)
    back_out[...] = jnp.zeros(back_out.shape, BF16)
    down_out[...] = jnp.zeros(down_out.shape, BF16)
    down_back_out[...] = jnp.zeros(down_back_out.shape, BF16)
    four = 4 * channels
    a, b = slice(0, channels), slice(LANE, LANE + channels)
    for j in range(9):
        for k in range(3):
            weight = conv_ref[3 * j + k]
            turned = weight.astype(F32).T.astype(BF16)
            for z in range(2):
                at, side = j * four + (k + z) * channels, (a, b)[z]
                conv_out[at : at + channels, side] = weight
                at = (8 - j) * four + (2 - k + z) * channels
                back_out[at : at + channels, side] = turned
    for j in range(8):
        part = slice(j * LANE, j * LANE + channels)
        down_out[part, :] = down_ref[j]
        down_back_out[:, part] = down_ref[j].astype(F32).T.astype(BF16)
    columns, depth = occ_ref.shape
    rows, coarse = cot_ref.shape
    half = depth // 2
    rest = WIDE - coarse
    occ = occ_ref[...].astype(F32).astype(BF16)
    row = iota((rows, columns), 0)
    place, column = row // half, iota((rows, columns), 1)
    base = place // (ext_y // 2) * 2 * ext_y + place % (ext_y // 2) * 2
    level = iota((rows, depth), 1) // 2 == iota((rows, depth), 0) % half
    total = jnp.zeros((rows, rest), F32)
    for j in range(4):
        pick = one_hot(base + j // 2 * ext_y + j % 2 == column)
        found = jnp.where(level, mm(pick, occ), 0.0).astype(BF16)
        spot = iota((depth, rest), 1) == 2 * j + iota((depth, rest), 0) % 2
        total = total + mm(found, one_hot(spot))
    coarse_out[:, :coarse] = cot_ref[...]
    coarse_out[:, coarse:] = total.astype(BF16)


def fill_four(pad_ref, four_ref, channels):
    ext_x, ext_y, half, wide = pad_ref.shape
    columns = ext_x * ext_y
    level = iota((columns, half, LANE), 1)
    even = pad_ref[:, :, :, :LANE].reshape(columns, half, LANE)
    odd = pad_ref[:, :, :, LANE:].reshape(columns, half, LANE)
    after = jnp.where(level == half - 1, 0.0, pltpu.roll(even, half - 1, 1))
    before = jnp.where(level == 0, 0.0, pltpu.roll(odd, 1, 1))
    parts = [part[:, :, :channels] for part in (before, even, odd, after)]
    four = jnp.concatenate(parts, axis=2)
    four_ref[...] = four.reshape(ext_x, ext_y, half, 4 * channels)


def windows(ref, first_x, count_x, first_y, count_y):
    parts = []
    for j in range(9):
        x, y = first_x + j // 3, first_y + j % 3
        part = ref[x : x + count_x, y : y + count_y]
        parts.append(part.reshape(count_x * count_y * part.shape[2], part.shape[3]).astype(BF16))
    return parts


def convolve(four_ref, weight_ref, boxes):
    weight = weight_ref[...]
    return [mm(jnp.concatenate(windows(four_ref, *box), axis=1), weight) for box in boxes]


def logistic(values):
    return 1.0 / (1.0 + jnp.exp(-values))


def silu_and_slope(pre):
    sigma = logistic(pre)
    return (pre * sigma).astype(BF16), sigma * (1.0 + pre * (1.0 - sigma))


def rows_of(field):
    return field.reshape(field.shape[0] * field.shape[1] * field.shape[2], field.shape[3])


def child_masks(coarse_s, mask_s, coarse):
    count_x, count_y, half, wide = coarse_s.shape
    given = rows_of(coarse_s[:, :, :, LANE:]).astype(BF16)
    spot = iota((LANE, 4 * wide), 0) == coarse - LANE + iota((LANE, 4 * wide), 1) // LANE
    masks = mm(given, one_hot(spot))
    largest = None
    for j in range(4):
        mask = masks[:, j * wide : (j + 1) * wide]
        mask_s[:, j // 2, :, j % 2] = mask.reshape(count_x, count_y, half, wide)
        largest = mask if largest is None else jnp.maximum(largest, mask)
    largest = jnp.maximum(largest[:, :LANE], largest[:, LANE:])
    largest = jnp.concatenate([largest, largest[:, : coarse - LANE]], axis=1)
    return largest.reshape(count_x, count_y, half, coarse)


def coarse_pass(
    fine_s, slope_s, delta_s, coarse_s, coarse_mask, down_ref, down_back_ref, first, count
):
    coarse = down_ref.shape[1]
    columns = slice(first, first + count)
    pieces = [rows_of(fine_s[:, j // 2, columns, j % 2]).astype(BF16) for j in range(4)]
    pre = mm(jnp.concatenate(pieces, axis=1), down_ref[...])
    sigma = logistic(pre)
    shape = (coarse_s.shape[0], count, coarse_s.shape[2], coarse)
    mask = rows_of(coarse_mask[:, columns])
    features = (pre * sigma * mask).reshape(shape)
    slope = sigma * (1.0 + pre * (1.0 - sigma))
    delta = (rows_of(coarse_s[:, columns, :, :coarse]) * mask * slope).astype(BF16)
    back = mm(delta, down_back_ref[...])
    for j in range(4):
        part = back[:, j * WIDE : (j + 1) * WIDE].reshape(*shape[:3], WIDE)
        delta_s[:, j // 2, :, j % 2] = part * slope_s[:, j // 2, columns, j % 2]
    return features, delta.astype(F32).reshape(shape)


def as_columns(ref):
    count_x, _, count_y, _, half, wide = ref.shape
    return ref[...].reshape(2 * count_x, 2 * count_y, half, wide)


def middle_kernel(
    place_ref, grid_ref, coarse_ref, x_even, x_odd, conv_ref, down_ref, down_back_ref,
    fine_ref, slope_ref, features_ref, delta_ref, conv_grad_ref, down_grad_ref,
    pad_ref, four_ref, coarse_s, mask_s, fine_s, slope_s, delta_s, *, channels, rim,
):
    ext_x, ext_y, half = pad_ref.shape[0], pad_ref.shape[1], pad_ref.shape[2]
    refs = (x_even, x_odd)
    (low, high), start = faces_of(place_ref[0], refs, 0, (rim, ext_y, half), True)
    pad_ref[:rim], pad_ref[ext_x - rim :] = low, high
    pad_ref[rim : ext_x - rim] = as_field(grid_ref[...], ext_x - 2 * rim, ext_y, half)
    fill_four(pad_ref, four_ref, channels)
    coarse_x, coarse_y = coarse_s.shape[0], coarse_s.shape[1]
    coarse = down_ref.shape[1]
    (low, high), _ = faces_of(place_ref[0], refs, start, (1, coarse_y, half), False)
    coarse_s[:1], coarse_s[coarse_x - 1 :] = low, high
    coarse_s[1 : coarse_x - 1] = as_field(coarse_ref[...], coarse_x - 2, coarse_y, half)
    coarse_mask = child_masks(coarse_s, mask_s, coarse)
    count, inside_y = 4, ext_y - 2
    for first in range(0, ext_x - 2, count):
        (pre,) = convolve(four_ref, conv_ref, [(first, count, 0, inside_y)])
        silu, slope = silu_and_slope(pre)
        silu = as_field(silu, count, inside_y, half)
        slope = slope.reshape(silu.shape)
        part = slice(first // 2, (first + count) // 2)
        shape = (count // 2, 2, half, WIDE)
        for y in range(1, ext_y - 1):
            mask = mask_s[part, :, y // 2, y % 2]
            fine_s[part, :, y // 2, y % 2] = silu[:, y - 1].reshape(shape) * mask
            slope_s[part, :, y // 2, y % 2] = slope[:, y - 1].reshape(shape) * mask
    size = 2 * coarse_x * half
    for at, y in enumerate((1, ext_y - 2)):
        rows = slice(at * size, (at + 1) * size)
        fine_ref[rows, :] = fine_s[:, :, y // 2, y % 2].reshape(size, WIDE).astype(BF16)
        slope_ref[rows, :] = slope_s[:, :, y // 2, y % 2].reshape(size, WIDE)
    middle = coarse_y - 2
    features, delta_coarse = coarse_pass(
        fine_s, slope_s, delta_s, coarse_s, coarse_mask, down_ref, down_back_ref, 1, middle
    )
    features_ref[...] = rows_of(features[1 : coarse_x - 1]).astype(BF16)
    delta = as_columns(delta_s)
    delta_ref[...] = rows_of(delta[1 : 2 * coarse_x - 1]).astype(BF16)
    turned = rows_of(delta[2 : 2 * coarse_x - 2]).T.astype(BF16)
    box = (rim - 1, 2 * (coarse_x - 2), 1, 2 * middle)
    for j, part in enumerate(windows(four_ref, *box)):
        conv_grad_ref[j * LANE : (j + 1) * LANE, :] = fold(mm(turned, part), channels)
    ours = rows_of(delta_coarse[1 : coarse_x - 1]).astype(BF16)
    for j in range(4):
        piece = fine_s[1 : coarse_x - 1, j // 2, 1 : 1 + middle, j % 2]
        down_grad_ref[j * WIDE : (j + 1) * WIDE, :] = mm(rows_of(piece).astype(BF16), ours, TN)


def fold(grad, channels):
    return grad[:LANE, : 3 * channels] + grad[LANE:, channels:]


def strip_kernel(
    place_ref, grid_ref, coarse_ref, x_even, x_odd, y_even, y_odd, fine_ref, slope_ref,
    mid_features_ref, mid_delta_ref, conv_grad_ref, down_grad_ref, conv_ref, down_ref,
    down_back_ref, features_ref, delta_ref, keep_ref, give_ref,
    pad_ref, four_ref, coarse_s, mask_s, fine_s, slope_s, delta_s, sum_s,
    *, channels, fields, scale,
):
    (ext_x, ext_y, half, rim), (coarse_x, coarse_y, _, _) = fields
    long = ext_x + 2 * rim
    x_refs, y_refs = (x_even, x_odd), (y_even, y_odd)
    (low, high), x_start = faces_of(place_ref[0], x_refs, 0, (rim, ext_y, half), True)
    parts = (low, as_field(grid_ref[...], ext_x, ext_y, half), high)
    y_faces, y_start = faces_of(place_ref[1], y_refs, 0, (long, rim, half), True)
    for side, y_face in enumerate(y_faces):
        ours, here, there = ((0, rim, 0), (ext_y - rim, 0, rim))[side]
        at = side * long
        pad_ref[at : at + long, there : there + rim] = y_face
        for part in parts:
            count = part.shape[0]
            pad_ref[at : at + count, here : here + rim] = part[:, ours : ours + rim]
            at += count
    fill_four(pad_ref, four_ref, channels)
    (low, high), _ = faces_of(place_ref[0], x_refs, x_start, (1, coarse_y, half), False)
    parts = (low, as_field(coarse_ref[...], coarse_x, coarse_y, half), high)
    shape = (coarse_x + 2, 1, half)
    y_faces, _ = faces_of(place_ref[1], y_refs, y_start, shape, False)
    for side, y_face in enumerate(y_faces):
        y = side * (coarse_y - 1)
        theirs = 3 * side
        coarse_s[:, theirs : theirs + 1] = y_face
        at = 0
        for part in parts:
            count = part.shape[0]
            coarse_s[at : at + count, 1 + side : 2 + side] = part[:, y : y + 1]
            at += count
    coarse = down_ref.shape[1]
    coarse_mask = child_masks(coarse_s, mask_s, coarse)
    out_x, strip = ext_x + 4, 3
    boxes = [(0, out_x, 0, strip), (long, out_x, 1, strip)]
    shape = (out_x, strip, half, WIDE)
    ends = [silu_and_slope(pre) for pre in convolve(four_ref, conv_ref, boxes)]
    ends = [(silu.astype(F32).reshape(shape), slope.reshape(shape)) for silu, slope in ends]
    shape = (coarse_x + 2, 2, half, WIDE)
    size = out_x * half
    for y in range(8):
        if y in (3, 4):
            rows = slice((y - 3) * size, (y - 2) * size)
            fine_s[:, :, y // 2, y % 2] = fine_ref[rows, :].astype(F32).reshape(shape)
            slope_s[:, :, y // 2, y % 2] = slope_ref[rows, :].reshape(shape)
        else:
            side, at = y // 5, y % 5
            mask = mask_s[:, :, y // 2, y % 2]
            silu, slope = ends[side]
            fine_s[:, :, y // 2, y % 2] = silu[:, at].reshape(shape) * mask
            slope_s[:, :, y // 2, y % 2] = slope[:, at].reshape(shape) * mask
    features, delta_coarse = coarse_pass(
        fine_s, slope_s, delta_s, coarse_s, coarse_mask, down_ref, down_back_ref, 0, 4
    )
    features = features[1 : 1 + coarse_x]
    mid = as_field(mid_features_ref[...], coarse_x, coarse_y - 2, half)
    features = jnp.concatenate([features[:, 1:2], mid, features[:, 2:3]], axis=1)
    features_ref[...] = rows_of(features).astype(BF16)
    delta = as_columns(delta_s)
    mid = as_field(mid_delta_ref[...], ext_x + 2, ext_y - 4, half)
    near = delta[1 : out_x - 1]
    near = jnp.concatenate([near[:, 1:4], mid, near[:, 4:7]], axis=1)
    delta_ref[...] = rows_of(near).astype(BF16)
    ours = delta[2 : 2 + ext_x]
    turned = jnp.concatenate([rows_of(ours[:, 2:4]), rows_of(ours[:, 4:6])], axis=0)
    turned = turned.T.astype(BF16)
    low = windows(four_ref, rim - 1, ext_x, rim - 1, 2)
    high = windows(four_ref, long + rim - 1, ext_x, 0, 2)
    three = 3 * channels
    for j in range(9):
        grad = fold(mm(turned, jnp.concatenate([low[j], high[j]], axis=0)), channels)
        grad = grad + conv_grad_ref[j * LANE : (j + 1) * LANE, :]
        sum_s[j * three : (j + 1) * three, :] = (grad * scale).astype(BF16).T
    ours = rows_of(delta_coarse[1 : 1 + coarse_x, 1:3]).astype(BF16)
    base = 27 * channels
    for j in range(4):
        piece = rows_of(fine_s[1 : 1 + coarse_x, j // 2, 1:3, j % 2]).astype(BF16)
        grad = (mm(piece, ours, TN) + down_grad_ref[j * WIDE : (j + 1) * WIDE, :]) * scale
        grad = grad.astype(BF16)
        first, second = grad[:channels], grad[LANE : LANE + channels]
        start = base + 2 * j * channels
        sum_s[start : start + channels, :] = first[:, :LANE]
        sum_s[start + channels : start + 2 * channels, :] = second[:, :LANE]
        start = base + (8 + j) * channels
        sum_s[start : start + channels, :] = jnp.concatenate(
            [first[:, LANE:], second[:, LANE:]], axis=1
        )
    end = base + 12 * channels
    sum_s[end:, :] = jnp.zeros((sum_s.shape[0] - end, LANE), BF16)
    size = keep_ref.shape[0]
    core = place_ref[0] % 2
    keep_ref[...] = sum_s[pl.ds(pl.multiple_of(core * size, size), size), :]
    give_ref[...] = sum_s[pl.ds(pl.multiple_of((1 - core) * size, size), size), :]


def pair_kernel(keep_ref, other_ref, out_ref):
    out_ref[...] = (keep_ref[...].astype(F32) + other_ref[...].astype(F32)).astype(BF16)


def input_grad_kernel(delta_ref, conv_ref, got_ref, back_ref, pad_ref, four_ref, grad_s, *, channels):
    ext_x, ext_y, half = pad_ref.shape[0] - 2, pad_ref.shape[1] - 2, pad_ref.shape[2]
    pad_ref[...] = as_field(delta_ref[...], ext_x + 2, ext_y + 2, half)
    fill_four(pad_ref, four_ref, channels)
    count = 4
    for first in range(0, ext_x, count):
        rows = slice(first * ext_y * half, (first + count) * ext_y * half)
        (grad,) = convolve(four_ref, conv_ref, [(first, count, 0, ext_y)])
        grad_s[rows, :] = grad.astype(BF16)
    grad = grad_s[...]
    pairs = grad.shape[0]
    rows = got_ref.shape[0]
    step = min(256, rows)
    for start in range(0, rows, step):
        found = []
        for q in range(PACK):
            info = got_ref[start : start + step, q * LANE : (q + 1) * LANE].astype(F32)
            place = info[:, channels : channels + 1] * 32.0 + info[:, channels + 1 : channels + 2]
            pick = one_hot(iota((step, pairs), 1) == place.astype(jnp.int32))
            both = mm(pick, grad)
            odd = info[:, channels + 2 : channels + 3] > 0.5
            found.append(jnp.where(odd, both[:, LANE:], both[:, :LANE])[:, :channels])
        back_ref[start : start + step, :] = jnp.concatenate(found, axis=1).astype(BF16)


def join_kernel(terms_ref, back_ref, out_ref, *, block, per_axis):
    total = jnp.sum(terms_ref[...].astype(F32), axis=0)
    rows, wide = back_ref.shape
    out_ref[:, :wide] = back_ref[...]
    lines = total.shape[0] // 2
    halves = []
    for h in range(2):
        parts = [total[h * lines + k : h * lines + k + block] for k in range(0, lines, block)]
        half = jnp.concatenate(parts, axis=1)
        halves.append(jnp.concatenate([half] * per_axis, axis=0).astype(BF16))
    step = block * per_axis
    for g in range(rows // step):
        out_ref[g * step : (g + 1) * step, wide:] = halves[g % 2]


def collect_kernel(back_ref, slot_ref, out_ref):
    channels, points = out_ref.shape
    rows = back_ref.shape[0]
    back = back_ref[:, : PACK * channels]
    step = min(512, points)
    for start in range(0, points, step):
        row = slot_ref[0:1, start : start + step]
        quarter = slot_ref[1:2, start : start + step]
        pick = one_hot(iota((rows, step), 0) == row)
        found = mm(back, pick, TN)
        total = jnp.zeros((channels, step), F32)
        for q in range(PACK):
            total = jnp.where(quarter == q, found[q * channels : (q + 1) * channels], total)
        out_ref[:, start : start + step] = total.astype(BF16)


def unpack_kernel(place_ref, mine_ref, theirs_ref, conv_ref, down_ref, all_s, *, block, per_axis):
    channels = conv_ref.shape[1]
    count = all_s.shape[2] // 2
    skip = mine_ref.shape[1] - theirs_ref.shape[1]
    swap = place_ref[0] % 2 == 1
    step = block * per_axis
    for g in range(mine_ref.shape[0] // step):
        rows = slice(g * step, (g + 1) * step)
        chips = slice(g // 2 * per_axis, (g // 2 + 1) * per_axis)
        for k in range(count):
            mine = mine_ref[rows, skip + k * LANE : skip + (k + 1) * LANE].astype(F32)
            theirs = theirs_ref[rows, k * LANE : (k + 1) * LANE].astype(F32)
            shape = (per_axis, block, LANE)
            all_s[g % 2, chips, k] = jnp.where(swap, theirs, mine).reshape(shape)
            all_s[g % 2, chips, count + k] = jnp.where(swap, mine, theirs).reshape(shape)
    whole = all_s[...].reshape(mine_ref.shape[0] // block * 2 * count * block, LANE)
    base = 27 * channels
    for j in range(27):
        conv_ref[j] = whole[j * channels : (j + 1) * channels, :channels]
    rest = down_ref.shape[2] - LANE
    for j in range(8):
        start = base + j * channels
        down_ref[j, :, :LANE] = whole[start : start + channels]
        start = base + (8 + j // 2) * channels
        tail = whole[start : start + channels]
        down_ref[j, :, LANE:] = tail[:, (j % 2) * rest : (j % 2 + 1) * rest]


def swap_faces(even, odd, axis):
    count = lax.axis_size(axis)
    pairs = [
        [(i, (i + 1) % count) for i in range(start, count, 2)]
        + [((i + 1) % count, i) for i in range(start, count, 2)]
        for start in range(2)
    ]
    odd = lax.ppermute(odd, axis, pairs[1])
    return lax.ppermute(even, axis, pairs[0]), odd


def to_other_core(block):
    return lax.ppermute(block, "gx", [(i, i ^ 1) for i in range(lax.axis_size("gx"))])


def exchange(blocks, **groups):
    return lax.all_to_all(blocks, AXES, split_axis=0, concat_axis=0, tiled=True, **groups)


def shards(point_feats, point_owner, point_cell, occupancy, w_conv, w_down, cotangent):
    points, channels = point_feats.shape
    count_x, count_y = lax.axis_size("gx"), lax.axis_size("gy")
    devices = count_x * count_y
    cap = 32
    block = cap // PACK
    ext_x, ext_y, ext_z = occupancy.shape
    half = ext_z // 2
    pairs = ext_x * ext_y * half
    coarse = w_down.shape[2]
    coarse_x, coarse_y = ext_x // 2, ext_y // 2
    coarse_rows = coarse_x * coarse_y * half
    slot_rows = devices * block
    scale = 1.0 / math.sqrt(float(ext_x * ext_y * ext_z * devices))
    four = 4 * channels
    conv_flops = 2 * pairs * 9 * four * WIDE
    pick_flops = 2 * pairs * slot_rows * PACK * WIDE
    rim = 3
    fields = ((ext_x, ext_y, half, rim), (coarse_x, coarse_y, half, 1))

    send, slot = call(
        functools.partial(dispatch_kernel, devices=devices, cap=cap),
        (struct((slot_rows, PACK * LANE), BF16), struct((2, points), jnp.int32)),
        (point_feats.T, point_owner.reshape(1, points), point_cell.reshape(1, points)),
        "dispatch",
        scratch=[
            pltpu.VMEM((channels, points), BF16),
            pltpu.VMEM((1, points), jnp.int32),
            pltpu.VMEM((1, points), jnp.int32),
            pltpu.VMEM((slot_rows, PACK * LANE), BF16),
            pltpu.SemaphoreType.DMA((3,)),
            pltpu.SemaphoreType.DMA((-(-slot_rows // 256),)),
        ],
        flops=2 * points * slot_rows * PACK * LANE,
        far=(0, 1, 2),
        far_outs=(0,),
        grant=56,
    )
    got = exchange(send.reshape(devices, block, PACK * LANE)).reshape(slot_rows, PACK * LANE)
    conv_blocks, back_blocks, down_blocks, down_back, given = call(
        functools.partial(prepare_kernel, ext_y=ext_y),
        (
            struct((9 * four, WIDE), BF16),
            struct((9 * four, WIDE), BF16),
            struct((4 * WIDE, coarse), BF16),
            struct((coarse, 4 * WIDE), BF16),
            struct((coarse_rows, WIDE), BF16),
        ),
        (w_conv, w_down, cotangent.reshape(coarse_rows, coarse),
         occupancy.reshape(ext_x * ext_y, ext_z)),
        "prepare",
        flops=1000000000,
    )
    x_rows = packed_size(rim * ext_y * half) + coarse_y * half
    y_rows = packed_size(rim * (ext_x + 2 * rim) * half) + (coarse_x + 2) * half
    place = jnp.stack([lax.axis_index("gx"), lax.axis_index("gy")]).astype(jnp.int32)
    grid, x_even, x_odd = call(
        functools.partial(pool_kernel, channels=channels, fields=fields, count=count_x),
        tuple(struct((n, WIDE), BF16) for n in (pairs, x_rows, x_rows)),
        (place, got, given),
        "pool",
        scratch=[pltpu.VMEM((pairs, WIDE), F32)],
        flops=pick_flops,
    )
    x_faces = swap_faces(x_even, x_odd, "gx")
    y_even, y_odd = call(
        functools.partial(edge_kernel, fields=fields, count=count_y),
        tuple(struct((n, WIDE), BF16) for n in (y_rows, y_rows)),
        (place, grid, given, *x_faces),
        "edge",
    )
    y_faces = swap_faces(y_even, y_odd, "gy")
    long = ext_x + 2 * rim
    near = (ext_x + 2, ext_y + 2, half)
    near_rows = near[0] * near[1] * half
    edge_rows = 2 * (ext_x + 4) * half

    def split(columns):
        return pltpu.VMEM((coarse_x + 2, 2, columns, 2, half, WIDE), F32)

    middle = call(
        functools.partial(middle_kernel, channels=channels, rim=rim),
        (
            struct((edge_rows, WIDE), BF16),
            struct((edge_rows, WIDE), F32),
            struct((coarse_x * (coarse_y - 2) * half, coarse), BF16),
            struct(((ext_x + 2) * (ext_y - 4) * half, WIDE), BF16),
            struct((9 * LANE, 3 * channels), F32),
            struct((4 * WIDE, coarse), F32),
        ),
        (place, grid, given, *x_faces, conv_blocks, down_blocks, down_back),
        "middle",
        scratch=[
            pltpu.VMEM((long, ext_y, half, WIDE), F32),
            pltpu.VMEM((long, ext_y, half, four), F32),
            pltpu.VMEM((coarse_x + 2, coarse_y, half, WIDE), F32),
            split(coarse_y),
            split(coarse_y),
            split(coarse_y),
            split(coarse_y - 2),
        ],
        flops=3 * conv_flops,
    )
    used = 39 * channels
    chunk = -(-used // (32 * devices)) * 32
    half_rows = devices // 2 * chunk
    features, delta, keep, give = call(
        functools.partial(strip_kernel, channels=channels, fields=fields, scale=scale),
        (
            struct((coarse_rows, coarse), BF16),
            struct((near_rows, WIDE), BF16),
            struct((half_rows, LANE), BF16),
            struct((half_rows, LANE), BF16),
        ),
        (place, grid, given, *x_faces, *y_faces, *middle, conv_blocks, down_blocks, down_back),
        "strip",
        scratch=[
            pltpu.VMEM((2 * long, 2 * rim, half, WIDE), F32),
            pltpu.VMEM((2 * long, 2 * rim, half, four), F32),
            pltpu.VMEM((coarse_x + 2, 4, half, WIDE), F32),
            split(4),
            split(4),
            split(4),
            split(4),
            pltpu.VMEM((2 * half_rows, LANE), BF16),
        ],
        flops=conv_flops,
        megabytes=8,
    )
    both = call(
        pair_kernel, struct((half_rows, LANE), BF16), (keep, to_other_core(give)), "pair"
    )
    terms = exchange(
        both.reshape(devices // 2, chunk, LANE),
        axis_index_groups=[
            [x * count_y + y for x in range(core, count_x, 2) for y in range(count_y)]
            for core in range(2)
        ],
    )
    back = call(
        functools.partial(input_grad_kernel, channels=channels),
        struct((slot_rows, PACK * channels), BF16),
        (delta, back_blocks, got),
        "input_grad",
        scratch=[
            pltpu.VMEM((*near, WIDE), F32),
            pltpu.VMEM((*near, four), F32),
            pltpu.VMEM((pairs, WIDE), BF16),
        ],
        flops=conv_flops + pick_flops,
        megabytes=8,
    )
    half_lanes = chunk // 2 // block * LANE
    joined_lanes = PACK * channels + half_lanes
    joined = call(
        functools.partial(join_kernel, block=block, per_axis=count_y),
        struct((slot_rows, joined_lanes), BF16),
        (terms, back),
        "join",
        flops=devices * chunk * LANE,
    )
    returned = exchange(joined.reshape(devices, block, joined_lanes)).reshape(
        slot_rows, joined_lanes
    )
    theirs = to_other_core(returned[:, PACK * channels :])
    grad_points = call(
        collect_kernel,
        struct((channels, points), BF16),
        (returned, slot),
        "collect",
        flops=2 * points * slot_rows * PACK * LANE,
    ).T
    grad_conv, grad_down = call(
        functools.partial(unpack_kernel, block=block, per_axis=count_y),
        (struct(w_conv.shape, F32), struct(w_down.shape, F32)),
        (place, returned, theirs),
        "unpack",
        scratch=[pltpu.VMEM((2, devices // 2, chunk // block, block, LANE), F32)],
    )
    return (
        features.reshape(coarse_x, coarse_y, half, coarse),
        grad_points,
        grad_conv,
        grad_down,
    )


def solution(mesh):
    placed = (
        P(("gx", "gy"), None),
        P(("gx", "gy"), None),
        P(("gx", "gy")),
        P("gx", "gy", None),
        P(),
        P(),
        P("gx", "gy", None, None),
    )
    return jax.shard_map(
        shards,
        mesh=mesh,
        in_specs=placed,
        out_specs=(P("gx", "gy", None, None), P(("gx", "gy"), None), P(), P()),
        check_vma=False,
    )
```

```python
import functools
import math

import jax
import jax.numpy as jnp
from jax import lax
from jax.experimental import pallas as pl
from jax.experimental.pallas import tpu as pltpu
from jax.sharding import PartitionSpec as P

F32 = jnp.float32
BF16 = jnp.bfloat16
LANE = 128
WIDE = 256
PACK = 4
AXES = ("gx", "gy")
NT = (((1,), (1,)), ((), ()))
NN = (((1,), (0,)), ((), ()))
TN = (((0,), (0,)), ((), ()))


def iota(shape, dim):
    return lax.broadcasted_iota(jnp.int32, shape, dim)


def mm(a, b, dims=NN):
    return lax.dot_general(a, b, dims, preferred_element_type=F32)


def one_hot(mask):
    return jnp.where(mask, 1.0, 0.0).astype(BF16)


def call(
    kernel, outs, args, name, scratch=(), flops=0, megabytes=4, far=(), far_outs=(), grant=24
):
    def spec(index, array, group):
        if index in group:
            return pl.BlockSpec(memory_space=pl.ANY)
        scalars = array.ndim == 1
        return pl.BlockSpec(memory_space=pltpu.SMEM if scalars else pltpu.VMEM)

    single = not isinstance(outs, tuple)
    out_specs = [spec(i, out, far_outs) for i, out in enumerate((outs,) if single else outs)]
    return pl.pallas_call(
        kernel,
        out_shape=outs,
        in_specs=[spec(i, arg, far) for i, arg in enumerate(args)],
        out_specs=out_specs[0] if single else tuple(out_specs),
        scratch_shapes=list(scratch),
        compiler_params=pltpu.CompilerParams(vmem_limit_bytes=grant * 1024 * 1024),
        cost_estimate=pl.CostEstimate(
            flops=flops, bytes_accessed=megabytes * 1000000, transcendentals=0
        ),
        name=name,
    )(*args)


def struct(shape, dtype):
    return jax.ShapeDtypeStruct(shape, dtype)


def dispatch_kernel(
    feats_in, owner_in, cell_in, send_out, slot_ref,
    feats_ref, owner_ref, cell_ref, send_ref, in_sems, out_sems, *, devices, cap,
):
    loads = [
        pltpu.make_async_copy(source, target, in_sems.at[i])
        for i, (source, target) in enumerate(
            ((owner_in, owner_ref), (cell_in, cell_ref), (feats_in, feats_ref))
        )
    ]
    for load in loads:
        load.start()
    channels, points = feats_ref.shape
    loads[0].wait()
    owner = owner_ref[...]
    hot = iota((devices, points), 0) == owner
    block = min(256, points)
    upper = one_hot(iota((block, block), 0) < iota((block, block), 1))
    carry = jnp.zeros((devices, 1), F32)
    ranks = []
    for start in range(0, points, block):
        part = jnp.where(hot[:, start : start + block], 1.0, 0.0)
        before = mm(part.astype(BF16), upper) + carry
        ranks.append(jnp.sum(part * before, axis=0, keepdims=True))
        carry = carry + jnp.sum(part, axis=1, keepdims=True)
    rank = jnp.concatenate(ranks, axis=1).astype(jnp.int32)
    row = owner * (cap // PACK) + (rank >> 2)
    quarter = rank & 3
    slot_ref[0:1, :] = row
    slot_ref[1:2, :] = quarter
    loads[1].wait()
    cell = cell_ref[...]
    line = iota((LANE - channels, points), 0)
    extra = jnp.where(line == 0, cell >> 6, 0)
    extra = jnp.where(line == 1, (cell >> 1) & 31, extra)
    extra = jnp.where(line == 2, cell & 1, extra)
    loads[2].wait()
    whole = jnp.concatenate([feats_ref[...], extra.astype(F32).astype(BF16)], axis=0)
    spread = jnp.concatenate([whole * one_hot(quarter == q) for q in range(PACK)], axis=0)
    rows = send_ref.shape[0]
    step = min(256, rows)
    stores = []
    for start in range(0, rows, step):
        pick = one_hot(iota((step, points), 0) + start == row)
        part = slice(start, start + step)
        send_ref[part, :] = mm(pick, spread, NT).astype(BF16)
        store = pltpu.make_async_copy(
            send_ref.at[part], send_out.at[part], out_sems.at[start // step]
        )
        store.start()
        stores.append(store)
    for store in stores:
        store.wait()


def pool_kernel(
    place_ref, got_ref, coarse_ref, grid_ref, even_ref, odd_ref, total_ref,
    *, channels, fields, count,
):
    rows = got_ref.shape[0]
    pairs = grid_ref.shape[0]
    lane = iota((8, LANE), 1)
    weigh = jnp.where(lane == channels, 32.0, jnp.where(lane == channels + 1, 1.0, 0.0))
    weigh = weigh.astype(BF16)
    step = 256
    places, parts = [], []
    for q in range(PACK):
        block = got_ref[:, q * LANE : (q + 1) * LANE]
        places.append(mm(weigh, block, NT)[0:1].astype(jnp.int32))
        odd = block * block[:, channels + 2 : channels + 3]
        parts.append(jnp.concatenate([block - odd, odd], axis=1))
    place = jnp.concatenate(places, axis=1)
    both = jnp.concatenate(parts, axis=0)
    for start in range(0, pairs, step):
        pick = one_hot(iota((step, PACK * rows), 0) + start == place)
        total_ref[start : start + step, :] = mm(pick, both)
    at = 0
    for ref, (ext_x, ext_y, half, rim) in zip((total_ref, coarse_ref), fields):
        field = as_field(ref[...], ext_x, ext_y, half)
        packed = ref is total_ref
        first = field[:rim] * inside(place_ref[0], 0)
        last = field[ext_x - rim :] * inside(place_ref[0], count - 1)
        at = put_faces(place_ref[0], (even_ref, odd_ref), at, first, last, packed)
    grid_ref[...] = total_ref[...].astype(BF16)


def as_field(rows, ext_x, ext_y, half):
    return rows.astype(F32).reshape(ext_x, ext_y, half, rows.shape[1])


def packed_size(size):
    return size - size // 64 * 16


def pack_rows(rows):
    quarter = rows.shape[0] // 64 * 16
    third = LANE // 4
    spare = iota((quarter, LANE), 1) >= 3 * third
    halves = []
    for lanes in (slice(0, LANE), slice(LANE, WIDE)):
        moved = rows[3 * quarter : 4 * quarter, lanes]
        parts = [
            jnp.where(
                spare,
                pltpu.roll(moved, (3 - k) * third, 1),
                rows[k * quarter : (k + 1) * quarter, lanes],
            )
            for k in range(3)
        ]
        if rows.shape[0] > 4 * quarter:
            parts.append(rows[4 * quarter :, lanes])
        halves.append(jnp.concatenate(parts, axis=0))
    return jnp.concatenate(halves, axis=1)


def unpack_rows(rows, size):
    quarter = size // 64 * 16
    third = LANE // 4
    lane = iota((quarter, LANE), 1)
    halves = []
    for lanes in (slice(0, LANE), slice(LANE, WIDE)):
        parts = [rows[k * quarter : (k + 1) * quarter, lanes] for k in range(3)]
        back = [pltpu.roll(part, (k + 1) * third, 1) for k, part in enumerate(parts)]
        moved = jnp.where(lane < third, back[0], jnp.where(lane < 2 * third, back[1], back[2]))
        parts.append(moved)
        if size > 4 * quarter:
            parts.append(rows[3 * quarter :, lanes])
        halves.append(jnp.concatenate(parts, axis=0))
    return jnp.concatenate(halves, axis=1)


def faces_of(place, refs, start, shape, packed):
    count_x, count_y, half = shape
    size = count_x * count_y * half
    length = packed_size(size) if packed else size
    both = by_parity(place, *[ref[start : start + length, :].astype(F32) for ref in refs])
    if packed:
        both = [unpack_rows(rows, size) for rows in both]
    return [as_field(rows, count_x, count_y, half) for rows in both], start + length


def put_faces(place, refs, at, first, last, packed):
    for ref, field in zip(refs, by_parity(place, first, last)):
        rows = rows_of(field)
        rows = pack_rows(rows) if packed else rows
        ref[at : at + rows.shape[0], :] = rows.astype(BF16)
    return at + rows.shape[0]


def inside(place, end):
    return jnp.where(place == end, 0.0, 1.0)


def by_parity(place, one, other):
    swap = place % 2 == 1
    return jnp.where(swap, one, other), jnp.where(swap, other, one)


def edge_kernel(
    place_ref, grid_ref, coarse_ref, x_even, x_odd, even_ref, odd_ref, *, fields, count
):
    start, at = 0, 0
    for ref, (ext_x, ext_y, half, rim) in zip((grid_ref, coarse_ref), fields):
        packed = ref is grid_ref
        (low, high), start = faces_of(
            place_ref[0], (x_even, x_odd), start, (rim, ext_y, half), packed
        )
        field = jnp.concatenate([low, as_field(ref[...], ext_x, ext_y, half), high], axis=0)
        first = field[:, :rim] * inside(place_ref[1], 0)
        last = field[:, ext_y - rim :] * inside(place_ref[1], count - 1)
        at = put_faces(place_ref[1], (even_ref, odd_ref), at, first, last, packed)


def prepare_kernel(
    conv_ref, down_ref, cot_ref, occ_ref,
    conv_out, back_out, down_out, down_back_out, coarse_out, *, ext_y
):
    channels = conv_ref.shape[1]
    conv_out[...] = jnp.zeros(conv_out.shape, BF16)
    back_out[...] = jnp.zeros(back_out.shape, BF16)
    down_out[...] = jnp.zeros(down_out.shape, BF16)
    down_back_out[...] = jnp.zeros(down_back_out.shape, BF16)
    four = 4 * channels
    a, b = slice(0, channels), slice(LANE, LANE + channels)
    for j in range(9):
        for k in range(3):
            weight = conv_ref[3 * j + k]
            turned = weight.astype(F32).T.astype(BF16)
            for z in range(2):
                at, side = j * four + (k + z) * channels, (a, b)[z]
                conv_out[at : at + channels, side] = weight
                at = (8 - j) * four + (2 - k + z) * channels
                back_out[at : at + channels, side] = turned
    for j in range(8):
        part = slice(j * LANE, j * LANE + channels)
        down_out[part, :] = down_ref[j]
        down_back_out[:, part] = down_ref[j].astype(F32).T.astype(BF16)
    columns, depth = occ_ref.shape
    rows, coarse = cot_ref.shape
    half = depth // 2
    rest = WIDE - coarse
    occ = occ_ref[...].astype(F32).astype(BF16)
    row = iota((rows, columns), 0)
    place, column = row // half, iota((rows, columns), 1)
    base = place // (ext_y // 2) * 2 * ext_y + place % (ext_y // 2) * 2
    level = iota((rows, depth), 1) // 2 == iota((rows, depth), 0) % half
    total = jnp.zeros((rows, rest), F32)
    for j in range(4):
        pick = one_hot(base + j // 2 * ext_y + j % 2 == column)
        found = jnp.where(level, mm(pick, occ), 0.0).astype(BF16)
        spot = iota((depth, rest), 1) == 2 * j + iota((depth, rest), 0) % 2
        total = total + mm(found, one_hot(spot))
    coarse_out[:, :coarse] = cot_ref[...]
    coarse_out[:, coarse:] = total.astype(BF16)


def fill_four(pad_ref, four_ref, channels):
    ext_x, ext_y, half, wide = pad_ref.shape
    columns = ext_x * ext_y
    level = iota((columns, half, LANE), 1)
    even = pad_ref[:, :, :, :LANE].reshape(columns, half, LANE)
    odd = pad_ref[:, :, :, LANE:].reshape(columns, half, LANE)
    after = jnp.where(level == half - 1, 0.0, pltpu.roll(even, half - 1, 1))
    before = jnp.where(level == 0, 0.0, pltpu.roll(odd, 1, 1))
    parts = [part[:, :, :channels] for part in (before, even, odd, after)]
    four = jnp.concatenate(parts, axis=2)
    four_ref[...] = four.reshape(ext_x, ext_y, half, 4 * channels)


def windows(ref, first_x, count_x, first_y, count_y):
    parts = []
    for j in range(9):
        x, y = first_x + j // 3, first_y + j % 3
        part = ref[x : x + count_x, y : y + count_y]
        parts.append(part.reshape(count_x * count_y * part.shape[2], part.shape[3]).astype(BF16))
    return parts


def convolve(four_ref, weight_ref, boxes):
    weight = weight_ref[...]
    return [mm(jnp.concatenate(windows(four_ref, *box), axis=1), weight) for box in boxes]


def logistic(values):
    return 1.0 / (1.0 + jnp.exp(-values))


def silu_and_slope(pre):
    sigma = logistic(pre)
    return (pre * sigma).astype(BF16), sigma * (1.0 + pre * (1.0 - sigma))


def rows_of(field):
    return field.reshape(field.shape[0] * field.shape[1] * field.shape[2], field.shape[3])


def child_masks(coarse_s, mask_s, coarse):
    count_x, count_y, half, wide = coarse_s.shape
    given = rows_of(coarse_s[:, :, :, LANE:]).astype(BF16)
    spot = iota((LANE, 4 * wide), 0) == coarse - LANE + iota((LANE, 4 * wide), 1) // LANE
    masks = mm(given, one_hot(spot))
    largest = None
    for j in range(4):
        mask = masks[:, j * wide : (j + 1) * wide]
        mask_s[:, j // 2, :, j % 2] = mask.reshape(count_x, count_y, half, wide)
        largest = mask if largest is None else jnp.maximum(largest, mask)
    largest = jnp.maximum(largest[:, :LANE], largest[:, LANE:])
    largest = jnp.concatenate([largest, largest[:, : coarse - LANE]], axis=1)
    return largest.reshape(count_x, count_y, half, coarse)


def coarse_pass(
    fine_s, slope_s, delta_s, coarse_s, coarse_mask, down_ref, down_back_ref, first, count
):
    coarse = down_ref.shape[1]
    columns = slice(first, first + count)
    pieces = [rows_of(fine_s[:, j // 2, columns, j % 2]).astype(BF16) for j in range(4)]
    pre = mm(jnp.concatenate(pieces, axis=1), down_ref[...])
    sigma = logistic(pre)
    shape = (coarse_s.shape[0], count, coarse_s.shape[2], coarse)
    mask = rows_of(coarse_mask[:, columns])
    features = (pre * sigma * mask).reshape(shape)
    slope = sigma * (1.0 + pre * (1.0 - sigma))
    delta = (rows_of(coarse_s[:, columns, :, :coarse]) * mask * slope).astype(BF16)
    back = mm(delta, down_back_ref[...])
    for j in range(4):
        part = back[:, j * WIDE : (j + 1) * WIDE].reshape(*shape[:3], WIDE)
        delta_s[:, j // 2, :, j % 2] = part * slope_s[:, j // 2, columns, j % 2]
    return features, delta.astype(F32).reshape(shape)


def as_columns(ref):
    count_x, _, count_y, _, half, wide = ref.shape
    return ref[...].reshape(2 * count_x, 2 * count_y, half, wide)


def middle_kernel(
    place_ref, grid_ref, coarse_ref, x_even, x_odd, conv_ref, down_ref, down_back_ref,
    fine_ref, slope_ref, features_ref, delta_ref, conv_grad_ref, down_grad_ref,
    pad_ref, four_ref, coarse_s, mask_s, fine_s, slope_s, delta_s, *, channels, rim,
):
    ext_x, ext_y, half = pad_ref.shape[0], pad_ref.shape[1], pad_ref.shape[2]
    refs = (x_even, x_odd)
    (low, high), start = faces_of(place_ref[0], refs, 0, (rim, ext_y, half), True)
    pad_ref[:rim], pad_ref[ext_x - rim :] = low, high
    pad_ref[rim : ext_x - rim] = as_field(grid_ref[...], ext_x - 2 * rim, ext_y, half)
    fill_four(pad_ref, four_ref, channels)
    coarse_x, coarse_y = coarse_s.shape[0], coarse_s.shape[1]
    coarse = down_ref.shape[1]
    (low, high), _ = faces_of(place_ref[0], refs, start, (1, coarse_y, half), False)
    coarse_s[:1], coarse_s[coarse_x - 1 :] = low, high
    coarse_s[1 : coarse_x - 1] = as_field(coarse_ref[...], coarse_x - 2, coarse_y, half)
    coarse_mask = child_masks(coarse_s, mask_s, coarse)
    count, inside_y = 2, ext_y - 2
    for first in range(0, ext_x - 2, count):
        (pre,) = convolve(four_ref, conv_ref, [(first, count, 0, inside_y)])
        silu, slope = silu_and_slope(pre)
        silu = as_field(silu, count, inside_y, half)
        slope = slope.reshape(silu.shape)
        part = slice(first // 2, (first + count) // 2)
        shape = (count // 2, 2, half, WIDE)
        for y in range(1, ext_y - 1):
            mask = mask_s[part, :, y // 2, y % 2]
            fine_s[part, :, y // 2, y % 2] = silu[:, y - 1].reshape(shape) * mask
            slope_s[part, :, y // 2, y % 2] = slope[:, y - 1].reshape(shape) * mask
    size = 2 * coarse_x * half
    for at, y in enumerate((1, ext_y - 2)):
        rows = slice(at * size, (at + 1) * size)
        fine_ref[rows, :] = fine_s[:, :, y // 2, y % 2].reshape(size, WIDE).astype(BF16)
        slope_ref[rows, :] = slope_s[:, :, y // 2, y % 2].reshape(size, WIDE)
    middle = coarse_y - 2
    features, delta_coarse = coarse_pass(
        fine_s, slope_s, delta_s, coarse_s, coarse_mask, down_ref, down_back_ref, 1, middle
    )
    features_ref[...] = rows_of(features[1 : coarse_x - 1]).astype(BF16)
    delta = as_columns(delta_s)
    delta_ref[...] = rows_of(delta[1 : 2 * coarse_x - 1]).astype(BF16)
    turned = rows_of(delta[2 : 2 * coarse_x - 2]).T.astype(BF16)
    box = (rim - 1, 2 * (coarse_x - 2), 1, 2 * middle)
    grads = mm(turned, jnp.concatenate(windows(four_ref, *box), axis=1))
    for j in range(9):
        part = grads[:, 4 * j * channels : 4 * (j + 1) * channels]
        conv_grad_ref[j * LANE : (j + 1) * LANE, :] = fold(part, channels)
    ours = rows_of(delta_coarse[1 : coarse_x - 1]).astype(BF16)
    for j in range(4):
        piece = fine_s[1 : coarse_x - 1, j // 2, 1 : 1 + middle, j % 2]
        down_grad_ref[j * WIDE : (j + 1) * WIDE, :] = mm(rows_of(piece).astype(BF16), ours, TN)


def fold(grad, channels):
    return grad[:LANE, : 3 * channels] + grad[LANE:, channels:]


def strip_kernel(
    place_ref, grid_ref, coarse_ref, x_even, x_odd, y_even, y_odd, fine_ref, slope_ref,
    mid_features_ref, mid_delta_ref, conv_grad_ref, down_grad_ref, conv_ref, down_ref,
    down_back_ref, features_ref, delta_ref, keep_ref, give_ref,
    pad_ref, four_ref, coarse_s, mask_s, fine_s, slope_s, delta_s, sum_s,
    *, channels, fields, scale,
):
    (ext_x, ext_y, half, rim), (coarse_x, coarse_y, _, _) = fields
    long = ext_x + 2 * rim
    x_refs, y_refs = (x_even, x_odd), (y_even, y_odd)
    (low, high), x_start = faces_of(place_ref[0], x_refs, 0, (rim, ext_y, half), True)
    parts = (low, as_field(grid_ref[...], ext_x, ext_y, half), high)
    y_faces, y_start = faces_of(place_ref[1], y_refs, 0, (long, rim, half), True)
    for side, y_face in enumerate(y_faces):
        ours, here, there = ((0, rim, 0), (ext_y - rim, 0, rim))[side]
        at = side * long
        pad_ref[at : at + long, there : there + rim] = y_face
        for part in parts:
            count = part.shape[0]
            pad_ref[at : at + count, here : here + rim] = part[:, ours : ours + rim]
            at += count
    fill_four(pad_ref, four_ref, channels)
    (low, high), _ = faces_of(place_ref[0], x_refs, x_start, (1, coarse_y, half), False)
    parts = (low, as_field(coarse_ref[...], coarse_x, coarse_y, half), high)
    shape = (coarse_x + 2, 1, half)
    y_faces, _ = faces_of(place_ref[1], y_refs, y_start, shape, False)
    for side, y_face in enumerate(y_faces):
        y = side * (coarse_y - 1)
        theirs = 3 * side
        coarse_s[:, theirs : theirs + 1] = y_face
        at = 0
        for part in parts:
            count = part.shape[0]
            coarse_s[at : at + count, 1 + side : 2 + side] = part[:, y : y + 1]
            at += count
    coarse = down_ref.shape[1]
    coarse_mask = child_masks(coarse_s, mask_s, coarse)
    out_x, strip = ext_x + 4, 3
    boxes = [(0, out_x, 0, strip), (long, out_x, 1, strip)]
    shape = (out_x, strip, half, WIDE)
    ends = [silu_and_slope(pre) for pre in convolve(four_ref, conv_ref, boxes)]
    ends = [(silu.astype(F32).reshape(shape), slope.reshape(shape)) for silu, slope in ends]
    shape = (coarse_x + 2, 2, half, WIDE)
    size = out_x * half
    for y in range(8):
        if y in (3, 4):
            rows = slice((y - 3) * size, (y - 2) * size)
            fine_s[:, :, y // 2, y % 2] = fine_ref[rows, :].astype(F32).reshape(shape)
            slope_s[:, :, y // 2, y % 2] = slope_ref[rows, :].reshape(shape)
        else:
            side, at = y // 5, y % 5
            mask = mask_s[:, :, y // 2, y % 2]
            silu, slope = ends[side]
            fine_s[:, :, y // 2, y % 2] = silu[:, at].reshape(shape) * mask
            slope_s[:, :, y // 2, y % 2] = slope[:, at].reshape(shape) * mask
    features, delta_coarse = coarse_pass(
        fine_s, slope_s, delta_s, coarse_s, coarse_mask, down_ref, down_back_ref, 0, 4
    )
    features = features[1 : 1 + coarse_x]
    mid = as_field(mid_features_ref[...], coarse_x, coarse_y - 2, half)
    features = jnp.concatenate([features[:, 1:2], mid, features[:, 2:3]], axis=1)
    features_ref[...] = rows_of(features).astype(BF16)
    delta = as_columns(delta_s)
    mid = as_field(mid_delta_ref[...], ext_x + 2, ext_y - 4, half)
    near = delta[1 : out_x - 1]
    near = jnp.concatenate([near[:, 1:4], mid, near[:, 4:7]], axis=1)
    delta_ref[...] = rows_of(near).astype(BF16)
    ours = delta[2 : 2 + ext_x]
    turned = jnp.concatenate([rows_of(ours[:, 2:4]), rows_of(ours[:, 4:6])], axis=0)
    turned = turned.T.astype(BF16)
    low = windows(four_ref, rim - 1, ext_x, rim - 1, 2)
    high = windows(four_ref, long + rim - 1, ext_x, 0, 2)
    three = 3 * channels
    for j in range(9):
        grad = fold(mm(turned, jnp.concatenate([low[j], high[j]], axis=0)), channels)
        grad = grad + conv_grad_ref[j * LANE : (j + 1) * LANE, :]
        sum_s[j * three : (j + 1) * three, :] = (grad * scale).astype(BF16).T
    ours = rows_of(delta_coarse[1 : 1 + coarse_x, 1:3]).astype(BF16)
    base = 27 * channels
    for j in range(4):
        piece = rows_of(fine_s[1 : 1 + coarse_x, j // 2, 1:3, j % 2]).astype(BF16)
        grad = (mm(piece, ours, TN) + down_grad_ref[j * WIDE : (j + 1) * WIDE, :]) * scale
        grad = grad.astype(BF16)
        first, second = grad[:channels], grad[LANE : LANE + channels]
        start = base + 2 * j * channels
        sum_s[start : start + channels, :] = first[:, :LANE]
        sum_s[start + channels : start + 2 * channels, :] = second[:, :LANE]
        start = base + (8 + j) * channels
        sum_s[start : start + channels, :] = jnp.concatenate(
            [first[:, LANE:], second[:, LANE:]], axis=1
        )
    end = base + 12 * channels
    sum_s[end:, :] = jnp.zeros((sum_s.shape[0] - end, LANE), BF16)
    size = keep_ref.shape[0]
    core = place_ref[0] % 2
    keep_ref[...] = sum_s[pl.ds(pl.multiple_of(core * size, size), size), :]
    give_ref[...] = sum_s[pl.ds(pl.multiple_of((1 - core) * size, size), size), :]


def pair_kernel(keep_ref, other_ref, out_ref):
    out_ref[...] = (keep_ref[...].astype(F32) + other_ref[...].astype(F32)).astype(BF16)


def input_grad_kernel(delta_ref, conv_ref, got_ref, back_ref, pad_ref, four_ref, grad_s, *, channels):
    ext_x, ext_y, half = pad_ref.shape[0] - 2, pad_ref.shape[1] - 2, pad_ref.shape[2]
    pad_ref[...] = as_field(delta_ref[...], ext_x + 2, ext_y + 2, half)
    fill_four(pad_ref, four_ref, channels)
    count = 4
    for first in range(0, ext_x, count):
        rows = slice(first * ext_y * half, (first + count) * ext_y * half)
        (grad,) = convolve(four_ref, conv_ref, [(first, count, 0, ext_y)])
        grad_s[rows, :] = grad.astype(BF16)
    grad = grad_s[...]
    pairs = grad.shape[0]
    rows = got_ref.shape[0]
    step = min(256, rows)
    for start in range(0, rows, step):
        found = []
        for q in range(PACK):
            info = got_ref[start : start + step, q * LANE : (q + 1) * LANE].astype(F32)
            place = info[:, channels : channels + 1] * 32.0 + info[:, channels + 1 : channels + 2]
            pick = one_hot(iota((step, pairs), 1) == place.astype(jnp.int32))
            both = mm(pick, grad)
            odd = info[:, channels + 2 : channels + 3] > 0.5
            found.append(jnp.where(odd, both[:, LANE:], both[:, :LANE])[:, :channels])
        back_ref[start : start + step, :] = jnp.concatenate(found, axis=1).astype(BF16)


def join_kernel(terms_ref, back_ref, out_ref, *, block, per_axis):
    total = jnp.sum(terms_ref[...].astype(F32), axis=0)
    rows, wide = back_ref.shape
    out_ref[:, :wide] = back_ref[...]
    lines = total.shape[0] // 2
    halves = []
    for h in range(2):
        parts = [total[h * lines + k : h * lines + k + block] for k in range(0, lines, block)]
        half = jnp.concatenate(parts, axis=1)
        halves.append(jnp.concatenate([half] * per_axis, axis=0).astype(BF16))
    step = block * per_axis
    for g in range(rows // step):
        out_ref[g * step : (g + 1) * step, wide:] = halves[g % 2]


def collect_kernel(back_ref, slot_ref, out_ref):
    channels, points = out_ref.shape
    rows = back_ref.shape[0]
    back = back_ref[:, : PACK * channels]
    step = min(512, points)
    for start in range(0, points, step):
        row = slot_ref[0:1, start : start + step]
        quarter = slot_ref[1:2, start : start + step]
        pick = one_hot(iota((rows, step), 0) == row)
        found = mm(back, pick, TN)
        total = jnp.zeros((channels, step), F32)
        for q in range(PACK):
            total = jnp.where(quarter == q, found[q * channels : (q + 1) * channels], total)
        out_ref[:, start : start + step] = total.astype(BF16)


def unpack_kernel(place_ref, mine_ref, theirs_ref, conv_ref, down_ref, all_s, *, block, per_axis):
    channels = conv_ref.shape[1]
    count = all_s.shape[2] // 2
    skip = mine_ref.shape[1] - theirs_ref.shape[1]
    swap = place_ref[0] % 2 == 1
    step = block * per_axis
    for g in range(mine_ref.shape[0] // step):
        rows = slice(g * step, (g + 1) * step)
        chips = slice(g // 2 * per_axis, (g // 2 + 1) * per_axis)
        for k in range(count):
            mine = mine_ref[rows, skip + k * LANE : skip + (k + 1) * LANE].astype(F32)
            theirs = theirs_ref[rows, k * LANE : (k + 1) * LANE].astype(F32)
            shape = (per_axis, block, LANE)
            all_s[g % 2, chips, k] = jnp.where(swap, theirs, mine).reshape(shape)
            all_s[g % 2, chips, count + k] = jnp.where(swap, mine, theirs).reshape(shape)
    whole = all_s[...].reshape(mine_ref.shape[0] // block * 2 * count * block, LANE)
    base = 27 * channels
    for j in range(27):
        conv_ref[j] = whole[j * channels : (j + 1) * channels, :channels]
    rest = down_ref.shape[2] - LANE
    for j in range(8):
        start = base + j * channels
        down_ref[j, :, :LANE] = whole[start : start + channels]
        start = base + (8 + j // 2) * channels
        tail = whole[start : start + channels]
        down_ref[j, :, LANE:] = tail[:, (j % 2) * rest : (j % 2 + 1) * rest]


def swap_faces(even, odd, axis):
    count = lax.axis_size(axis)
    pairs = [
        [(i, (i + 1) % count) for i in range(start, count, 2)]
        + [((i + 1) % count, i) for i in range(start, count, 2)]
        for start in range(2)
    ]
    odd = lax.ppermute(odd, axis, pairs[1])
    return lax.ppermute(even, axis, pairs[0]), odd


def to_other_core(block):
    return lax.ppermute(block, "gx", [(i, i ^ 1) for i in range(lax.axis_size("gx"))])


def exchange(blocks, **groups):
    return lax.all_to_all(blocks, AXES, split_axis=0, concat_axis=0, tiled=True, **groups)


def shards(point_feats, point_owner, point_cell, occupancy, w_conv, w_down, cotangent):
    points, channels = point_feats.shape
    count_x, count_y = lax.axis_size("gx"), lax.axis_size("gy")
    devices = count_x * count_y
    cap = 32
    block = cap // PACK
    ext_x, ext_y, ext_z = occupancy.shape
    half = ext_z // 2
    pairs = ext_x * ext_y * half
    coarse = w_down.shape[2]
    coarse_x, coarse_y = ext_x // 2, ext_y // 2
    coarse_rows = coarse_x * coarse_y * half
    slot_rows = devices * block
    scale = 1.0 / math.sqrt(float(ext_x * ext_y * ext_z * devices))
    four = 4 * channels
    conv_flops = 2 * pairs * 9 * four * WIDE
    pick_flops = 2 * pairs * slot_rows * PACK * WIDE
    rim = 3
    fields = ((ext_x, ext_y, half, rim), (coarse_x, coarse_y, half, 1))

    send, slot = call(
        functools.partial(dispatch_kernel, devices=devices, cap=cap),
        (struct((slot_rows, PACK * LANE), BF16), struct((2, points), jnp.int32)),
        (point_feats.T, point_owner.reshape(1, points), point_cell.reshape(1, points)),
        "dispatch",
        scratch=[
            pltpu.VMEM((channels, points), BF16),
            pltpu.VMEM((1, points), jnp.int32),
            pltpu.VMEM((1, points), jnp.int32),
            pltpu.VMEM((slot_rows, PACK * LANE), BF16),
            pltpu.SemaphoreType.DMA((3,)),
            pltpu.SemaphoreType.DMA((-(-slot_rows // 256),)),
        ],
        flops=2 * points * slot_rows * PACK * LANE,
        far=(0, 1, 2),
        far_outs=(0,),
        grant=56,
    )
    got = exchange(send.reshape(devices, block, PACK * LANE)).reshape(slot_rows, PACK * LANE)
    conv_blocks, back_blocks, down_blocks, down_back, given = call(
        functools.partial(prepare_kernel, ext_y=ext_y),
        (
            struct((9 * four, WIDE), BF16),
            struct((9 * four, WIDE), BF16),
            struct((4 * WIDE, coarse), BF16),
            struct((coarse, 4 * WIDE), BF16),
            struct((coarse_rows, WIDE), BF16),
        ),
        (w_conv, w_down, cotangent.reshape(coarse_rows, coarse),
         occupancy.reshape(ext_x * ext_y, ext_z)),
        "prepare",
        flops=1000000000,
    )
    x_rows = packed_size(rim * ext_y * half) + coarse_y * half
    y_rows = packed_size(rim * (ext_x + 2 * rim) * half) + (coarse_x + 2) * half
    place = jnp.stack([lax.axis_index("gx"), lax.axis_index("gy")]).astype(jnp.int32)
    grid, x_even, x_odd = call(
        functools.partial(pool_kernel, channels=channels, fields=fields, count=count_x),
        tuple(struct((n, WIDE), BF16) for n in (pairs, x_rows, x_rows)),
        (place, got, given),
        "pool",
        scratch=[pltpu.VMEM((pairs, WIDE), F32)],
        flops=pick_flops,
    )
    x_faces = swap_faces(x_even, x_odd, "gx")
    y_even, y_odd = call(
        functools.partial(edge_kernel, fields=fields, count=count_y),
        tuple(struct((n, WIDE), BF16) for n in (y_rows, y_rows)),
        (place, grid, given, *x_faces),
        "edge",
    )
    y_faces = swap_faces(y_even, y_odd, "gy")
    long = ext_x + 2 * rim
    near = (ext_x + 2, ext_y + 2, half)
    near_rows = near[0] * near[1] * half
    edge_rows = 2 * (ext_x + 4) * half

    def split(columns):
        return pltpu.VMEM((coarse_x + 2, 2, columns, 2, half, WIDE), F32)

    middle = call(
        functools.partial(middle_kernel, channels=channels, rim=rim),
        (
            struct((edge_rows, WIDE), BF16),
            struct((edge_rows, WIDE), F32),
            struct((coarse_x * (coarse_y - 2) * half, coarse), BF16),
            struct(((ext_x + 2) * (ext_y - 4) * half, WIDE), BF16),
            struct((9 * LANE, 3 * channels), F32),
            struct((4 * WIDE, coarse), F32),
        ),
        (place, grid, given, *x_faces, conv_blocks, down_blocks, down_back),
        "middle",
        scratch=[
            pltpu.VMEM((long, ext_y, half, WIDE), F32),
            pltpu.VMEM((long, ext_y, half, four), F32),
            pltpu.VMEM((coarse_x + 2, coarse_y, half, WIDE), F32),
            split(coarse_y),
            split(coarse_y),
            split(coarse_y),
            split(coarse_y - 2),
        ],
        flops=3 * conv_flops,
    )
    used = 39 * channels
    chunk = -(-used // (32 * devices)) * 32
    half_rows = devices // 2 * chunk
    features, delta, keep, give = call(
        functools.partial(strip_kernel, channels=channels, fields=fields, scale=scale),
        (
            struct((coarse_rows, coarse), BF16),
            struct((near_rows, WIDE), BF16),
            struct((half_rows, LANE), BF16),
            struct((half_rows, LANE), BF16),
        ),
        (place, grid, given, *x_faces, *y_faces, *middle, conv_blocks, down_blocks, down_back),
        "strip",
        scratch=[
            pltpu.VMEM((2 * long, 2 * rim, half, WIDE), F32),
            pltpu.VMEM((2 * long, 2 * rim, half, four), F32),
            pltpu.VMEM((coarse_x + 2, 4, half, WIDE), F32),
            split(4),
            split(4),
            split(4),
            split(4),
            pltpu.VMEM((2 * half_rows, LANE), BF16),
        ],
        flops=conv_flops,
        megabytes=8,
    )
    both = call(
        pair_kernel, struct((half_rows, LANE), BF16), (keep, to_other_core(give)), "pair"
    )
    terms = exchange(
        both.reshape(devices // 2, chunk, LANE),
        axis_index_groups=[
            [x * count_y + y for x in range(core, count_x, 2) for y in range(count_y)]
            for core in range(2)
        ],
    )
    back = call(
        functools.partial(input_grad_kernel, channels=channels),
        struct((slot_rows, PACK * channels), BF16),
        (delta, back_blocks, got),
        "input_grad",
        scratch=[
            pltpu.VMEM((*near, WIDE), F32),
            pltpu.VMEM((*near, four), F32),
            pltpu.VMEM((pairs, WIDE), BF16),
        ],
        flops=conv_flops + pick_flops,
        megabytes=8,
    )
    half_lanes = chunk // 2 // block * LANE
    joined_lanes = PACK * channels + half_lanes
    joined = call(
        functools.partial(join_kernel, block=block, per_axis=count_y),
        struct((slot_rows, joined_lanes), BF16),
        (terms, back),
        "join",
        flops=devices * chunk * LANE,
    )
    returned = exchange(joined.reshape(devices, block, joined_lanes)).reshape(
        slot_rows, joined_lanes
    )
    theirs = to_other_core(returned[:, PACK * channels :])
    grad_points = call(
        collect_kernel,
        struct((channels, points), BF16),
        (returned, slot),
        "collect",
        flops=2 * points * slot_rows * PACK * LANE,
    ).T
    grad_conv, grad_down = call(
        functools.partial(unpack_kernel, block=block, per_axis=count_y),
        (struct(w_conv.shape, F32), struct(w_down.shape, F32)),
        (place, returned, theirs),
        "unpack",
        scratch=[pltpu.VMEM((2, devices // 2, chunk // block, block, LANE), F32)],
    )
    return (
        features.reshape(coarse_x, coarse_y, half, coarse),
        grad_points,
        grad_conv,
        grad_down,
    )


def solution(mesh):
    placed = (
        P(("gx", "gy"), None),
        P(("gx", "gy"), None),
        P(("gx", "gy")),
        P("gx", "gy", None),
        P(),
        P(),
        P("gx", "gy", None, None),
    )
    return jax.shard_map(
        shards,
        mesh=mesh,
        in_specs=placed,
        out_specs=(P("gx", "gy", None, None), P(("gx", "gy"), None), P(), P()),
        check_vma=False,
    )
```
